128 devices in a mesh: group: 4 (over x), brick: 32 (over y, z, core).
Axes of the slice: x: 4, y: 4, z: 4, core: 2. Of those that a mesh axis runs over, the one named last changes fastest.
Arguments:
- forcing_vector: float32 [1024, 64, 256], P(('group', 'brick')), may hold values from -6 to 6
- thermal_iterate: float32 [1024, 64, 256], P(('group', 'brick')), may hold values from -6 to 6
- storage_over_step: float32 [1024, 64, 256], P(('group', 'brick')), may hold values from 0.05 to 1
- opening_shares: float32 [3, 1024, 64, 256], P(None, ('group', 'brick')), may hold values from 0.05 to 1
- flow_speed: float32 [3, 1024, 64, 256], P(None, ('group', 'brick')), may hold values from 0 to 1
- diffusivity_root: float32 [1024, 64, 256], P(('group', 'brick')), may hold values from 0.5 to 2
- sanction_weight: float32 [1024, 64, 256], P(('group', 'brick')), may hold values from 0.5 to 4
- rigidity_matrix: float32 [3, 8, 8], replicated, may hold values from -0.3 to 3.4, as said below
- contact_fluid_part: int32 [128, 128], P('brick'), may hold values from 0 to 2
- contact_fluid_volume: int32 [128, 128], P('brick'), may hold values from 0 to 131071
- contact_solid_vertex: int32 [128, 128], P('brick'), may hold values from 0 to 131071
- exchange_rate_factor: float32 [128, 128], P('brick'), may hold values from 0.5 to 4
Outputs:
- updated: float32 [1024, 64, 256], P(('group', 'brick'))
The draws below stay inside these ranges and needn't reach their ends.
Inputs may be any that keep to these rules, and one draw needn't show every extreme that they name: `rigidity_matrix`: symmetric along the last two dimensions, each diagonal entry larger than the sum of magnitudes of the other entries of its row.
All inputs are finite; a program needn't handle non-finite values.
Results may differ from the reference program's by a relative error of at most 0.0003.
Values sent between devices are 32-bit elements; how exact they have to be, the bound alone decides.
A program may use at most 128 MiB of HBM per device.

```python
import math
import jax
import jax.numpy as jnp
import numpy as np
from jax import lax

NODES = 8
VOLUMES_MIDDLE = 64
VOLUMES_LAST = 256
ITERS = 8
IROWS = 4
FGROUPS = 3
CELLS = 131072
NXF = 768
NXS = 256
LINES_LEADING = 1024
ROWS = 128
N_BRICK = 32


def draw_rigidity_matrix(key, part):
    key = jax.random.fold_in(key, 7)
    first, second = jax.random.split(key)
    raw = jnp.clip(0.15 * jax.random.normal(first, (3, NODES, NODES), jnp.float32), -0.3, 0.3)
    mirror = 0.5 * (raw + jnp.swapaxes(raw, 1, 2))
    unit = jnp.eye(NODES, dtype=jnp.float32)
    lifted = 0.3 * (NODES - 1) + 0.05 + jax.random.uniform(second, (3, NODES, 1), jnp.float32, 0.0, 0.9)
    return mirror * (1.0 - unit) + unit * lifted


def touch_ends(values, own_key, least, largest):
    extent = values.shape
    index_at = [jax.random.randint(jax.random.fold_in(own_key, axis), (), 0, extent[axis]) for axis in range(len(extent))]
    values = values.at[tuple(index_at)].set(least)
    longest = extent.index(max(extent))
    index_at[longest] = (index_at[longest] + 1) % extent[longest]
    return values.at[tuple(index_at)].set(largest)


def level_of(key, shape, cuts, low, top_value):
    level = 1.0
    for axis_at, parts in cuts:
        steps = jax.random.uniform(jax.random.fold_in(jax.random.fold_in(key, 6), axis_at), (parts,), jnp.float32, low / len(cuts), top_value / len(cuts))
        level = level * jnp.repeat(jnp.exp(steps), shape[axis_at] // parts).reshape((-1,) + (1,) * (len(shape) - 1 - axis_at))
    return level


def cumulative_ranks(number_of, lean):
    portions = [(1 << 20) // math.isqrt(grade ** lean) + 1 for grade in range(1, number_of + 1)]
    width = 1 + sum(portions) // (1 << 30)
    return np.cumsum(np.array([max(1, weight // width) for weight in portions]))


def skewed_ids(rng, dims, number_of, slope):
    table = cumulative_ranks(number_of, slope)
    pick = jax.random.randint(jax.random.fold_in(rng, 1), dims, 0, int(table[number_of - 1]))
    rank = jnp.searchsorted(jnp.asarray(table, jnp.int32), pick, side="right")
    return jax.random.permutation(jax.random.fold_in(rng, 2), number_of)[rank].astype(jnp.int32)


def gaussian(key, dims, spread, limit, cuts=(), held_as=jnp.bfloat16):
    drawn = spread * jax.random.normal(key, dims, jnp.float32)
    if cuts:
        drawn = drawn * level_of(key, dims, cuts, -0.22, 0.18)
    return jnp.clip(drawn, -limit, limit).astype(held_as)


def setup_inputs(seed: int = 0) -> dict:
    key_of = jax.random.split(jax.random.key(seed), 13)
    return {
        "forcing_vector": gaussian(key_of[0], (LINES_LEADING, VOLUMES_MIDDLE, VOLUMES_LAST), 1.0, 6.0, ((0, 128),), jnp.float32),
        "thermal_iterate": gaussian(key_of[1], (LINES_LEADING, VOLUMES_MIDDLE, VOLUMES_LAST), 1.0, 6.0, ((0, 128),), jnp.float32),
        "storage_over_step": jnp.clip(jnp.exp(math.log(1.0) - 2.9957323 * jax.random.uniform(key_of[2], (LINES_LEADING, VOLUMES_MIDDLE, VOLUMES_LAST), jnp.float32) ** level_of(key_of[2], (LINES_LEADING, VOLUMES_MIDDLE, VOLUMES_LAST), ((0, 128),), -0.2, 0.2)), 0.05, 1.0),
        "opening_shares": jnp.clip(0.05 + 0.95 * jax.random.uniform(key_of[3], (3, LINES_LEADING, VOLUMES_MIDDLE, VOLUMES_LAST), jnp.float32) ** level_of(key_of[3], (3, LINES_LEADING, VOLUMES_MIDDLE, VOLUMES_LAST), ((1, 128),), -0.2, 0.2), 0.05, 1.0),
        "flow_speed": jnp.clip(1.0 * jax.random.uniform(key_of[4], (3, LINES_LEADING, VOLUMES_MIDDLE, VOLUMES_LAST), jnp.float32) ** level_of(key_of[4], (3, LINES_LEADING, VOLUMES_MIDDLE, VOLUMES_LAST), ((1, 128),), -0.2, 0.2), 0.0, 1.0),
        "diffusivity_root": jnp.clip(jnp.exp(math.log(2.0) - 1.3862944 * jax.random.uniform(key_of[5], (LINES_LEADING, VOLUMES_MIDDLE, VOLUMES_LAST), jnp.float32) ** level_of(key_of[5], (LINES_LEADING, VOLUMES_MIDDLE, VOLUMES_LAST), ((0, 128),), -0.2, 0.2)), 0.5, 2.0),
        "sanction_weight": jnp.clip(jnp.exp(math.log(4.0) - 2.0794415 * jax.random.uniform(key_of[6], (LINES_LEADING, VOLUMES_MIDDLE, VOLUMES_LAST), jnp.float32) ** level_of(key_of[6], (LINES_LEADING, VOLUMES_MIDDLE, VOLUMES_LAST), ((0, 128),), -0.2, 0.2)), 0.5, 4.0),
        "rigidity_matrix": draw_rigidity_matrix(jax.random.fold_in(key_of[12], 71), 0),
        "contact_fluid_part": touch_ends(skewed_ids(key_of[8], (ROWS, 128), FGROUPS, 2), jax.random.fold_in(key_of[8], 3), 0, FGROUPS - 1).astype(jnp.int32),
        "contact_fluid_volume": touch_ends(jax.random.randint(key_of[9], (ROWS, 128), 0, CELLS), jax.random.fold_in(key_of[9], 1), 0, CELLS - 1).astype(jnp.int32),
        "contact_solid_vertex": touch_ends(jax.random.randint(key_of[10], (ROWS, 128), 0, CELLS), jax.random.fold_in(key_of[10], 1), 0, CELLS - 1).astype(jnp.int32),
        "exchange_rate_factor": jnp.clip(jnp.exp(math.log(4.0) - 2.0794415 * jax.random.uniform(key_of[11], (ROWS, 128), jnp.float32) ** level_of(key_of[11], (ROWS, 128), ((0, 32),), -0.2, 0.2)), 0.5, 4.0),
    }


HIGH = lax.Precision.HIGHEST

def shift_next(v, axis):
    size = v.shape[axis]
    inner = lax.slice_in_dim(v, 1, size, axis=axis)
    zero = jnp.zeros_like(lax.slice_in_dim(v, 0, 1, axis=axis))
    return jnp.concatenate([inner, zero], axis=axis)

def shift_prev(v, axis):
    size = v.shape[axis]
    inner = lax.slice_in_dim(v, 0, size - 1, axis=axis)
    zero = jnp.zeros_like(lax.slice_in_dim(v, 0, 1, axis=axis))
    return jnp.concatenate([zero, inner], axis=axis)

def open_faces(shape, axis):
    index = lax.broadcasted_iota(jnp.int32, shape, axis)
    return (index < shape[axis] - 1).astype(jnp.float32)

def element_faces(shape, axis):
    index = lax.broadcasted_iota(jnp.int32, shape, axis)
    inside = (index % NODES == NODES - 1) & (index < shape[axis] - 1)
    return inside.astype(jnp.float32)

def fluid_apply(v, faces, speeds, diagonal):
    out = diagonal * v
    for d in range(3):
        flux = faces[d] * ((1.0 + speeds[d]) * v - shift_next(v, d))
        out = out + flux - shift_prev(flux, d)
    return out

def stiffness_apply(u, rigidity_matrix):
    blocks = u.reshape(NXS // NODES, NODES, VOLUMES_MIDDLE // NODES, NODES, VOLUMES_LAST // NODES, NODES)
    along_x = jnp.einsum('pq,iqjbkc->ipjbkc', rigidity_matrix[0], blocks, precision=HIGH)
    along_y = jnp.einsum('pq,iajqkc->iajpkc', rigidity_matrix[1], blocks, precision=HIGH)
    along_z = jnp.einsum('pq,iajbkq->iajbkp', rigidity_matrix[2], blocks, precision=HIGH)
    return (along_x + along_y + along_z).reshape(NXS, VOLUMES_MIDDLE, VOLUMES_LAST)

def solid_apply(v, mass, diffusivity_root, pairs, rigidity_matrix):
    out = mass * v + diffusivity_root * stiffness_apply(diffusivity_root * v, rigidity_matrix)
    for d in range(3):
        jump = pairs[d] * (v - shift_next(v, d))
        out = out + jump - shift_prev(jump, d)
    return out

def least_squares(hess, beta):
    gram = jnp.dot(hess.T, hess, precision=HIGH)
    lower = jnp.linalg.cholesky(gram)
    right = (beta * hess[0])[:, None]
    middle = lax.linalg.triangular_solve(lower, right, left_side=True, lower=True)
    coeffs = lax.linalg.triangular_solve(lower, middle, left_side=True, lower=True, transpose_a=True)
    return coeffs[:, 0]

def gmres(operator, right):
    beta = jnp.sqrt(jnp.sum(right * right))
    basis = [right / beta]
    columns = []
    for step in range(ITERS):
        image = operator(basis[step])
        heights = jnp.stack([jnp.sum(basis[j] * image) for j in range(step + 1)])
        for j in range(step + 1):
            image = image - heights[j] * basis[j]
        length = jnp.sqrt(jnp.sum(image * image))
        basis.append(image / length)
        columns.append(jnp.concatenate([heights, length[None], jnp.zeros((ITERS - 1 - step,), jnp.float32)]))
    coeffs = least_squares(jnp.stack(columns, axis=1), beta)
    result = jnp.zeros_like(right)
    for step in range(ITERS):
        result = result + coeffs[step] * basis[step]
    return result

def conjugate(operator, right):
    solution = jnp.zeros_like(right)
    resid = right
    direction = right
    norm_now = jnp.sum(resid * resid)
    for step in range(ITERS):
        image = operator(direction)
        alpha = norm_now / jnp.sum(direction * image)
        solution = solution + alpha * direction
        resid = resid - alpha * image
        norm_next = jnp.sum(resid * resid)
        direction = resid + norm_next / norm_now * direction
        norm_now = norm_next
    return solution

def reference(forcing_vector, thermal_iterate, storage_over_step, opening_shares, flow_speed, diffusivity_root, sanction_weight, rigidity_matrix, contact_fluid_part, contact_fluid_volume, contact_solid_vertex, exchange_rate_factor):
    unrolled_array = thermal_iterate.reshape(-1)
    column = lax.broadcasted_iota(jnp.int32, contact_fluid_part.shape, 0) // IROWS
    fluid_index = ((contact_fluid_part * N_BRICK + column) * CELLS + contact_fluid_volume).reshape(-1)
    solid_index = (column * CELLS + contact_solid_vertex).reshape(-1)
    wall = unrolled_array[solid_index + NXF * VOLUMES_MIDDLE * VOLUMES_LAST]
    near = unrolled_array[fluid_index]
    coeff = exchange_rate_factor.reshape(-1)
    fluid_rhs = forcing_vector[:NXF].reshape(-1).at[fluid_index].add(coeff * wall).reshape(NXF, VOLUMES_MIDDLE, VOLUMES_LAST)
    fluid_diag = storage_over_step[:NXF].reshape(-1).at[fluid_index].add(coeff).reshape(NXF, VOLUMES_MIDDLE, VOLUMES_LAST)
    solid_rhs = forcing_vector[NXF:].reshape(-1).at[solid_index].add(coeff * (near - wall)).reshape(NXS, VOLUMES_MIDDLE, VOLUMES_LAST)
    shape_f = (NXF, VOLUMES_MIDDLE, VOLUMES_LAST)
    faces = [opening_shares[d, :NXF] * open_faces(shape_f, d) for d in range(3)]
    speeds = [flow_speed[d, :NXF] for d in range(3)]
    shape_s = (NXS, VOLUMES_MIDDLE, VOLUMES_LAST)
    weights = sanction_weight[NXF:]
    pairs = [0.5 * (weights + shift_next(weights, d)) * element_faces(shape_s, d) for d in range(3)]
    mass = storage_over_step[NXF:]
    gains = diffusivity_root[NXF:]
    fluid_new = gmres(lambda v: fluid_apply(v, faces, speeds, fluid_diag), fluid_rhs)
    solid_new = conjugate(lambda v: solid_apply(v, mass, gains, pairs, rigidity_matrix), solid_rhs)
    return jnp.concatenate([fluid_new, solid_new], axis=0)
```

```python
import functools

import jax
import jax.numpy as jnp
from jax import lax
from jax.experimental import pallas as pl
from jax.experimental.pallas import tpu as pltpu
from jax.sharding import PartitionSpec as P

ITERS = 8


HIGH = lax.Precision.HIGHEST


def passed_along(value, axis, steps):
    count = lax.axis_size(axis)
    leading, last = (max(0, -steps), min(count, count - steps))
    return lax.ppermute(value, axis, [(source, source + steps) for source in range(leading, last)])


def extended(cells, sides, width):
    for axis, dim in sides:
        count = lax.axis_size(axis)
        ends = count - 1
        head = lax.slice_in_dim(cells, 0, width, axis=dim)
        tail = lax.slice_in_dim(cells, cells.shape[dim] - width, cells.shape[dim], axis=dim)
        cells = jnp.concatenate(
            [
                lax.ppermute(tail, axis, [(i, (i + 1) % count) for i in range(ends)]),
                cells,
                lax.ppermute(head, axis, [((i + 1) % count, i) for i in range(ends)]),
            ],
            axis=dim,
        )
    return cells


def shift_next(v, axis):
    size = v.shape[axis]
    inner = lax.slice_in_dim(v, 1, size, axis=axis)
    zero = jnp.zeros_like(lax.slice_in_dim(v, 0, 1, axis=axis))
    return jnp.concatenate([inner, zero], axis=axis)


def shift_prev(v, axis):
    size = v.shape[axis]
    inner = lax.slice_in_dim(v, 0, size - 1, axis=axis)
    zero = jnp.zeros_like(lax.slice_in_dim(v, 0, 1, axis=axis))
    return jnp.concatenate([zero, inner], axis=axis)


def open_faces(shape, axis):
    index = lax.broadcasted_iota(jnp.int32, shape, axis)
    return (index < shape[axis] - 1).astype(jnp.float32)


def element_faces(shape, axis, nodes):
    index = lax.broadcasted_iota(jnp.int32, shape, axis)
    inside = (index % nodes == nodes - 1) & (index < shape[axis] - 1)
    return inside.astype(jnp.float32)


def stiffness_apply(u, rigidity_matrix):
    nodes = rigidity_matrix.shape[1]
    rows, width, depth = u.shape
    block = min(depth, 128)
    along_x = jnp.einsum("pq,qyz->pyz", rigidity_matrix[0], u, precision=HIGH)
    split_y = u.reshape(rows, width // nodes, nodes, depth)
    along_y = jnp.einsum("pq,xeqz->xepz", rigidity_matrix[1], split_y, precision=HIGH).reshape(
        rows, width, depth
    )
    wide = jnp.kron(jnp.eye(block // nodes, dtype=jnp.float32), rigidity_matrix[2])
    split_z = u.reshape(rows, width, depth // block, block)
    along_z = jnp.einsum("xyeq,pq->xyep", split_z, wide, precision=HIGH).reshape(rows, width, depth)
    return along_x + along_y + along_z


def least_squares(hess, beta):
    gram = jnp.dot(hess.T, hess, precision=HIGH)
    lower = jnp.linalg.cholesky(gram)
    right = (beta * hess[0])[:, None]
    middle = lax.linalg.triangular_solve(lower, right, left_side=True, lower=True)
    coeffs = lax.linalg.triangular_solve(
        lower, middle, left_side=True, lower=True, transpose_a=True
    )
    return coeffs[:, 0]


def iterated(
    forcing_vector,
    thermal_iterate,
    storage_over_step,
    opening_shares,
    flow_speed,
    diffusivity_root,
    sanction_weight,
    rigidity_matrix,
    contact_fluid_part,
    contact_fluid_volume,
    contact_solid_vertex,
    exchange_rate_factor,
):
    groups = lax.axis_size("group")
    bricks = lax.axis_size("brick")
    group_id = lax.axis_index("group")
    brick_id = lax.axis_index("brick")
    solid = group_id == groups - 1
    solid_flag = solid.astype(jnp.float32)
    fluid_flag = 1.0 - solid_flag
    rows, width, depth = forcing_vector.shape
    nodes = rigidity_matrix.shape[1]
    device = group_id * bricks + brick_id
    first_solid = (groups - 1) * bricks
    unrolled_array = thermal_iterate.reshape(-1)
    owned = (contact_fluid_part == group_id).astype(jnp.float32)
    target = jnp.where(solid, contact_solid_vertex, contact_fluid_volume).reshape(-1)
    picked = unrolled_array[target].reshape(contact_solid_vertex.shape)
    wall, near = lax.psum((picked * solid_flag, picked * owned * fluid_flag), "group")
    extra_rhs = jnp.where(
        solid, exchange_rate_factor * (near - wall), exchange_rate_factor * wall * owned
    )
    extra_diag = exchange_rate_factor * owned * fluid_flag
    rhs = (
        forcing_vector.reshape(-1)
        .at[target]
        .add(extra_rhs.reshape(-1))
        .reshape(forcing_vector.shape)
    )
    fluid_diag = (
        storage_over_step.reshape(-1)
        .at[target]
        .add(extra_diag.reshape(-1))
        .reshape(forcing_vector.shape)
    )
    shape = (rows, width, depth)
    global_row = device * rows + lax.broadcasted_iota(jnp.int32, shape, 0)
    face_x = opening_shares[0] * (global_row != first_solid * rows - 1).astype(jnp.float32)
    face_y = opening_shares[1] * open_faces(shape, 1)
    face_z = opening_shares[2] * open_faces(shape, 2)
    rims = passed_along(
        jnp.stack([face_x[-1], flow_speed[0][-1], sanction_weight[-1]]), ("group", "brick"), 1
    )
    face_low = rims[0]
    speed_low = rims[1]
    weight_low = rims[2]
    pair_low = 0.5 * (weight_low + sanction_weight[0]) * (device != first_solid).astype(jnp.float32)
    pair_up = passed_along(pair_low, "brick", -1)
    pair_y = (
        0.5 * (sanction_weight + shift_next(sanction_weight, 1)) * element_faces(shape, 1, nodes)
    )
    pair_z = (
        0.5 * (sanction_weight + shift_next(sanction_weight, 2)) * element_faces(shape, 2, nodes)
    )
    local_square = jnp.sum(rhs * rhs)
    solution = jnp.zeros_like(rhs)
    resid = rhs
    columns = []
    fluid_square, solid_square = lax.psum(
        (local_square * fluid_flag, local_square * solid_flag), ("group", "brick")
    )
    beta = jnp.sqrt(fluid_square)
    basis = [rhs / beta]
    direction = rhs
    norm_now = solid_square
    for step in range(ITERS):
        vector = jnp.where(solid, direction, basis[step])
        padded = extended(vector, ((("group", "brick"), 0),), 1)
        below = padded[0]
        above = padded[-1]

        def fluid_branch(unused):
            following = jnp.concatenate([vector[1:], above[None]], axis=0)
            flux_x = face_x * ((1.0 + flow_speed[0]) * vector - following)
            flux_low = face_low * ((1.0 + speed_low) * below - vector[0])
            out = (
                fluid_diag * vector
                + flux_x
                - jnp.concatenate([flux_low[None], flux_x[:-1]], axis=0)
            )
            flux_y = face_y * ((1.0 + flow_speed[1]) * vector - shift_next(vector, 1))
            flux_z = face_z * ((1.0 + flow_speed[2]) * vector - shift_next(vector, 2))
            return out + flux_y - shift_prev(flux_y, 1) + flux_z - shift_prev(flux_z, 2)

        def solid_branch(unused):
            out = storage_over_step * vector + diffusivity_root * stiffness_apply(
                diffusivity_root * vector, rigidity_matrix
            )
            jump_up = pair_up * (vector[-1] - above)
            jump_low = pair_low * (below - vector[0])
            out = out.at[0].add(-jump_low).at[rows - 1].add(jump_up)
            jump_y = pair_y * (vector - shift_next(vector, 1))
            jump_z = pair_z * (vector - shift_next(vector, 2))
            return out + jump_y - shift_prev(jump_y, 1) + jump_z - shift_prev(jump_z, 2)

        image = lax.cond(solid, solid_branch, fluid_branch, 0)
        inner = jnp.stack([jnp.sum(basis[j] * image) for j in range(step + 1)])
        heights, curvature = lax.psum(
            (inner * fluid_flag, jnp.sum(direction * image) * solid_flag), ("group", "brick")
        )
        fresh = image
        for j in range(step + 1):
            fresh = fresh - heights[j] * basis[j]
        alpha = norm_now / curvature
        solution = solution + alpha * direction
        resid = resid - alpha * image
        fresh_square, norm_next = lax.psum(
            (jnp.sum(fresh * fresh) * fluid_flag, jnp.sum(resid * resid) * solid_flag),
            ("group", "brick"),
        )
        length = jnp.sqrt(fresh_square)
        basis.append(fresh / length)
        columns.append(
            jnp.concatenate([heights, length[None], jnp.zeros((ITERS - 1 - step,), jnp.float32)])
        )
        direction = resid + norm_next / norm_now * direction
        norm_now = norm_next
    coeffs = least_squares(jnp.stack(columns, axis=1), beta)
    fluid_new = jnp.zeros_like(rhs)
    for step in range(ITERS):
        fluid_new = fluid_new + coeffs[step] * basis[step]
    return jnp.where(solid, solution, fluid_new)


F32 = jnp.float32
BF16 = jnp.bfloat16
MESH = pl.DeviceIdType.MESH
PIVOT_LEAST = 1e-3
REFINE_MOST = 3e-4


def iota(shape, dim):
    return lax.broadcasted_iota(jnp.int32, shape, dim)


def pieces(x):
    high = x.astype(BF16)
    return high, (x - high.astype(F32)).astype(BF16)


def total(x):
    return jnp.sum(jnp.sum(x, axis=0, keepdims=True), axis=1, keepdims=True)


def greatest(x):
    return jnp.max(jnp.max(x, axis=0, keepdims=True), axis=1, keepdims=True)


def dot(a, b, dims):
    return lax.dot_general(a, b, ((dims[0], dims[1]), ((), ())), preferred_element_type=F32)


def shift_rows(x, gamma):
    size = x.shape[0]
    after = pltpu.roll(x, size - 1, 0)
    row = iota(x.shape, 0)
    out = gamma * x + 0.5 * (pltpu.roll(x, 1, 0) + after) + jnp.where(row == 0, 0.5 * after, 0.0)
    return jnp.where(row < ITERS, out, 0.0)


def shift_lanes(x, gamma):
    size = x.shape[1]
    after = pltpu.roll(x, size - 1, 1)
    lane = iota(x.shape, 1)
    out = gamma * x + 0.5 * (pltpu.roll(x, 1, 1) + after) + jnp.where(lane == 0, 0.5 * after, 0.0)
    return jnp.where(lane < ITERS, out, 0.0)


def projected(gram, gamma, fluid):
    shape = gram.shape
    row, lane = iota(shape, 0), iota(shape, 1)
    wide = shift_lanes(gram, gamma)
    if fluid:
        normal, right = shift_rows(wide, gamma), shift_rows(gram, gamma)
    else:
        normal, right = jnp.where(row < ITERS, wide, 0.0), jnp.where(row < ITERS, gram, 0.0)
    table = jnp.where(lane < ITERS, normal, 0.0)
    table = jnp.where((lane == row + 8) & (row < ITERS), 1.0, table)
    table = jnp.where(lane == 16, pltpu.roll(right, 16, 1), table)
    margin = None
    for k in range(ITERS):
        pivot = table[k : k + 1, k : k + 1]
        spare = pivot - PIVOT_LEAST * normal[k : k + 1, k : k + 1]
        margin = spare if margin is None else jnp.minimum(margin, spare)
        scaled = table[k : k + 1, :] * (1.0 / pivot)
        column = jnp.where(row[:, :1] == k, 0.0, table[:, k : k + 1])
        table = jnp.where(row == k, scaled, table - column * scaled)
    coeffs = jnp.broadcast_to(table[:, 16:17], shape)
    inverse = jnp.where(lane < ITERS, pltpu.roll(table, shape[1] - 8, 1), 0.0)
    applied = gamma * coeffs + 0.5 * (pltpu.roll(coeffs, 1, 0) + pltpu.roll(coeffs, shape[0] - 1, 0))
    applied = applied + jnp.where(row == 1, 0.5 * pltpu.roll(coeffs, 1, 0), 0.0)
    rest = jnp.where(row == 0, 1.0, 0.0) - applied
    image = jnp.broadcast_to(jnp.sum(gram * rest, axis=0, keepdims=True), shape)
    image = shift_lanes(image, gamma) if fluid else jnp.where(lane < ITERS, image, 0.0)
    change = jnp.sum(inverse * image, axis=1, keepdims=True)
    coeffs = coeffs[:, :1] + change
    size = jnp.sum(jnp.abs(coeffs), axis=0, keepdims=True)
    moved = jnp.sum(jnp.abs(change), axis=0, keepdims=True)
    good = (margin > 0.0) & (moved < REFINE_MOST * size)
    return coeffs, jnp.where(good, 1.0, 0.0)


def kernel(
    groups,
    bricks,
    forcing_hbm,
    thermal_hbm,
    storage_hbm,
    opening_hbm,
    flow_hbm,
    root_hbm,
    weight_hbm,
    rigidity_hbm,
    part_hbm,
    volume_hbm,
    vertex_hbm,
    factor_hbm,
    out_hbm,
    flag_hbm,
    thermal,
    forcing,
    storage,
    opening,
    flow,
    root,
    weight,
    rigidity,
    part,
    volume,
    vertex,
    factor,
    basis,
    ax,
    gx,
    diag,
    uy,
    ly,
    uz,
    lz,
    stiff,
    uh,
    ul,
    wz,
    wxy,
    weight_low,
    weight_up,
    row_hot,
    col_hot,
    picked,
    walls,
    nears,
    gram_tile,
    near_slots,
    far_slots,
    out,
    flag,
    load_sem,
    store_sem,
    halo_send,
    halo_recv,
    coef_send,
    coef_recv,
    contact_send,
    contact_recv,
    near_send,
    near_recv,
    far_send,
    far_recv,
):
    group = lax.axis_index("group")
    brick = lax.axis_index("brick")
    rows, width, depth = forcing.shape
    plane = (width, depth)
    cells = rows * width
    solid = group == groups - 1
    fluid = group != groups - 1
    inner, outer = 8, bricks // 8
    low_id = lax.rem(brick, inner)
    high_id = group * outer + brick // inner
    n_far = groups * outer
    at_top = (brick == bricks - 1) & (group >= groups - 2)
    at_bottom = (brick == 0) & ((group == 0) | (group == groups - 1))
    has_up, has_down = jnp.logical_not(at_top), jnp.logical_not(at_bottom)
    device = group * bricks + brick
    up_id = lax.rem(device + 1, groups * bricks)
    down_id = lax.rem(device + groups * bricks - 1, groups * bricks)
    up = (up_id // bricks, lax.rem(up_id, bricks))
    down = (down_id // bricks, lax.rem(down_id, bricks))

    names = [
        (vertex_hbm, vertex),
        (volume_hbm, volume),
        (thermal_hbm, thermal),
        (part_hbm, part),
        (factor_hbm, factor),
        (opening_hbm, opening),
        (flow_hbm, flow),
        (storage_hbm, storage),
        (weight_hbm, weight),
        (root_hbm, root),
        (rigidity_hbm, rigidity),
        (forcing_hbm, forcing),
    ]
    loads = [pltpu.make_async_copy(s, d, load_sem.at[i]) for i, (s, d) in enumerate(names)]
    for load in loads:
        load.start()
    (l_vertex, l_volume, l_thermal, l_part, l_factor, l_opening, l_flow, l_storage, l_weight, l_root, l_rigid, l_forcing) = loads

    def near_peer(o):
        peer = lax.rem(low_id + o, inner)
        return peer, (group, (brick // inner) * inner + peer)

    def far_peer(o):
        peer = lax.rem(high_id + o, n_far)
        return peer, (peer // outer, lax.rem(peer, outer) * inner + low_id)

    barrier = pltpu.get_barrier_semaphore()
    for o in range(1, inner):
        pl.semaphore_signal(barrier, inc=1, device_id=near_peer(o)[1], device_id_type=MESH)
    for o in range(1, n_far):
        pl.semaphore_signal(barrier, inc=1, device_id=far_peer(o)[1], device_id_type=MESH)

    @pl.when(has_up)
    def _():
        pl.semaphore_signal(barrier, inc=1, device_id=up, device_id_type=MESH)

    @pl.when(has_down)
    def _():
        pl.semaphore_signal(barrier, inc=1, device_id=down, device_id_type=MESH)

    @pl.when(at_bottom)
    def _():
        for k in range(ITERS):
            basis[k, 0] = jnp.zeros(plane, F32)

    @pl.when(at_top)
    def _():
        for k in range(ITERS):
            basis[k, rows + 1] = jnp.zeros(plane, F32)

    l_vertex.wait()
    l_volume.wait()
    target = jnp.where(solid, vertex[...], volume[...])
    cell_row, cell_col = target >> 8, target & 255
    lines = target.shape[0]
    points = lines * 128
    for j in range(lines):
        span = pl.ds(j * 128, 128)
        row_hot[:, span] = jnp.where(iota((cells, 128), 0) == cell_row[j : j + 1], 1.0, 0.0).astype(BF16)
        col_hot[:, span] = jnp.where(iota((depth, 128), 0) == cell_col[j : j + 1], 1.0, 0.0).astype(BF16)
    l_thermal.wait()
    high, low = pieces(thermal[...].reshape(cells, depth))
    hot = row_hot[...]
    found = dot(high, hot, ((0,), (0,))) + dot(low, hot, ((0,), (0,)))
    value = jnp.sum(found * col_hot[...].astype(F32), axis=0, keepdims=True)
    value = jnp.concatenate([value[:, j * 128 : (j + 1) * 128] for j in range(lines)], axis=0)
    l_part.wait()
    l_factor.wait()
    owned = jnp.where(part[...] == group, 1.0, 0.0)
    picked[0:lines] = jnp.where(solid, value, value * owned)
    picked[lines:] = jnp.zeros((8 - lines, 128), F32)

    pl.semaphore_wait(barrier, inner - 1 + n_far - 1 + has_up.astype(jnp.int32) + has_down.astype(jnp.int32))

    def wall_copy(g):
        return pltpu.make_async_remote_copy(
            picked, walls, contact_send.at[g], contact_recv.at[groups - 1], device_id=(g, brick), device_id_type=MESH
        )

    near_copy = pltpu.make_async_remote_copy(
        picked, nears.at[group], contact_send.at[0], contact_recv.at[group], device_id=(groups - 1, brick), device_id_type=MESH
    )

    @pl.when(solid)
    def _():
        for g in range(groups - 1):
            wall_copy(g).start()

    @pl.when(fluid)
    def _():
        near_copy.start()

    l_opening.wait()
    l_flow.wait()
    l_weight.wait()
    coef_a = pltpu.make_async_remote_copy(
        ax.at[rows], ax.at[0], coef_send.at[0], coef_recv.at[0], device_id=up, device_id_type=MESH
    )
    coef_g = pltpu.make_async_remote_copy(
        gx.at[rows], gx.at[0], coef_send.at[1], coef_recv.at[1], device_id=up, device_id_type=MESH
    )
    coef_up = pltpu.make_async_remote_copy(
        weight.at[rows - 1], weight_low, coef_send.at[0], coef_recv.at[0], device_id=up, device_id_type=MESH
    )
    coef_down = pltpu.make_async_remote_copy(
        weight.at[0], weight_up, coef_send.at[1], coef_recv.at[1], device_id=down, device_id_type=MESH
    )

    @pl.when(fluid)
    def _():
        last = jnp.where(at_top, 0.0, opening[0, rows - 1])
        ax[rows] = last
        gx[rows] = last * (1.0 + flow[0, rows - 1])

    @pl.when(fluid & has_up)
    def _():
        coef_a.start()
        coef_g.start()

    @pl.when(solid & has_up)
    def _():
        coef_up.start()

    @pl.when(solid & has_down)
    def _():
        coef_down.start()

    l_storage.wait()
    l_root.wait()
    l_rigid.wait()

    def spread(values):
        flat = jnp.concatenate([values[j : j + 1] for j in range(lines)], axis=1)
        high, low = pieces(flat)
        cols = col_hot[...].astype(F32)
        return dot(row_hot[...], (cols * high.astype(F32)).astype(BF16), ((1,), (1,))) + dot(
            row_hot[...], (cols * low.astype(F32)).astype(BF16), ((1,), (1,))
        )

    def fold(x, op):
        y = x.reshape(width // 8, 8, depth)
        return op(y, axis=0)

    y_at, z_at = iota(plane, 0), iota(plane, 1)

    def write_stats(d_max, d_min, o_sum):
        lane = iota((8, 128), 1)
        tile = jnp.where(lane == 0, greatest(d_max), jnp.where(lane == 1, greatest(-d_min), jnp.where(lane == 2, total(o_sum), 0.0)))
        near_slots[0, low_id, 0:8] = tile

    start = (jnp.full((8, depth), -1e30, F32), jnp.full((8, depth), 1e30, F32), jnp.zeros((8, depth), F32))

    @pl.when(fluid)
    def _():
        extra = spread(factor[...] * owned).reshape(rows, width, depth)
        storage[...] = storage[...] + extra

        def first(r, carry):
            a = opening[0, r]
            ax[r + 1] = a
            gx[r + 1] = a * (1.0 + flow[0, r])
            return carry

        lax.fori_loop(0, rows - 1, first, 0)

        @pl.when(has_down)
        def _():
            coef_a.wait_recv()
            coef_g.wait_recv()

        @pl.when(at_bottom)
        def _():
            ax[0] = jnp.zeros(plane, F32)
            gx[0] = jnp.zeros(plane, F32)

        def second(r, carry):
            d_max, d_min, o_sum = carry
            a_y = jnp.where(y_at == width - 1, 0.0, opening[1, r])
            g_y = a_y * (1.0 + flow[1, r])
            g_low = pltpu.roll(g_y, 1, 0)
            uy[r] = a_y
            ly[r] = g_low
            d = storage[r] + ax[r] + gx[r + 1] + g_y + pltpu.roll(a_y, 1, 0)
            o = ax[r + 1] + gx[r] + a_y + g_low
            a_z = jnp.where(z_at == depth - 1, 0.0, opening[2, r])
            g_z = a_z * (1.0 + flow[2, r])
            g_low = pltpu.roll(g_z, 1, 1)
            uz[r] = a_z
            lz[r] = g_low
            d = d + g_z + pltpu.roll(a_z, 1, 1)
            o = o + a_z + g_low
            diag[r] = d
            return jnp.maximum(d_max, fold(d, jnp.max)), jnp.minimum(d_min, fold(d, jnp.min)), o_sum + fold(o, jnp.sum)

        write_stats(*lax.fori_loop(0, rows, second, start))

    @pl.when(solid)
    def _():
        eye = iota((8, 8), 0) == iota((8, 8), 1)
        both = rigidity[0] + rigidity[1] + rigidity[2]
        size = jnp.abs(rigidity[0]) + jnp.abs(rigidity[1]) + jnp.abs(rigidity[2])
        trace = total(jnp.where(eye, both, 0.0)) * (1.0 / 8)
        off = total(jnp.where(eye, 0.0, size)) * (1.0 / 8)
        block_z = jnp.where(iota((8, depth), 1) % 8 == iota((8, depth), 0), 1.0, 0.0)
        spread_z = lax.dot_general(
            lax.dot_general(block_z, rigidity[2], (((0,), (1,)), ((), ())), precision=HIGH, preferred_element_type=F32),
            block_z,
            (((1,), (0,)), ((), ())),
            precision=HIGH,
            preferred_element_type=F32,
        )
        same = (iota((depth, depth), 0) // 8) == (iota((depth, depth), 1) // 8)
        high, low = pieces(jnp.where(same, spread_z, 0.0))
        wz[0], wz[1] = high, low
        outer_x = jnp.where(iota((8, 64), 1) // 8 == iota((8, 64), 0), 1.0, 0.0)
        inner_y = jnp.where(iota((8, 64), 1) % 8 == iota((8, 64), 0), 1.0, 0.0)

        def expand(matrix, hot):
            left = lax.dot_general(hot, matrix, (((0,), (0,)), ((), ())), precision=HIGH, preferred_element_type=F32)
            return lax.dot_general(left, hot, (((1,), (0,)), ((), ())), precision=HIGH, preferred_element_type=F32)

        same_y = iota((64, 64), 0) % 8 == iota((64, 64), 1) % 8
        same_x = iota((64, 64), 0) // 8 == iota((64, 64), 1) // 8
        mixed = jnp.where(same_y, expand(rigidity[0], outer_x), 0.0) + jnp.where(same_x, expand(rigidity[1], inner_y), 0.0)
        high, low = pieces(mixed)
        wxy[...] = jnp.concatenate([high, high, low], axis=1)

        @pl.when(has_down)
        def _():
            coef_up.wait_recv()
            gx[0] = 0.5 * (weight_low[...] + weight[0])

        @pl.when(at_bottom)
        def _():
            gx[0] = jnp.zeros(plane, F32)

        @pl.when(has_up)
        def _():
            coef_down.wait_recv()
            ax[rows] = 0.5 * (weight[rows - 1] + weight_up[...])

        @pl.when(at_top)
        def _():
            ax[rows] = jnp.zeros(plane, F32)

        def second(r, carry):
            d_max, d_min, o_sum = carry
            w = weight[r]
            b_y = jnp.where((y_at % 8 == 7) & (y_at < width - 1), 0.5 * (w + pltpu.roll(w, width - 1, 0)), 0.0)
            b_low = pltpu.roll(b_y, 1, 0)
            uy[r] = b_y
            ly[r] = b_low
            pair = b_y + b_low
            b_z = jnp.where((z_at % 8 == 7) & (z_at < depth - 1), 0.5 * (w + pltpu.roll(w, depth - 1, 1)), 0.0)
            b_low = pltpu.roll(b_z, 1, 1)
            uz[r] = b_z
            lz[r] = b_low
            pair = pair + b_z + b_low
            d = storage[r] + pair
            diag[r] = d
            square = root[r] * root[r]
            whole = d + square * trace
            o = pair + square * off
            return jnp.maximum(d_max, fold(whole, jnp.max)), jnp.minimum(d_min, fold(whole, jnp.min)), o_sum + fold(o, jnp.sum)

        write_stats(*lax.fori_loop(0, rows, second, start))
        diag[0] = diag[0] + gx[0]
        diag[rows - 1] = diag[rows - 1] + ax[rows]

    def near_start(which, height):
        for o in range(1, inner):
            peer, where = near_peer(o)
            pltpu.make_async_remote_copy(
                near_slots.at[which, low_id, pl.ds(0, height)],
                near_slots.at[which, low_id, pl.ds(0, height)],
                near_send.at[which, o],
                near_recv.at[which, low_id],
                device_id=where,
                device_id_type=MESH,
            ).start()

    def near_wait(which, height):
        for o in range(1, inner):
            peer, where = near_peer(o)
            copy = pltpu.make_async_remote_copy(
                near_slots.at[which, peer, pl.ds(0, height)],
                near_slots.at[which, peer, pl.ds(0, height)],
                near_send.at[which, o],
                near_recv.at[which, peer],
                device_id=where,
                device_id_type=MESH,
            )
            copy.wait_recv()
            copy.wait_send()

    def far_start(which, height):
        for o in range(1, n_far):
            peer, where = far_peer(o)
            pltpu.make_async_remote_copy(
                far_slots.at[which, high_id, pl.ds(0, height)],
                far_slots.at[which, high_id, pl.ds(0, height)],
                far_send.at[which, o],
                far_recv.at[which, high_id],
                device_id=where,
                device_id_type=MESH,
            ).start()

    def far_wait(which, height):
        for o in range(1, n_far):
            peer, where = far_peer(o)
            copy = pltpu.make_async_remote_copy(
                far_slots.at[which, peer, pl.ds(0, height)],
                far_slots.at[which, peer, pl.ds(0, height)],
                far_send.at[which, o],
                far_recv.at[which, peer],
                device_id=where,
                device_id_type=MESH,
            )
            copy.wait_recv()
            copy.wait_send()

    def merge_stats(tiles):
        lane = iota((8, 128), 1)
        most, summed = tiles[0], tiles[0]
        for tile in tiles[1:]:
            most, summed = jnp.maximum(most, tile), summed + tile
        return jnp.where(lane == 2, summed, most)

    near_start(0, 8)

    l_forcing.wait()

    def halo_up(k):
        return pltpu.make_async_remote_copy(
            basis.at[k, rows], basis.at[k, 0], halo_send.at[k, 0], halo_recv.at[k, 0], device_id=up, device_id_type=MESH
        )

    def halo_down(k):
        return pltpu.make_async_remote_copy(
            basis.at[k, 1], basis.at[k, rows + 1], halo_send.at[k, 1], halo_recv.at[k, 1], device_id=down, device_id_type=MESH
        )

    def send_halos(k):
        @pl.when(has_up)
        def _():
            halo_up(k).start()

        @pl.when(has_down)
        def _():
            halo_down(k).start()

    @pl.when(fluid)
    def _():
        pltpu.make_async_remote_copy(
            picked, walls, contact_send.at[0], contact_recv.at[groups - 1], device_id=(groups - 1, brick), device_id_type=MESH
        ).wait_recv()

    @pl.when(solid)
    def _():
        for g in range(groups - 1):
            pltpu.make_async_remote_copy(
                picked, nears.at[g], contact_send.at[g], contact_recv.at[g], device_id=(g, brick), device_id_type=MESH
            ).wait_recv()
        walls[...] = nears[0] + nears[1] + nears[2] - picked[...]

    heat = factor[...] * walls[0:lines]
    extra = spread(jnp.where(solid, heat, heat * owned)).reshape(rows, width, depth)
    basis[0, 1 : rows + 1] = forcing[...] + extra
    send_halos(0)

    near_wait(0, 8)
    far_slots[0, high_id, 0:8] = merge_stats([near_slots[0, i, 0:8] for i in range(inner)])
    far_start(0, 8)

    def gram_row(k):
        def body(r, accs):
            accs = list(accs)
            for j in range(width // 8):
                span = slice(8 * j, 8 * j + 8)
                mine = basis[k, r + 1, span, :]
                for i in range(k + 1):
                    other = mine if i == k else basis[i, r + 1, span, :]
                    accs[i] = accs[i] + mine * other
            return tuple(accs)

        accs = lax.fori_loop(0, rows, body, tuple(jnp.zeros((8, depth), F32) for _ in range(k + 1)))
        row, lane = iota((16, 128), 0), iota((16, 128), 1)
        tile = jnp.zeros((16, 128), F32) if k == 0 else gram_tile[...]
        for i in range(k + 1):
            spot = ((row == i) & (lane == k)) | ((row == k) & (lane == i))
            tile = jnp.where(spot, total(accs[i]), tile)
        gram_tile[...] = tile

    def local(r, v):
        return (
            diag[r] * v
            - uy[r] * pltpu.roll(v, width - 1, 0)
            - ly[r] * pltpu.roll(v, 1, 0)
            - uz[r] * pltpu.roll(v, depth - 1, 1)
            - lz[r] * pltpu.roll(v, 1, 1)
        )

    def apply(k, scale):
        def keep(r, q):
            if k == 0:
                basis[1, r + 1] = q
            else:
                basis[k + 1, r + 1] = scale * q - basis[k - 1, r + 1]

        @pl.when(fluid)
        def _():
            def middle(r, carry):
                v = basis[k, r + 1]
                keep(r, local(r, v) - gx[r] * basis[k, r] - ax[r + 1] * basis[k, r + 2])
                return carry

            keep(0, local(0, basis[k, 1]) - ax[1] * basis[k, 2])
            keep(rows - 1, local(rows - 1, basis[k, rows]) - gx[rows - 1] * basis[k, rows - 1])
            lax.fori_loop(1, rows - 1, middle, 0)

        @pl.when(solid)
        def _():
            for e in range(width // 8):
                u = (root[:, 8 * e : 8 * e + 8, :] * basis[k, 1 : rows + 1, 8 * e : 8 * e + 8, :]).reshape(64, depth)
                high, low = pieces(u)
                uh[e], ul[e] = high, low
                stiff[e] = dot(wxy[...], jnp.concatenate([high, low, high], axis=0), ((1,), (0,)))
            high, low = uh[...].reshape(cells, depth), ul[...].reshape(cells, depth)
            along = dot(high, wz[0], ((1,), (0,))) + dot(low, wz[0], ((1,), (0,))) + dot(high, wz[1], ((1,), (0,)))
            stiff[...] = stiff[...] + along.reshape(width // 8, 64, depth)

            def each(r, carry):
                force = stiff[:, pl.ds(r * 8, 8), :].reshape(width, depth)
                keep(r, local(r, basis[k, r + 1]) + root[r] * force)
                return carry

            lax.fori_loop(0, rows, each, 0)

    def finish(k, scale):
        @pl.when(has_down)
        def _():
            halo_up(k).wait_recv()

        @pl.when(has_up)
        def _():
            halo_down(k).wait_recv()

        low = gx[0] * basis[k, 0]
        top = ax[rows] * basis[k, rows + 1]
        if k == 0:
            basis[1, 1] = basis[1, 1] - low
            basis[1, rows] = basis[1, rows] - top
        else:
            basis[k + 1, 1] = basis[k + 1, 1] - scale * low
            basis[k + 1, rows] = basis[k + 1, rows] - scale * top

    apply(0, None)
    finish(0, None)
    gram_row(0)
    far_wait(0, 8)
    split = (groups - 1) * outer

    def interval(tiles, count):
        stats = merge_stats(tiles)
        mean = stats[0:1, 2:3] * (1.0 / count)
        high = stats[0:1, 0:1] + 0.25 * mean
        low = jnp.maximum(-stats[0:1, 1:2] - 0.5 * mean, 0.0)
        return 0.5 * (high + low), 0.5 * (high - low)

    c_fluid, e_fluid = interval([far_slots[0, i, 0:8] for i in range(split)], float((groups - 1) * bricks * cells * depth))
    c_solid, e_solid = interval([far_slots[0, i, 0:8] for i in range(split, n_far)], float(bricks * cells * depth))
    center = jnp.where(solid, c_solid, c_fluid)
    inv_e = 1.0 / jnp.where(solid, e_solid, e_fluid)
    scale = 2.0 * inv_e

    def rescale(r):
        basis[1, r + 1] = (basis[1, r + 1] - center * basis[0, r + 1]) * inv_e
        diag[r] = diag[r] - center

    rescale(0)
    rescale(rows - 1)
    send_halos(1)

    def rescale_body(r, carry):
        rescale(r)
        return carry

    lax.fori_loop(1, rows - 1, rescale_body, 0)
    for k in range(1, ITERS):
        apply(k, scale)
        gram_row(k)
        finish(k, scale)
        if k + 1 < ITERS:
            send_halos(k + 1)
    gram_row(ITERS)

    near_slots[1, low_id] = gram_tile[...]
    near_start(1, 16)
    near_wait(1, 16)
    summed = near_slots[1, 0]
    for i in range(1, inner):
        summed = summed + near_slots[1, i]
    far_slots[1, high_id] = summed
    far_start(1, 16)
    far_wait(1, 16)
    gram_fluid = far_slots[1, 0]
    for i in range(1, split):
        gram_fluid = gram_fluid + far_slots[1, i]
    gram_solid = far_slots[1, split]
    for i in range(split + 1, n_far):
        gram_solid = gram_solid + far_slots[1, i]
    y_fluid, ok_fluid = projected(gram_fluid, c_fluid / e_fluid, True)
    y_solid, ok_solid = projected(gram_solid, c_solid / e_solid, False)
    coeffs = jnp.where(solid, y_solid, y_fluid) * inv_e
    flag[...] = jnp.broadcast_to(ok_fluid * ok_solid, (8, 128))
    weights = [coeffs[k : k + 1, :1] for k in range(ITERS)]

    def combine(r, carry):
        acc = weights[0] * basis[0, r + 1]
        for k in range(1, ITERS):
            acc = acc + weights[k] * basis[k, r + 1]
        out[r] = acc
        return carry

    lax.fori_loop(0, rows, combine, 0)
    stores = [
        pltpu.make_async_copy(out, out_hbm, store_sem.at[0]),
        pltpu.make_async_copy(flag, flag_hbm, store_sem.at[1]),
    ]
    for store in stores:
        store.start()

    @pl.when(solid)
    def _():
        for g in range(groups - 1):
            wall_copy(g).wait_send()

    @pl.when(fluid)
    def _():
        near_copy.wait_send()

    @pl.when(fluid & has_up)
    def _():
        coef_a.wait_send()
        coef_g.wait_send()

    @pl.when(solid & has_up)
    def _():
        coef_up.wait_send()

    @pl.when(solid & has_down)
    def _():
        coef_down.wait_send()

    for k in range(ITERS):
        @pl.when(has_up)
        def _():
            halo_up(k).wait_send()

        @pl.when(has_down)
        def _():
            halo_down(k).wait_send()

    for store in stores:
        store.wait()


def shards(*arguments):
    groups, bricks = lax.axis_size("group"), lax.axis_size("brick")
    forcing = arguments[0]
    rows, width, depth = slab = forcing.shape
    lines = arguments[8].shape[0]
    points = lines * 128
    n_far = groups * (bricks // 8)
    vm = pltpu.VMEM
    scratch = (
        [vm(slab, F32)] * 3
        + [vm((3,) + slab, F32)] * 2
        + [vm(slab, F32)] * 2
        + [vm((3, 8, 8), F32)]
        + [vm((lines, 128), jnp.int32)] * 3
        + [vm((lines, 128), F32)]
        + [vm((ITERS + 1, rows + 2, width, depth), F32)]
        + [vm((rows + 1, width, depth), F32)] * 2
        + [vm(slab, F32)] * 5
        + [vm((width // 8, 64, depth), F32)]
        + [vm((width // 8, 64, depth), BF16)] * 2
        + [vm((2, depth, depth), BF16), vm((64, 192), BF16)]
        + [vm((width, depth), F32)] * 2
        + [vm((rows * width, points), BF16), vm((depth, points), BF16)]
        + [vm((8, 128), F32)] * 2
        + [vm((groups - 1, 8, 128), F32)]
        + [vm((16, 128), F32), vm((2, 8, 16, 128), F32), vm((2, n_far, 16, 128), F32)]
        + [vm(slab, F32), vm((8, 128), F32)]
    )
    dma = pltpu.SemaphoreType.DMA
    semaphores = [
        dma((12,)),
        dma((2,)),
        dma((ITERS, 2)),
        dma((ITERS, 2)),
        dma((2,)),
        dma((2,)),
        dma((groups,)),
        dma((groups,)),
        dma((2, 8)),
        dma((2, 8)),
        dma((2, n_far)),
        dma((2, n_far)),
    ]
    result, flag = pl.pallas_call(
        functools.partial(kernel, groups, bricks),
        out_shape=(jax.ShapeDtypeStruct(slab, F32), jax.ShapeDtypeStruct((8, 128), F32)),
        in_specs=[pl.BlockSpec(memory_space=pl.ANY)] * 12,
        out_specs=(pl.BlockSpec(memory_space=pl.ANY),) * 2,
        scratch_shapes=scratch + semaphores,
        compiler_params=pltpu.CompilerParams(collective_id=0, has_side_effects=True, vmem_limit_bytes=56 * 2**20),
        name="coupled",
    )(*arguments)
    return lax.cond(flag[0, 0] > 0.5, lambda: result, lambda: iterated(*arguments))


def solution(mesh):
    return jax.shard_map(
        shards,
        mesh=mesh,
        in_specs=(
            P(("group", "brick"), None, None),
            P(("group", "brick"), None, None),
            P(("group", "brick"), None, None),
            P(None, ("group", "brick"), None, None),
            P(None, ("group", "brick"), None, None),
            P(("group", "brick"), None, None),
            P(("group", "brick"), None, None),
            P(),
            P("brick", None),
            P("brick", None),
            P("brick", None),
            P("brick", None),
        ),
        out_specs=P(("group", "brick"), None, None),
        check_vma=False,
    )
```

```python
import functools

import jax
import jax.numpy as jnp
from jax import lax
from jax.experimental import pallas as pl
from jax.experimental.pallas import tpu as pltpu
from jax.sharding import PartitionSpec as P

ITERS = 8


HIGH = lax.Precision.HIGHEST


def passed_along(value, axis, steps):
    count = lax.axis_size(axis)
    leading, last = (max(0, -steps), min(count, count - steps))
    return lax.ppermute(value, axis, [(source, source + steps) for source in range(leading, last)])


def extended(cells, sides, width):
    for axis, dim in sides:
        count = lax.axis_size(axis)
        ends = count - 1
        head = lax.slice_in_dim(cells, 0, width, axis=dim)
        tail = lax.slice_in_dim(cells, cells.shape[dim] - width, cells.shape[dim], axis=dim)
        cells = jnp.concatenate(
            [
                lax.ppermute(tail, axis, [(i, (i + 1) % count) for i in range(ends)]),
                cells,
                lax.ppermute(head, axis, [((i + 1) % count, i) for i in range(ends)]),
            ],
            axis=dim,
        )
    return cells


def shift_next(v, axis):
    size = v.shape[axis]
    inner = lax.slice_in_dim(v, 1, size, axis=axis)
    zero = jnp.zeros_like(lax.slice_in_dim(v, 0, 1, axis=axis))
    return jnp.concatenate([inner, zero], axis=axis)


def shift_prev(v, axis):
    size = v.shape[axis]
    inner = lax.slice_in_dim(v, 0, size - 1, axis=axis)
    zero = jnp.zeros_like(lax.slice_in_dim(v, 0, 1, axis=axis))
    return jnp.concatenate([zero, inner], axis=axis)


def open_faces(shape, axis):
    index = lax.broadcasted_iota(jnp.int32, shape, axis)
    return (index < shape[axis] - 1).astype(jnp.float32)


def element_faces(shape, axis, nodes):
    index = lax.broadcasted_iota(jnp.int32, shape, axis)
    inside = (index % nodes == nodes - 1) & (index < shape[axis] - 1)
    return inside.astype(jnp.float32)


def stiffness_apply(u, rigidity_matrix):
    nodes = rigidity_matrix.shape[1]
    rows, width, depth = u.shape
    block = min(depth, 128)
    along_x = jnp.einsum("pq,qyz->pyz", rigidity_matrix[0], u, precision=HIGH)
    split_y = u.reshape(rows, width // nodes, nodes, depth)
    along_y = jnp.einsum("pq,xeqz->xepz", rigidity_matrix[1], split_y, precision=HIGH).reshape(
        rows, width, depth
    )
    wide = jnp.kron(jnp.eye(block // nodes, dtype=jnp.float32), rigidity_matrix[2])
    split_z = u.reshape(rows, width, depth // block, block)
    along_z = jnp.einsum("xyeq,pq->xyep", split_z, wide, precision=HIGH).reshape(rows, width, depth)
    return along_x + along_y + along_z


def least_squares(hess, beta):
    gram = jnp.dot(hess.T, hess, precision=HIGH)
    lower = jnp.linalg.cholesky(gram)
    right = (beta * hess[0])[:, None]
    middle = lax.linalg.triangular_solve(lower, right, left_side=True, lower=True)
    coeffs = lax.linalg.triangular_solve(
        lower, middle, left_side=True, lower=True, transpose_a=True
    )
    return coeffs[:, 0]


def iterated(
    forcing_vector,
    thermal_iterate,
    storage_over_step,
    opening_shares,
    flow_speed,
    diffusivity_root,
    sanction_weight,
    rigidity_matrix,
    contact_fluid_part,
    contact_fluid_volume,
    contact_solid_vertex,
    exchange_rate_factor,
):
    groups = lax.axis_size("group")
    bricks = lax.axis_size("brick")
    group_id = lax.axis_index("group")
    brick_id = lax.axis_index("brick")
    solid = group_id == groups - 1
    solid_flag = solid.astype(jnp.float32)
    fluid_flag = 1.0 - solid_flag
    rows, width, depth = forcing_vector.shape
    nodes = rigidity_matrix.shape[1]
    device = group_id * bricks + brick_id
    first_solid = (groups - 1) * bricks
    unrolled_array = thermal_iterate.reshape(-1)
    owned = (contact_fluid_part == group_id).astype(jnp.float32)
    target = jnp.where(solid, contact_solid_vertex, contact_fluid_volume).reshape(-1)
    picked = unrolled_array[target].reshape(contact_solid_vertex.shape)
    wall, near = lax.psum((picked * solid_flag, picked * owned * fluid_flag), "group")
    extra_rhs = jnp.where(
        solid, exchange_rate_factor * (near - wall), exchange_rate_factor * wall * owned
    )
    extra_diag = exchange_rate_factor * owned * fluid_flag
    rhs = (
        forcing_vector.reshape(-1)
        .at[target]
        .add(extra_rhs.reshape(-1))
        .reshape(forcing_vector.shape)
    )
    fluid_diag = (
        storage_over_step.reshape(-1)
        .at[target]
        .add(extra_diag.reshape(-1))
        .reshape(forcing_vector.shape)
    )
    shape = (rows, width, depth)
    global_row = device * rows + lax.broadcasted_iota(jnp.int32, shape, 0)
    face_x = opening_shares[0] * (global_row != first_solid * rows - 1).astype(jnp.float32)
    face_y = opening_shares[1] * open_faces(shape, 1)
    face_z = opening_shares[2] * open_faces(shape, 2)
    rims = passed_along(
        jnp.stack([face_x[-1], flow_speed[0][-1], sanction_weight[-1]]), ("group", "brick"), 1
    )
    face_low = rims[0]
    speed_low = rims[1]
    weight_low = rims[2]
    pair_low = 0.5 * (weight_low + sanction_weight[0]) * (device != first_solid).astype(jnp.float32)
    pair_up = passed_along(pair_low, "brick", -1)
    pair_y = (
        0.5 * (sanction_weight + shift_next(sanction_weight, 1)) * element_faces(shape, 1, nodes)
    )
    pair_z = (
        0.5 * (sanction_weight + shift_next(sanction_weight, 2)) * element_faces(shape, 2, nodes)
    )
    local_square = jnp.sum(rhs * rhs)
    solution = jnp.zeros_like(rhs)
    resid = rhs
    columns = []
    fluid_square, solid_square = lax.psum(
        (local_square * fluid_flag, local_square * solid_flag), ("group", "brick")
    )
    beta = jnp.sqrt(fluid_square)
    basis = [rhs / beta]
    direction = rhs
    norm_now = solid_square
    for step in range(ITERS):
        vector = jnp.where(solid, direction, basis[step])
        padded = extended(vector, ((("group", "brick"), 0),), 1)
        below = padded[0]
        above = padded[-1]

        def fluid_branch(unused):
            following = jnp.concatenate([vector[1:], above[None]], axis=0)
            flux_x = face_x * ((1.0 + flow_speed[0]) * vector - following)
            flux_low = face_low * ((1.0 + speed_low) * below - vector[0])
            out = (
                fluid_diag * vector
                + flux_x
                - jnp.concatenate([flux_low[None], flux_x[:-1]], axis=0)
            )
            flux_y = face_y * ((1.0 + flow_speed[1]) * vector - shift_next(vector, 1))
            flux_z = face_z * ((1.0 + flow_speed[2]) * vector - shift_next(vector, 2))
            return out + flux_y - shift_prev(flux_y, 1) + flux_z - shift_prev(flux_z, 2)

        def solid_branch(unused):
            out = storage_over_step * vector + diffusivity_root * stiffness_apply(
                diffusivity_root * vector, rigidity_matrix
            )
            jump_up = pair_up * (vector[-1] - above)
            jump_low = pair_low * (below - vector[0])
            out = out.at[0].add(-jump_low).at[rows - 1].add(jump_up)
            jump_y = pair_y * (vector - shift_next(vector, 1))
            jump_z = pair_z * (vector - shift_next(vector, 2))
            return out + jump_y - shift_prev(jump_y, 1) + jump_z - shift_prev(jump_z, 2)

        image = lax.cond(solid, solid_branch, fluid_branch, 0)
        inner = jnp.stack([jnp.sum(basis[j] * image) for j in range(step + 1)])
        heights, curvature = lax.psum(
            (inner * fluid_flag, jnp.sum(direction * image) * solid_flag), ("group", "brick")
        )
        fresh = image
        for j in range(step + 1):
            fresh = fresh - heights[j] * basis[j]
        alpha = norm_now / curvature
        solution = solution + alpha * direction
        resid = resid - alpha * image
        fresh_square, norm_next = lax.psum(
            (jnp.sum(fresh * fresh) * fluid_flag, jnp.sum(resid * resid) * solid_flag),
            ("group", "brick"),
        )
        length = jnp.sqrt(fresh_square)
        basis.append(fresh / length)
        columns.append(
            jnp.concatenate([heights, length[None], jnp.zeros((ITERS - 1 - step,), jnp.float32)])
        )
        direction = resid + norm_next / norm_now * direction
        norm_now = norm_next
    coeffs = least_squares(jnp.stack(columns, axis=1), beta)
    fluid_new = jnp.zeros_like(rhs)
    for step in range(ITERS):
        fluid_new = fluid_new + coeffs[step] * basis[step]
    return jnp.where(solid, solution, fluid_new)


F32 = jnp.float32
BF16 = jnp.bfloat16
MESH = pl.DeviceIdType.MESH
PIVOT_LEAST = 1e-3
REFINE_MOST = 3e-4
PARTS = 4
RAW = {1: ITERS + 1, 2: ITERS + 2}


def iota(shape, dim):
    return lax.broadcasted_iota(jnp.int32, shape, dim)


def pieces(x):
    high = x.astype(BF16)
    return high, (x - high.astype(F32)).astype(BF16)


def total(x):
    return jnp.sum(jnp.sum(x, axis=0, keepdims=True), axis=1, keepdims=True)


def greatest(x):
    return jnp.max(jnp.max(x, axis=0, keepdims=True), axis=1, keepdims=True)


def dot(a, b, dims):
    return lax.dot_general(a, b, ((dims[0], dims[1]), ((), ())), preferred_element_type=F32)


def shift_rows(x, gamma):
    size = x.shape[0]
    after = pltpu.roll(x, size - 1, 0)
    row = iota(x.shape, 0)
    out = gamma * x + 0.5 * (pltpu.roll(x, 1, 0) + after) + jnp.where(row == 0, 0.5 * after, 0.0)
    return jnp.where(row < ITERS, out, 0.0)


def shift_lanes(x, gamma):
    size = x.shape[1]
    after = pltpu.roll(x, size - 1, 1)
    lane = iota(x.shape, 1)
    out = gamma * x + 0.5 * (pltpu.roll(x, 1, 1) + after) + jnp.where(lane == 0, 0.5 * after, 0.0)
    return jnp.where(lane < ITERS, out, 0.0)


def projected(gram, gamma, fluid):
    shape = gram.shape
    row, lane = iota(shape, 0), iota(shape, 1)
    wide = shift_lanes(gram, gamma)
    if fluid:
        normal, right = shift_rows(wide, gamma), shift_rows(gram, gamma)
    else:
        normal, right = jnp.where(row < ITERS, wide, 0.0), jnp.where(row < ITERS, gram, 0.0)
    table = jnp.where(lane < ITERS, normal, 0.0)
    table = jnp.where((lane == row + 8) & (row < ITERS), 1.0, table)
    table = jnp.where(lane == 16, pltpu.roll(right, 16, 1), table)
    margin = None
    for k in range(ITERS):
        pivot = table[k : k + 1, k : k + 1]
        spare = pivot - PIVOT_LEAST * normal[k : k + 1, k : k + 1]
        margin = spare if margin is None else jnp.minimum(margin, spare)
        scaled = table[k : k + 1, :] * (1.0 / pivot)
        column = jnp.where(row[:, :1] == k, 0.0, table[:, k : k + 1])
        table = jnp.where(row == k, scaled, table - column * scaled)
    coeffs = jnp.broadcast_to(table[:, 16:17], shape)
    inverse = jnp.where(lane < ITERS, pltpu.roll(table, shape[1] - 8, 1), 0.0)
    applied = gamma * coeffs + 0.5 * (pltpu.roll(coeffs, 1, 0) + pltpu.roll(coeffs, shape[0] - 1, 0))
    applied = applied + jnp.where(row == 1, 0.5 * pltpu.roll(coeffs, 1, 0), 0.0)
    rest = jnp.where(row == 0, 1.0, 0.0) - applied
    image = jnp.broadcast_to(jnp.sum(gram * rest, axis=0, keepdims=True), shape)
    image = shift_lanes(image, gamma) if fluid else jnp.where(lane < ITERS, image, 0.0)
    change = jnp.sum(inverse * image, axis=1, keepdims=True)
    coeffs = coeffs[:, :1] + change
    size = jnp.sum(jnp.abs(coeffs), axis=0, keepdims=True)
    moved = jnp.sum(jnp.abs(change), axis=0, keepdims=True)
    good = (margin > 0.0) & (moved < REFINE_MOST * size)
    return coeffs, jnp.where(good, 1.0, 0.0)


def ring_far(step, size):
    return min(step, size - step)


def kernel(
    groups,
    bricks,
    forcing_hbm,
    thermal_hbm,
    storage_hbm,
    opening_hbm,
    flow_hbm,
    root_hbm,
    weight_hbm,
    rigidity_hbm,
    part_hbm,
    volume_hbm,
    vertex_hbm,
    factor_hbm,
    out_hbm,
    flag,
    thermal,
    forcing,
    storage,
    opening,
    flow,
    root,
    weight,
    rigidity,
    part,
    volume,
    vertex,
    factor,
    basis,
    ax,
    gx,
    diag,
    uy,
    ly,
    uz,
    lz,
    stiff,
    uh,
    ul,
    wz,
    wxy,
    weight_low,
    weight_up,
    row_hot,
    col_hot,
    picked,
    walls,
    nears,
    gram_tile,
    near_slots,
    far_slots,
    out,
    load_sem,
    store_sem,
    halo_send,
    halo_recv,
    coef_send,
    coef_recv,
    contact_send,
    contact_recv,
    near_send,
    near_recv,
    far_send,
    far_recv,
):
    group = lax.axis_index("group")
    brick = lax.axis_index("brick")
    rows, width, depth = forcing.shape
    plane = (width, depth)
    cells = rows * width
    solid = group == groups - 1
    fluid = group != groups - 1
    inner, outer = 8, bricks // 8
    low_id = lax.rem(brick, inner)
    high_id = group * outer + brick // inner
    n_far = groups * outer
    at_top = (brick == bricks - 1) & (group >= groups - 2)
    at_bottom = (brick == 0) & ((group == 0) | (group == groups - 1))
    has_up, has_down = jnp.logical_not(at_top), jnp.logical_not(at_bottom)
    device = group * bricks + brick
    up_id = lax.rem(device + 1, groups * bricks)
    down_id = lax.rem(device + groups * bricks - 1, groups * bricks)
    up = (up_id // bricks, lax.rem(up_id, bricks))
    down = (down_id // bricks, lax.rem(down_id, bricks))

    names = [
        (vertex_hbm, vertex),
        (volume_hbm, volume),
        (thermal_hbm, thermal),
        (part_hbm, part),
        (factor_hbm, factor),
        (opening_hbm, opening),
        (flow_hbm, flow),
        (storage_hbm, storage),
        (weight_hbm, weight),
        (root_hbm, root),
        (rigidity_hbm, rigidity),
        (forcing_hbm, forcing),
    ]
    loads = [pltpu.make_async_copy(s, d, load_sem.at[i]) for i, (s, d) in enumerate(names)]
    for load in loads:
        load.start()
    (l_vertex, l_volume, l_thermal, l_part, l_factor, l_opening, l_flow, l_storage, l_weight, l_root, l_rigid, l_forcing) = loads

    plane_id = brick // inner
    near_peers, far_peers = [], []
    for dz, dc in sorted(((a, b) for a in range(inner // 2) for b in range(2)), key=lambda at: -ring_far(at[0], inner // 2)):
        if dz or dc:
            peer = lax.rem(low_id // 2 + dz, inner // 2) * 2 + lax.rem(low_id + dc, 2)
            near_peers.append((peer, (group, plane_id * inner + peer)))
    steps = sorted(
        ((a, b) for a in range(groups) for b in range(outer)), key=lambda at: -ring_far(at[0], groups) - ring_far(at[1], outer)
    )
    for dx, dy in steps:
        if dx or dy:
            x_id, y_id = lax.rem(group + dx, groups), lax.rem(plane_id + dy, outer)
            far_peers.append((x_id * outer + y_id, (x_id, y_id * inner + low_id)))

    barrier = pltpu.get_barrier_semaphore()
    for peer, where in far_peers + near_peers:
        pl.semaphore_signal(barrier, inc=1, device_id=where, device_id_type=MESH)

    @pl.when(has_up)
    def _():
        pl.semaphore_signal(barrier, inc=1, device_id=up, device_id_type=MESH)

    @pl.when(has_down)
    def _():
        pl.semaphore_signal(barrier, inc=1, device_id=down, device_id_type=MESH)

    @pl.when(at_bottom)
    def _():
        for k in range(ITERS):
            basis[RAW.get(k, k), 0] = jnp.zeros(plane, F32)

    @pl.when(at_top)
    def _():
        for k in range(ITERS):
            basis[RAW.get(k, k), rows + 1] = jnp.zeros(plane, F32)

    l_vertex.wait()
    l_volume.wait()
    target = jnp.where(solid, vertex[...], volume[...])
    cell_row, cell_col = target >> 8, target & 255
    lines = target.shape[0]
    points = lines * 128
    for j in range(lines):
        span = pl.ds(j * 128, 128)
        row_hot[:, span] = jnp.where(iota((cells, 128), 0) == cell_row[j : j + 1], 1.0, 0.0).astype(BF16)
        col_hot[:, span] = jnp.where(iota((depth, 128), 0) == cell_col[j : j + 1], 1.0, 0.0).astype(BF16)
    l_thermal.wait()
    high, low = pieces(thermal[...].reshape(cells, depth))
    hot = row_hot[...]
    found = dot(high, hot, ((0,), (0,))) + dot(low, hot, ((0,), (0,)))
    value = jnp.sum(found * col_hot[...].astype(F32), axis=0, keepdims=True)
    value = jnp.concatenate([value[:, j * 128 : (j + 1) * 128] for j in range(lines)], axis=0)
    l_part.wait()
    l_factor.wait()
    owned = jnp.where(part[...] == group, 1.0, 0.0)
    picked[0:lines] = jnp.where(solid, value, value * owned)
    picked[lines:] = jnp.zeros((8 - lines, 128), F32)

    pl.semaphore_wait(barrier, inner - 1 + n_far - 1 + has_up.astype(jnp.int32) + has_down.astype(jnp.int32))

    def wall_copy(g):
        return pltpu.make_async_remote_copy(
            picked, walls, contact_send.at[g], contact_recv.at[groups - 1], device_id=(g, brick), device_id_type=MESH
        )

    near_copy = pltpu.make_async_remote_copy(
        picked, nears.at[group], contact_send.at[0], contact_recv.at[group], device_id=(groups - 1, brick), device_id_type=MESH
    )

    @pl.when(solid)
    def _():
        for g in range(groups - 1):
            wall_copy(g).start()

    @pl.when(fluid)
    def _():
        near_copy.start()

    l_opening.wait()
    l_flow.wait()
    l_weight.wait()
    coef_a = pltpu.make_async_remote_copy(
        ax.at[rows], ax.at[0], coef_send.at[0], coef_recv.at[0], device_id=up, device_id_type=MESH
    )
    coef_g = pltpu.make_async_remote_copy(
        gx.at[rows], gx.at[0], coef_send.at[1], coef_recv.at[1], device_id=up, device_id_type=MESH
    )
    coef_up = pltpu.make_async_remote_copy(
        weight.at[rows - 1], weight_low, coef_send.at[0], coef_recv.at[0], device_id=up, device_id_type=MESH
    )
    coef_down = pltpu.make_async_remote_copy(
        weight.at[0], weight_up, coef_send.at[1], coef_recv.at[1], device_id=down, device_id_type=MESH
    )

    @pl.when(fluid)
    def _():
        last = jnp.where(at_top, 0.0, opening[0, rows - 1])
        ax[rows] = last
        gx[rows] = last * (1.0 + flow[0, rows - 1])

    @pl.when(fluid & has_up)
    def _():
        coef_a.start()
        coef_g.start()

    @pl.when(solid & has_up)
    def _():
        coef_up.start()

    @pl.when(solid & has_down)
    def _():
        coef_down.start()

    l_storage.wait()
    l_root.wait()
    l_rigid.wait()

    def spread(values):
        flat = jnp.concatenate([values[j : j + 1] for j in range(lines)], axis=1)
        high, low = pieces(flat)
        cols = col_hot[...].astype(F32)
        return dot(row_hot[...], (cols * high.astype(F32)).astype(BF16), ((1,), (1,))) + dot(
            row_hot[...], (cols * low.astype(F32)).astype(BF16), ((1,), (1,))
        )

    def fold(x, op):
        y = x.reshape(width // 8, 8, depth)
        return op(y, axis=0)

    y_at, z_at = iota(plane, 0), iota(plane, 1)

    def write_stats(d_max, d_min, o_sum):
        lane = iota((8, 128), 1)
        tile = jnp.where(lane == 0, greatest(d_max), jnp.where(lane == 1, greatest(-d_min), jnp.where(lane == 2, total(o_sum), 0.0)))
        near_slots[0, low_id, 0:8] = tile

    start = (jnp.full((8, depth), -1e30, F32), jnp.full((8, depth), 1e30, F32), jnp.zeros((8, depth), F32))

    @pl.when(fluid)
    def _():
        extra = spread(factor[...] * owned).reshape(rows, width, depth)
        storage[...] = storage[...] + extra

        def first(r, carry):
            a = opening[0, r]
            ax[r + 1] = a
            gx[r + 1] = a * (1.0 + flow[0, r])
            return carry

        lax.fori_loop(0, rows - 1, first, 0)

        @pl.when(has_down)
        def _():
            coef_a.wait_recv()
            coef_g.wait_recv()

        @pl.when(at_bottom)
        def _():
            ax[0] = jnp.zeros(plane, F32)
            gx[0] = jnp.zeros(plane, F32)

        def second(r, carry):
            d_max, d_min, o_sum = carry
            a_y = jnp.where(y_at == width - 1, 0.0, opening[1, r])
            g_y = a_y * (1.0 + flow[1, r])
            g_low = pltpu.roll(g_y, 1, 0)
            uy[r] = a_y
            ly[r] = g_low
            d = storage[r] + ax[r] + gx[r + 1] + g_y + pltpu.roll(a_y, 1, 0)
            o = ax[r + 1] + gx[r] + a_y + g_low
            a_z = jnp.where(z_at == depth - 1, 0.0, opening[2, r])
            g_z = a_z * (1.0 + flow[2, r])
            g_low = pltpu.roll(g_z, 1, 1)
            uz[r] = a_z
            lz[r] = g_low
            d = d + g_z + pltpu.roll(a_z, 1, 1)
            o = o + a_z + g_low
            diag[r] = d
            return jnp.maximum(d_max, fold(d, jnp.max)), jnp.minimum(d_min, fold(d, jnp.min)), o_sum + fold(o, jnp.sum)

        write_stats(*lax.fori_loop(0, rows, second, start))

    @pl.when(solid)
    def _():
        eye = iota((8, 8), 0) == iota((8, 8), 1)
        both = rigidity[0] + rigidity[1] + rigidity[2]
        size = jnp.abs(rigidity[0]) + jnp.abs(rigidity[1]) + jnp.abs(rigidity[2])
        trace = total(jnp.where(eye, both, 0.0)) * (1.0 / 8)
        off = total(jnp.where(eye, 0.0, size)) * (1.0 / 8)
        block_z = jnp.where(iota((8, depth), 1) % 8 == iota((8, depth), 0), 1.0, 0.0)
        spread_z = lax.dot_general(
            lax.dot_general(block_z, rigidity[2], (((0,), (1,)), ((), ())), precision=HIGH, preferred_element_type=F32),
            block_z,
            (((1,), (0,)), ((), ())),
            precision=HIGH,
            preferred_element_type=F32,
        )
        same = (iota((depth, depth), 0) // 8) == (iota((depth, depth), 1) // 8)
        high, low = pieces(jnp.where(same, spread_z, 0.0))
        wz[0], wz[1] = high, low
        outer_x = jnp.where(iota((8, 64), 1) // 8 == iota((8, 64), 0), 1.0, 0.0)
        inner_y = jnp.where(iota((8, 64), 1) % 8 == iota((8, 64), 0), 1.0, 0.0)

        def expand(matrix, hot):
            left = lax.dot_general(hot, matrix, (((0,), (0,)), ((), ())), precision=HIGH, preferred_element_type=F32)
            return lax.dot_general(left, hot, (((1,), (0,)), ((), ())), precision=HIGH, preferred_element_type=F32)

        same_y = iota((64, 64), 0) % 8 == iota((64, 64), 1) % 8
        same_x = iota((64, 64), 0) // 8 == iota((64, 64), 1) // 8
        mixed = jnp.where(same_y, expand(rigidity[0], outer_x), 0.0) + jnp.where(same_x, expand(rigidity[1], inner_y), 0.0)
        high, low = pieces(mixed)
        wxy[...] = jnp.concatenate([high, high, low], axis=1)

        @pl.when(has_down)
        def _():
            coef_up.wait_recv()
            gx[0] = 0.5 * (weight_low[...] + weight[0])

        @pl.when(at_bottom)
        def _():
            gx[0] = jnp.zeros(plane, F32)

        @pl.when(has_up)
        def _():
            coef_down.wait_recv()
            ax[rows] = 0.5 * (weight[rows - 1] + weight_up[...])

        @pl.when(at_top)
        def _():
            ax[rows] = jnp.zeros(plane, F32)

        def second(r, carry):
            d_max, d_min, o_sum = carry
            w = weight[r]
            b_y = jnp.where((y_at % 8 == 7) & (y_at < width - 1), 0.5 * (w + pltpu.roll(w, width - 1, 0)), 0.0)
            b_low = pltpu.roll(b_y, 1, 0)
            uy[r] = b_y
            ly[r] = b_low
            pair = b_y + b_low
            b_z = jnp.where((z_at % 8 == 7) & (z_at < depth - 1), 0.5 * (w + pltpu.roll(w, depth - 1, 1)), 0.0)
            b_low = pltpu.roll(b_z, 1, 1)
            uz[r] = b_z
            lz[r] = b_low
            pair = pair + b_z + b_low
            d = storage[r] + pair
            diag[r] = d
            square = root[r] * root[r]
            whole = d + square * trace
            o = pair + square * off
            return jnp.maximum(d_max, fold(whole, jnp.max)), jnp.minimum(d_min, fold(whole, jnp.min)), o_sum + fold(o, jnp.sum)

        write_stats(*lax.fori_loop(0, rows, second, start))
        diag[0] = diag[0] + gx[0]
        diag[rows - 1] = diag[rows - 1] + ax[rows]

    def near_start(which, height):
        for o, (peer, where) in enumerate(near_peers):
            pltpu.make_async_remote_copy(
                near_slots.at[which, low_id, pl.ds(0, height)],
                near_slots.at[which, low_id, pl.ds(0, height)],
                near_send.at[which, o],
                near_recv.at[which, low_id],
                device_id=where,
                device_id_type=MESH,
            ).start()

    def near_wait(which, height):
        for o, (peer, where) in enumerate(near_peers):
            copy = pltpu.make_async_remote_copy(
                near_slots.at[which, peer, pl.ds(0, height)],
                near_slots.at[which, peer, pl.ds(0, height)],
                near_send.at[which, o],
                near_recv.at[which, peer],
                device_id=where,
                device_id_type=MESH,
            )
            copy.wait_recv()
            copy.wait_send()

    def far_start(which, height):
        for o, (peer, where) in enumerate(far_peers):
            pltpu.make_async_remote_copy(
                far_slots.at[which, high_id, pl.ds(0, height)],
                far_slots.at[which, high_id, pl.ds(0, height)],
                far_send.at[which, o],
                far_recv.at[which, high_id],
                device_id=where,
                device_id_type=MESH,
            ).start()

    def far_wait(which, height):
        for o, (peer, where) in enumerate(far_peers):
            copy = pltpu.make_async_remote_copy(
                far_slots.at[which, peer, pl.ds(0, height)],
                far_slots.at[which, peer, pl.ds(0, height)],
                far_send.at[which, o],
                far_recv.at[which, peer],
                device_id=where,
                device_id_type=MESH,
            )
            copy.wait_recv()
            copy.wait_send()

    def merge_stats(tiles):
        lane = iota((8, 128), 1)
        most, summed = tiles[0], tiles[0]
        for tile in tiles[1:]:
            most, summed = jnp.maximum(most, tile), summed + tile
        return jnp.where(lane == 2, summed, most)

    near_start(0, 8)

    l_forcing.wait()

    part_rows = width // PARTS

    def halo_up(k, j):
        span = pl.ds(j * part_rows, part_rows)
        at = RAW.get(k, k)
        return pltpu.make_async_remote_copy(
            basis.at[at, rows, span],
            basis.at[at, 0, span],
            halo_send.at[k, 0, j],
            halo_recv.at[k, 0, j],
            device_id=up,
            device_id_type=MESH,
        )

    def halo_down(k, j):
        span = pl.ds(j * part_rows, part_rows)
        at = RAW.get(k, k)
        return pltpu.make_async_remote_copy(
            basis.at[at, 1, span],
            basis.at[at, rows + 1, span],
            halo_send.at[k, 1, j],
            halo_recv.at[k, 1, j],
            device_id=down,
            device_id_type=MESH,
        )

    def send_halos(k, j):
        @pl.when(has_up)
        def _():
            halo_up(k, j).start()

        @pl.when(has_down)
        def _():
            halo_down(k, j).start()

    @pl.when(fluid)
    def _():
        pltpu.make_async_remote_copy(
            picked, walls, contact_send.at[0], contact_recv.at[groups - 1], device_id=(groups - 1, brick), device_id_type=MESH
        ).wait_recv()

    @pl.when(solid)
    def _():
        for g in range(groups - 1):
            pltpu.make_async_remote_copy(
                picked, nears.at[g], contact_send.at[g], contact_recv.at[g], device_id=(g, brick), device_id_type=MESH
            ).wait_recv()
        walls[...] = nears[0] + nears[1] + nears[2] - picked[...]

    heat = factor[...] * walls[0:lines]
    extra = spread(jnp.where(solid, heat, heat * owned)).reshape(rows, width, depth)
    basis[0, 1 : rows + 1] = forcing[...] + extra
    for j in range(PARTS):
        send_halos(0, j)

    def gram_row(k):
        def body(r, accs):
            accs = list(accs)
            for j in range(width // 8):
                span = slice(8 * j, 8 * j + 8)
                mine = basis[k, r + 1, span, :]
                for i in range(k + 1):
                    other = mine if i == k else basis[i, r + 1, span, :]
                    accs[i] = accs[i] + mine * other
            return tuple(accs)

        accs = lax.fori_loop(0, rows, body, tuple(jnp.zeros((8, depth), F32) for _ in range(k + 1)))
        row, lane = iota((16, 128), 0), iota((16, 128), 1)
        tile = jnp.zeros((16, 128), F32) if k == 0 else gram_tile[...]
        for i in range(k + 1):
            spot = ((row == i) & (lane == k)) | ((row == k) & (lane == i))
            tile = jnp.where(spot, total(accs[i]), tile)
        gram_tile[...] = tile

    def local(r, v):
        return (
            diag[r] * v
            - uy[r] * pltpu.roll(v, width - 1, 0)
            - ly[r] * pltpu.roll(v, 1, 0)
            - uz[r] * pltpu.roll(v, depth - 1, 1)
            - lz[r] * pltpu.roll(v, 1, 1)
        )

    def apply(k, scale):
        at, to = (RAW.get(k, k), RAW[k + 1]) if scale is None else (k, k + 1)

        def keep(r, q):
            if scale is None:
                basis[to, r + 1] = q
            else:
                basis[to, r + 1] = scale * q - basis[k - 1, r + 1]

        @pl.when(fluid)
        def _():
            def middle(r, carry):
                v = basis[at, r + 1]
                keep(r, local(r, v) - gx[r] * basis[at, r] - ax[r + 1] * basis[at, r + 2])
                return carry

            keep(0, local(0, basis[at, 1]) - ax[1] * basis[at, 2])
            keep(rows - 1, local(rows - 1, basis[at, rows]) - gx[rows - 1] * basis[at, rows - 1])
            lax.fori_loop(1, rows - 1, middle, 0)

        @pl.when(solid)
        def _():
            for e in range(width // 8):
                u = (root[:, 8 * e : 8 * e + 8, :] * basis[at, 1 : rows + 1, 8 * e : 8 * e + 8, :]).reshape(64, depth)
                high, low = pieces(u)
                uh[e], ul[e] = high, low
                stiff[e] = dot(wxy[...], jnp.concatenate([high, low, high], axis=0), ((1,), (0,)))
            high, low = uh[...].reshape(cells, depth), ul[...].reshape(cells, depth)
            along = dot(high, wz[0], ((1,), (0,))) + dot(low, wz[0], ((1,), (0,))) + dot(high, wz[1], ((1,), (0,)))
            stiff[...] = stiff[...] + along.reshape(width // 8, 64, depth)

            def each(r, carry):
                force = stiff[:, pl.ds(r * 8, 8), :].reshape(width, depth)
                keep(r, local(r, basis[at, r + 1]) + root[r] * force)
                return carry

            lax.fori_loop(0, rows, each, 0)

    def finish(k, scale, mix=None):
        at, to = RAW.get(k, k), (RAW[k + 1] if scale is None else k + 1)
        for j in range(PARTS):
            span = slice(j * part_rows, (j + 1) * part_rows)

            @pl.when(has_down)
            def _():
                halo_up(k, j).wait_recv()

            @pl.when(has_up)
            def _():
                halo_down(k, j).wait_recv()

            for own, halo, coef in ((1, 0, gx.at[0]), (rows, rows + 1, ax.at[rows])):
                value = basis[at, halo, span]
                if mix is not None:
                    value = mix[0] * value + mix[1] * basis[RAW[1], halo, span] + mix[2] * basis[0, halo, span]
                value = coef[span] * value
                if scale is not None:
                    value = scale * value
                basis[to, own, span] = basis[to, own, span] - value
            if k + 1 < ITERS:
                send_halos(k + 1, j)

    apply(0, None)
    near_wait(0, 8)
    far_slots[0, high_id, 0:8] = merge_stats([near_slots[0, i, 0:8] for i in range(inner)])
    far_start(0, 8)
    finish(0, None)
    apply(1, None)
    gram_row(0)
    finish(1, None)
    far_wait(0, 8)
    split = (groups - 1) * outer

    def interval(tiles, count):
        stats = merge_stats(tiles)
        mean = stats[0:1, 2:3] * (1.0 / count)
        high = stats[0:1, 0:1] + 0.25 * mean
        low = jnp.maximum(-stats[0:1, 1:2] - 0.5 * mean, 0.0)
        return 0.5 * (high + low), 0.5 * (high - low)

    c_fluid, e_fluid = interval([far_slots[0, i, 0:8] for i in range(split)], float((groups - 1) * bricks * cells * depth))
    c_solid, e_solid = interval([far_slots[0, i, 0:8] for i in range(split, n_far)], float(bricks * cells * depth))
    center = jnp.where(solid, c_solid, c_fluid)
    inv_e = 1.0 / jnp.where(solid, e_solid, e_fluid)
    scale = 2.0 * inv_e

    mix = (scale * inv_e, -2.0 * scale * center * inv_e, scale * inv_e * center * center - 1.0)

    def convert(r, carry):
        zero, one, two = basis[0, r + 1], basis[RAW[1], r + 1], basis[RAW[2], r + 1]
        basis[1, r + 1] = (one - center * zero) * inv_e
        basis[2, r + 1] = mix[0] * two + mix[1] * one + mix[2] * zero
        diag[r] = diag[r] - center
        return carry

    lax.fori_loop(0, rows, convert, 0)
    for k in range(2, ITERS):
        apply(k, scale)
        if k == 2:
            gram_row(1)
        gram_row(k)
        finish(k, scale, mix if k == 2 else None)
    gram_row(ITERS)

    near_slots[1, low_id] = gram_tile[...]
    near_start(1, 16)
    near_wait(1, 16)
    summed = near_slots[1, 0]
    for i in range(1, inner):
        summed = summed + near_slots[1, i]
    far_slots[1, high_id] = summed
    far_start(1, 16)
    far_wait(1, 16)
    gram_fluid = far_slots[1, 0]
    for i in range(1, split):
        gram_fluid = gram_fluid + far_slots[1, i]
    gram_solid = far_slots[1, split]
    for i in range(split + 1, n_far):
        gram_solid = gram_solid + far_slots[1, i]
    y_fluid, ok_fluid = projected(gram_fluid, c_fluid / e_fluid, True)
    y_solid, ok_solid = projected(gram_solid, c_solid / e_solid, False)
    coeffs = jnp.where(solid, y_solid, y_fluid) * inv_e
    flag[0] = jnp.max(ok_fluid * ok_solid).astype(jnp.int32)
    weights = [coeffs[k : k + 1, :1] for k in range(ITERS)]

    def combine(r, carry):
        acc = weights[0] * basis[0, r + 1]
        for k in range(1, ITERS):
            acc = acc + weights[k] * basis[k, r + 1]
        out[r] = acc
        return carry

    lax.fori_loop(0, rows, combine, 0)
    store = pltpu.make_async_copy(out, out_hbm, store_sem)
    store.start()

    @pl.when(solid)
    def _():
        for g in range(groups - 1):
            wall_copy(g).wait_send()

    @pl.when(fluid)
    def _():
        near_copy.wait_send()

    @pl.when(fluid & has_up)
    def _():
        coef_a.wait_send()
        coef_g.wait_send()

    @pl.when(solid & has_up)
    def _():
        coef_up.wait_send()

    @pl.when(solid & has_down)
    def _():
        coef_down.wait_send()

    for k in range(ITERS):
        for j in range(PARTS):

            @pl.when(has_up)
            def _():
                halo_up(k, j).wait_send()

            @pl.when(has_down)
            def _():
                halo_down(k, j).wait_send()

    store.wait()


def handed_on(result):
    def body(source, target, sem):
        copy = pltpu.make_async_copy(source, target, sem)
        copy.start()
        copy.wait()

    return pl.pallas_call(
        body,
        out_shape=jax.ShapeDtypeStruct(result.shape, result.dtype),
        in_specs=[pl.BlockSpec(memory_space=pl.ANY)],
        out_specs=pl.BlockSpec(memory_space=pl.ANY),
        scratch_shapes=[pltpu.SemaphoreType.DMA],
        name="handed_on",
    )(result)


def shards(*arguments):
    groups, bricks = lax.axis_size("group"), lax.axis_size("brick")
    forcing = arguments[0]
    rows, width, depth = slab = forcing.shape
    lines = arguments[8].shape[0]
    points = lines * 128
    n_far = groups * (bricks // 8)
    vm = pltpu.VMEM
    scratch = (
        [vm(slab, F32)] * 3
        + [vm((3,) + slab, F32)] * 2
        + [vm(slab, F32)] * 2
        + [vm((3, 8, 8), F32)]
        + [vm((lines, 128), jnp.int32)] * 3
        + [vm((lines, 128), F32)]
        + [vm((ITERS + 3, rows + 2, width, depth), F32)]
        + [vm((rows + 1, width, depth), F32)] * 2
        + [vm(slab, F32)] * 5
        + [vm((width // 8, 64, depth), F32)]
        + [vm((width // 8, 64, depth), BF16)] * 2
        + [vm((2, depth, depth), BF16), vm((64, 192), BF16)]
        + [vm((width, depth), F32)] * 2
        + [vm((rows * width, points), BF16), vm((depth, points), BF16)]
        + [vm((8, 128), F32)] * 2
        + [vm((groups - 1, 8, 128), F32)]
        + [vm((16, 128), F32), vm((2, 8, 16, 128), F32), vm((2, n_far, 16, 128), F32)]
        + [vm(slab, F32)]
    )
    dma = pltpu.SemaphoreType.DMA
    semaphores = [
        dma((12,)),
        dma,
        dma((ITERS, 2, PARTS)),
        dma((ITERS, 2, PARTS)),
        dma((2,)),
        dma((2,)),
        dma((groups,)),
        dma((groups,)),
        dma((2, 8)),
        dma((2, 8)),
        dma((2, n_far)),
        dma((2, n_far)),
    ]
    result, flag = pl.pallas_call(
        functools.partial(kernel, groups, bricks),
        out_shape=(jax.ShapeDtypeStruct(slab, F32), jax.ShapeDtypeStruct((1,), jnp.int32)),
        in_specs=[pl.BlockSpec(memory_space=pl.ANY)] * 12,
        out_specs=(pl.BlockSpec(memory_space=pl.ANY), pl.BlockSpec(memory_space=pltpu.SMEM)),
        scratch_shapes=scratch + semaphores,
        compiler_params=pltpu.CompilerParams(collective_id=0, has_side_effects=True, vmem_limit_bytes=56 * 2**20),
        name="coupled",
    )(*arguments)
    return lax.cond(flag[0] > 0, lambda: handed_on(result), lambda: iterated(*arguments))


def solution(mesh):
    return jax.shard_map(
        shards,
        mesh=mesh,
        in_specs=(
            P(("group", "brick"), None, None),
            P(("group", "brick"), None, None),
            P(("group", "brick"), None, None),
            P(None, ("group", "brick"), None, None),
            P(None, ("group", "brick"), None, None),
            P(("group", "brick"), None, None),
            P(("group", "brick"), None, None),
            P(),
            P("brick", None),
            P("brick", None),
            P("brick", None),
            P("brick", None),
        ),
        out_specs=P(("group", "brick"), None, None),
        check_vma=False,
    )
```

```python
import functools

import jax
import jax.numpy as jnp
from jax import lax
from jax.experimental import pallas as pl
from jax.experimental.pallas import tpu as pltpu
from jax.sharding import PartitionSpec as P

ITERS = 8


HIGH = lax.Precision.HIGHEST


def passed_along(value, axis, steps):
    count = lax.axis_size(axis)
    leading, last = (max(0, -steps), min(count, count - steps))
    return lax.ppermute(value, axis, [(source, source + steps) for source in range(leading, last)])


def extended(cells, sides, width):
    for axis, dim in sides:
        count = lax.axis_size(axis)
        ends = count - 1
        head = lax.slice_in_dim(cells, 0, width, axis=dim)
        tail = lax.slice_in_dim(cells, cells.shape[dim] - width, cells.shape[dim], axis=dim)
        cells = jnp.concatenate(
            [
                lax.ppermute(tail, axis, [(i, (i + 1) % count) for i in range(ends)]),
                cells,
                lax.ppermute(head, axis, [((i + 1) % count, i) for i in range(ends)]),
            ],
            axis=dim,
        )
    return cells


def shift_next(v, axis):
    size = v.shape[axis]
    inner = lax.slice_in_dim(v, 1, size, axis=axis)
    zero = jnp.zeros_like(lax.slice_in_dim(v, 0, 1, axis=axis))
    return jnp.concatenate([inner, zero], axis=axis)


def shift_prev(v, axis):
    size = v.shape[axis]
    inner = lax.slice_in_dim(v, 0, size - 1, axis=axis)
    zero = jnp.zeros_like(lax.slice_in_dim(v, 0, 1, axis=axis))
    return jnp.concatenate([zero, inner], axis=axis)


def open_faces(shape, axis):
    index = lax.broadcasted_iota(jnp.int32, shape, axis)
    return (index < shape[axis] - 1).astype(jnp.float32)


def element_faces(shape, axis, nodes):
    index = lax.broadcasted_iota(jnp.int32, shape, axis)
    inside = (index % nodes == nodes - 1) & (index < shape[axis] - 1)
    return inside.astype(jnp.float32)


def stiffness_apply(u, rigidity_matrix):
    nodes = rigidity_matrix.shape[1]
    rows, width, depth = u.shape
    block = min(depth, 128)
    along_x = jnp.einsum("pq,qyz->pyz", rigidity_matrix[0], u, precision=HIGH)
    split_y = u.reshape(rows, width // nodes, nodes, depth)
    along_y = jnp.einsum("pq,xeqz->xepz", rigidity_matrix[1], split_y, precision=HIGH).reshape(
        rows, width, depth
    )
    wide = jnp.kron(jnp.eye(block // nodes, dtype=jnp.float32), rigidity_matrix[2])
    split_z = u.reshape(rows, width, depth // block, block)
    along_z = jnp.einsum("xyeq,pq->xyep", split_z, wide, precision=HIGH).reshape(rows, width, depth)
    return along_x + along_y + along_z


def least_squares(hess, beta):
    gram = jnp.dot(hess.T, hess, precision=HIGH)
    lower = jnp.linalg.cholesky(gram)
    right = (beta * hess[0])[:, None]
    middle = lax.linalg.triangular_solve(lower, right, left_side=True, lower=True)
    coeffs = lax.linalg.triangular_solve(
        lower, middle, left_side=True, lower=True, transpose_a=True
    )
    return coeffs[:, 0]


def iterated(
    forcing_vector,
    thermal_iterate,
    storage_over_step,
    opening_shares,
    flow_speed,
    diffusivity_root,
    sanction_weight,
    rigidity_matrix,
    contact_fluid_part,
    contact_fluid_volume,
    contact_solid_vertex,
    exchange_rate_factor,
):
    groups = lax.axis_size("group")
    bricks = lax.axis_size("brick")
    group_id = lax.axis_index("group")
    brick_id = lax.axis_index("brick")
    solid = group_id == groups - 1
    solid_flag = solid.astype(jnp.float32)
    fluid_flag = 1.0 - solid_flag
    rows, width, depth = forcing_vector.shape
    nodes = rigidity_matrix.shape[1]
    device = group_id * bricks + brick_id
    first_solid = (groups - 1) * bricks
    unrolled_array = thermal_iterate.reshape(-1)
    owned = (contact_fluid_part == group_id).astype(jnp.float32)
    target = jnp.where(solid, contact_solid_vertex, contact_fluid_volume).reshape(-1)
    picked = unrolled_array[target].reshape(contact_solid_vertex.shape)
    wall, near = lax.psum((picked * solid_flag, picked * owned * fluid_flag), "group")
    extra_rhs = jnp.where(
        solid, exchange_rate_factor * (near - wall), exchange_rate_factor * wall * owned
    )
    extra_diag = exchange_rate_factor * owned * fluid_flag
    rhs = (
        forcing_vector.reshape(-1)
        .at[target]
        .add(extra_rhs.reshape(-1))
        .reshape(forcing_vector.shape)
    )
    fluid_diag = (
        storage_over_step.reshape(-1)
        .at[target]
        .add(extra_diag.reshape(-1))
        .reshape(forcing_vector.shape)
    )
    shape = (rows, width, depth)
    global_row = device * rows + lax.broadcasted_iota(jnp.int32, shape, 0)
    face_x = opening_shares[0] * (global_row != first_solid * rows - 1).astype(jnp.float32)
    face_y = opening_shares[1] * open_faces(shape, 1)
    face_z = opening_shares[2] * open_faces(shape, 2)
    rims = passed_along(
        jnp.stack([face_x[-1], flow_speed[0][-1], sanction_weight[-1]]), ("group", "brick"), 1
    )
    face_low = rims[0]
    speed_low = rims[1]
    weight_low = rims[2]
    pair_low = 0.5 * (weight_low + sanction_weight[0]) * (device != first_solid).astype(jnp.float32)
    pair_up = passed_along(pair_low, "brick", -1)
    pair_y = (
        0.5 * (sanction_weight + shift_next(sanction_weight, 1)) * element_faces(shape, 1, nodes)
    )
    pair_z = (
        0.5 * (sanction_weight + shift_next(sanction_weight, 2)) * element_faces(shape, 2, nodes)
    )
    local_square = jnp.sum(rhs * rhs)
    solution = jnp.zeros_like(rhs)
    resid = rhs
    columns = []
    fluid_square, solid_square = lax.psum(
        (local_square * fluid_flag, local_square * solid_flag), ("group", "brick")
    )
    beta = jnp.sqrt(fluid_square)
    basis = [rhs / beta]
    direction = rhs
    norm_now = solid_square
    for step in range(ITERS):
        vector = jnp.where(solid, direction, basis[step])
        padded = extended(vector, ((("group", "brick"), 0),), 1)
        below = padded[0]
        above = padded[-1]

        def fluid_branch(unused):
            following = jnp.concatenate([vector[1:], above[None]], axis=0)
            flux_x = face_x * ((1.0 + flow_speed[0]) * vector - following)
            flux_low = face_low * ((1.0 + speed_low) * below - vector[0])
            out = (
                fluid_diag * vector
                + flux_x
                - jnp.concatenate([flux_low[None], flux_x[:-1]], axis=0)
            )
            flux_y = face_y * ((1.0 + flow_speed[1]) * vector - shift_next(vector, 1))
            flux_z = face_z * ((1.0 + flow_speed[2]) * vector - shift_next(vector, 2))
            return out + flux_y - shift_prev(flux_y, 1) + flux_z - shift_prev(flux_z, 2)

        def solid_branch(unused):
            out = storage_over_step * vector + diffusivity_root * stiffness_apply(
                diffusivity_root * vector, rigidity_matrix
            )
            jump_up = pair_up * (vector[-1] - above)
            jump_low = pair_low * (below - vector[0])
            out = out.at[0].add(-jump_low).at[rows - 1].add(jump_up)
            jump_y = pair_y * (vector - shift_next(vector, 1))
            jump_z = pair_z * (vector - shift_next(vector, 2))
            return out + jump_y - shift_prev(jump_y, 1) + jump_z - shift_prev(jump_z, 2)

        image = lax.cond(solid, solid_branch, fluid_branch, 0)
        inner = jnp.stack([jnp.sum(basis[j] * image) for j in range(step + 1)])
        heights, curvature = lax.psum(
            (inner * fluid_flag, jnp.sum(direction * image) * solid_flag), ("group", "brick")
        )
        fresh = image
        for j in range(step + 1):
            fresh = fresh - heights[j] * basis[j]
        alpha = norm_now / curvature
        solution = solution + alpha * direction
        resid = resid - alpha * image
        fresh_square, norm_next = lax.psum(
            (jnp.sum(fresh * fresh) * fluid_flag, jnp.sum(resid * resid) * solid_flag),
            ("group", "brick"),
        )
        length = jnp.sqrt(fresh_square)
        basis.append(fresh / length)
        columns.append(
            jnp.concatenate([heights, length[None], jnp.zeros((ITERS - 1 - step,), jnp.float32)])
        )
        direction = resid + norm_next / norm_now * direction
        norm_now = norm_next
    coeffs = least_squares(jnp.stack(columns, axis=1), beta)
    fluid_new = jnp.zeros_like(rhs)
    for step in range(ITERS):
        fluid_new = fluid_new + coeffs[step] * basis[step]
    return jnp.where(solid, solution, fluid_new)


F32 = jnp.float32
BF16 = jnp.bfloat16
MESH = pl.DeviceIdType.MESH
PIVOT_LEAST = 1e-3
REFINE_MOST = 3e-4
PARTS = 4
RAW = {1: ITERS + 1, 2: ITERS + 2}


def iota(shape, dim):
    return lax.broadcasted_iota(jnp.int32, shape, dim)


def pieces(x):
    high = x.astype(BF16)
    return high, (x - high.astype(F32)).astype(BF16)


def total(x):
    return jnp.sum(jnp.sum(x, axis=0, keepdims=True), axis=1, keepdims=True)


def greatest(x):
    return jnp.max(jnp.max(x, axis=0, keepdims=True), axis=1, keepdims=True)


def dot(a, b, dims):
    return lax.dot_general(a, b, ((dims[0], dims[1]), ((), ())), preferred_element_type=F32)


def shift_rows(x, gamma):
    size = x.shape[0]
    after = pltpu.roll(x, size - 1, 0)
    row = iota(x.shape, 0)
    out = gamma * x + 0.5 * (pltpu.roll(x, 1, 0) + after) + jnp.where(row == 0, 0.5 * after, 0.0)
    return jnp.where(row < ITERS, out, 0.0)


def shift_lanes(x, gamma):
    size = x.shape[1]
    after = pltpu.roll(x, size - 1, 1)
    lane = iota(x.shape, 1)
    out = gamma * x + 0.5 * (pltpu.roll(x, 1, 1) + after) + jnp.where(lane == 0, 0.5 * after, 0.0)
    return jnp.where(lane < ITERS, out, 0.0)


def projected(gram, gamma, fluid):
    shape = gram.shape
    row, lane = iota(shape, 0), iota(shape, 1)
    wide = shift_lanes(gram, gamma)
    if fluid:
        normal, right = shift_rows(wide, gamma), shift_rows(gram, gamma)
    else:
        normal, right = jnp.where(row < ITERS, wide, 0.0), jnp.where(row < ITERS, gram, 0.0)
    table = jnp.where(lane < ITERS, normal, 0.0)
    table = jnp.where((lane == row + 8) & (row < ITERS), 1.0, table)
    table = jnp.where(lane == 16, pltpu.roll(right, 16, 1), table)
    margin = None
    for k in range(ITERS):
        pivot = table[k : k + 1, k : k + 1]
        spare = pivot - PIVOT_LEAST * normal[k : k + 1, k : k + 1]
        margin = spare if margin is None else jnp.minimum(margin, spare)
        scaled = table[k : k + 1, :] * (1.0 / pivot)
        column = jnp.where(row[:, :1] == k, 0.0, table[:, k : k + 1])
        table = jnp.where(row == k, scaled, table - column * scaled)
    coeffs = jnp.broadcast_to(table[:, 16:17], shape)
    inverse = jnp.where(lane < ITERS, pltpu.roll(table, shape[1] - 8, 1), 0.0)
    applied = gamma * coeffs + 0.5 * (pltpu.roll(coeffs, 1, 0) + pltpu.roll(coeffs, shape[0] - 1, 0))
    applied = applied + jnp.where(row == 1, 0.5 * pltpu.roll(coeffs, 1, 0), 0.0)
    rest = jnp.where(row == 0, 1.0, 0.0) - applied
    image = jnp.broadcast_to(jnp.sum(gram * rest, axis=0, keepdims=True), shape)
    image = shift_lanes(image, gamma) if fluid else jnp.where(lane < ITERS, image, 0.0)
    change = jnp.sum(inverse * image, axis=1, keepdims=True)
    coeffs = coeffs[:, :1] + change
    size = jnp.sum(jnp.abs(coeffs), axis=0, keepdims=True)
    moved = jnp.sum(jnp.abs(change), axis=0, keepdims=True)
    good = (margin > 0.0) & (moved < REFINE_MOST * size)
    return coeffs, jnp.where(good, 1.0, 0.0)


def ring_far(step, size):
    return min(step, size - step)


def kernel(
    groups,
    bricks,
    forcing_hbm,
    thermal_hbm,
    storage_hbm,
    opening_hbm,
    flow_hbm,
    root_hbm,
    weight_hbm,
    rigidity_hbm,
    part_hbm,
    volume_hbm,
    vertex_hbm,
    factor_hbm,
    out_hbm,
    flag,
    thermal,
    forcing,
    storage,
    opening,
    flow,
    root,
    weight,
    rigidity,
    part,
    volume,
    vertex,
    factor,
    basis,
    ax,
    gx,
    diag,
    uy,
    ly,
    uz,
    lz,
    stiff,
    uh,
    ul,
    wz,
    wxy,
    weight_low,
    weight_up,
    row_hot,
    col_hot,
    picked,
    walls,
    nears,
    gram_tile,
    near_slots,
    far_slots,
    out,
    load_sem,
    store_sem,
    halo_send,
    halo_recv,
    coef_send,
    coef_recv,
    contact_send,
    contact_recv,
    near_send,
    near_recv,
    far_send,
    far_recv,
):
    group = lax.axis_index("group")
    brick = lax.axis_index("brick")
    rows, width, depth = forcing.shape
    plane = (width, depth)
    cells = rows * width
    solid = group == groups - 1
    fluid = group != groups - 1
    inner, outer = 8, bricks // 8
    low_id = lax.rem(brick, inner)
    high_id = group * outer + brick // inner
    n_far = groups * outer
    at_top = (brick == bricks - 1) & (group >= groups - 2)
    at_bottom = (brick == 0) & ((group == 0) | (group == groups - 1))
    has_up, has_down = jnp.logical_not(at_top), jnp.logical_not(at_bottom)
    device = group * bricks + brick
    up_id = lax.rem(device + 1, groups * bricks)
    down_id = lax.rem(device + groups * bricks - 1, groups * bricks)
    up = (up_id // bricks, lax.rem(up_id, bricks))
    down = (down_id // bricks, lax.rem(down_id, bricks))

    names = [
        (vertex_hbm, vertex),
        (volume_hbm, volume),
        (thermal_hbm, thermal),
        (part_hbm, part),
        (factor_hbm, factor),
        (opening_hbm, opening),
        (flow_hbm, flow),
        (storage_hbm, storage),
        (weight_hbm, weight),
        (root_hbm, root),
        (rigidity_hbm, rigidity),
        (forcing_hbm, forcing),
    ]
    loads = [pltpu.make_async_copy(s, d, load_sem.at[i]) for i, (s, d) in enumerate(names)]
    for load in loads:
        load.start()
    (l_vertex, l_volume, l_thermal, l_part, l_factor, l_opening, l_flow, l_storage, l_weight, l_root, l_rigid, l_forcing) = loads

    plane_id = brick // inner
    near_peers, far_peers = [], []
    for dz, dc in sorted(((a, b) for a in range(inner // 2) for b in range(2)), key=lambda at: -ring_far(at[0], inner // 2)):
        if dz or dc:
            peer = lax.rem(low_id // 2 + dz, inner // 2) * 2 + lax.rem(low_id + dc, 2)
            near_peers.append((peer, (group, plane_id * inner + peer)))
    steps = sorted(
        ((a, b) for a in range(groups) for b in range(outer)), key=lambda at: -ring_far(at[0], groups) - ring_far(at[1], outer)
    )
    for dx, dy in steps:
        if dx or dy:
            x_id, y_id = lax.rem(group + dx, groups), lax.rem(plane_id + dy, outer)
            far_peers.append((x_id * outer + y_id, (x_id, y_id * inner + low_id)))

    barrier = pltpu.get_barrier_semaphore()
    for peer, where in far_peers + near_peers:
        pl.semaphore_signal(barrier, inc=1, device_id=where, device_id_type=MESH)

    @pl.when(has_up)
    def _():
        pl.semaphore_signal(barrier, inc=1, device_id=up, device_id_type=MESH)

    @pl.when(has_down)
    def _():
        pl.semaphore_signal(barrier, inc=1, device_id=down, device_id_type=MESH)

    @pl.when(at_bottom)
    def _():
        for k in range(ITERS):
            basis[RAW.get(k, k), 0] = jnp.zeros(plane, F32)

    @pl.when(at_top)
    def _():
        for k in range(ITERS):
            basis[RAW.get(k, k), rows + 1] = jnp.zeros(plane, F32)

    l_vertex.wait()
    l_volume.wait()
    target = jnp.where(solid, vertex[...], volume[...])
    cell_row, cell_col = target >> 8, target & 255
    lines = target.shape[0]
    points = lines * 128
    for j in range(lines):
        span = pl.ds(j * 128, 128)
        row_hot[:, span] = jnp.where(iota((cells, 128), 0) == cell_row[j : j + 1], 1.0, 0.0).astype(BF16)
        col_hot[:, span] = jnp.where(iota((depth, 128), 0) == cell_col[j : j + 1], 1.0, 0.0).astype(BF16)
    l_thermal.wait()
    high, low = pieces(thermal[...].reshape(cells, depth))
    hot = row_hot[...]
    found = dot(high, hot, ((0,), (0,))) + dot(low, hot, ((0,), (0,)))
    value = jnp.sum(found * col_hot[...].astype(F32), axis=0, keepdims=True)
    value = jnp.concatenate([value[:, j * 128 : (j + 1) * 128] for j in range(lines)], axis=0)
    l_part.wait()
    l_factor.wait()
    owned = jnp.where(part[...] == group, 1.0, 0.0)
    picked[0:lines] = jnp.where(solid, value, value * owned)
    picked[lines:] = jnp.zeros((8 - lines, 128), F32)

    pl.semaphore_wait(barrier, inner - 1 + n_far - 1 + has_up.astype(jnp.int32) + has_down.astype(jnp.int32))

    def wall_copy(g):
        return pltpu.make_async_remote_copy(
            picked, walls, contact_send.at[g], contact_recv.at[groups - 1], device_id=(g, brick), device_id_type=MESH
        )

    near_copy = pltpu.make_async_remote_copy(
        picked, nears.at[group], contact_send.at[0], contact_recv.at[group], device_id=(groups - 1, brick), device_id_type=MESH
    )

    @pl.when(solid)
    def _():
        for g in range(groups - 1):
            wall_copy(g).start()

    @pl.when(fluid)
    def _():
        near_copy.start()

    l_opening.wait()
    l_flow.wait()
    l_weight.wait()
    coef_a = pltpu.make_async_remote_copy(
        ax.at[rows], ax.at[0], coef_send.at[0], coef_recv.at[0], device_id=up, device_id_type=MESH
    )
    coef_g = pltpu.make_async_remote_copy(
        gx.at[rows], gx.at[0], coef_send.at[1], coef_recv.at[1], device_id=up, device_id_type=MESH
    )
    coef_up = pltpu.make_async_remote_copy(
        weight.at[rows - 1], weight_low, coef_send.at[0], coef_recv.at[0], device_id=up, device_id_type=MESH
    )
    coef_down = pltpu.make_async_remote_copy(
        weight.at[0], weight_up, coef_send.at[1], coef_recv.at[1], device_id=down, device_id_type=MESH
    )

    @pl.when(fluid)
    def _():
        last = jnp.where(at_top, 0.0, opening[0, rows - 1])
        ax[rows] = last
        gx[rows] = last * (1.0 + flow[0, rows - 1])

    @pl.when(fluid & has_up)
    def _():
        coef_a.start()
        coef_g.start()

    @pl.when(solid & has_up)
    def _():
        coef_up.start()

    @pl.when(solid & has_down)
    def _():
        coef_down.start()

    l_storage.wait()
    l_root.wait()
    l_rigid.wait()

    def spread(values):
        flat = jnp.concatenate([values[j : j + 1] for j in range(lines)], axis=1)
        high, low = pieces(flat)
        cols = col_hot[...].astype(F32)
        return dot(row_hot[...], (cols * high.astype(F32)).astype(BF16), ((1,), (1,))) + dot(
            row_hot[...], (cols * low.astype(F32)).astype(BF16), ((1,), (1,))
        )

    def fold(x, op):
        y = x.reshape(width // 8, 8, depth)
        return op(y, axis=0)

    y_at, z_at = iota(plane, 0), iota(plane, 1)

    def write_stats(d_max, d_min, o_sum):
        lane = iota((8, 128), 1)
        tile = jnp.where(lane == 0, greatest(d_max), jnp.where(lane == 1, greatest(-d_min), jnp.where(lane == 2, total(o_sum), 0.0)))
        near_slots[0, low_id, 0:8] = tile

    start = (jnp.full((8, depth), -1e30, F32), jnp.full((8, depth), 1e30, F32), jnp.zeros((8, depth), F32))

    @pl.when(fluid)
    def _():
        extra = spread(factor[...] * owned).reshape(rows, width, depth)
        storage[...] = storage[...] + extra

        def second(r, carry):
            d_max, d_min, o_sum = carry
            a_y = jnp.where(y_at == width - 1, 0.0, opening[1, r])
            g_y = a_y * (1.0 + flow[1, r])
            g_low = pltpu.roll(g_y, 1, 0)
            uy[r] = a_y
            ly[r] = g_low
            a_x = jnp.where(at_top & (r == rows - 1), 0.0, opening[0, r])
            g_x = a_x * (1.0 + flow[0, r])

            @pl.when(r < rows - 1)
            def _():
                ax[r + 1] = a_x
                gx[r + 1] = g_x

            d = storage[r] + g_x + g_y + pltpu.roll(a_y, 1, 0)
            o = a_x + g_x + a_y + g_low
            a_z = jnp.where(z_at == depth - 1, 0.0, opening[2, r])
            g_z = a_z * (1.0 + flow[2, r])
            g_low = pltpu.roll(g_z, 1, 1)
            uz[r] = a_z
            lz[r] = g_low
            d = d + g_z + pltpu.roll(a_z, 1, 1)
            o = o + a_z + g_low
            d = d + jnp.where(r == 0, 0.0, opening[0, jnp.maximum(r - 1, 0)])
            diag[r] = d
            return jnp.maximum(d_max, fold(d, jnp.max)), jnp.minimum(d_min, fold(d, jnp.min)), o_sum + fold(o, jnp.sum)

        write_stats(*lax.fori_loop(0, rows, second, start))

    @pl.when(solid)
    def _():
        eye = iota((8, 8), 0) == iota((8, 8), 1)
        both = rigidity[0] + rigidity[1] + rigidity[2]
        size = jnp.abs(rigidity[0]) + jnp.abs(rigidity[1]) + jnp.abs(rigidity[2])
        trace = total(jnp.where(eye, both, 0.0)) * (1.0 / 8)
        off = total(jnp.where(eye, 0.0, size)) * (1.0 / 8)
        block_z = jnp.where(iota((8, depth), 1) % 8 == iota((8, depth), 0), 1.0, 0.0)
        spread_z = lax.dot_general(
            lax.dot_general(block_z, rigidity[2], (((0,), (1,)), ((), ())), precision=HIGH, preferred_element_type=F32),
            block_z,
            (((1,), (0,)), ((), ())),
            precision=HIGH,
            preferred_element_type=F32,
        )
        same = (iota((depth, depth), 0) // 8) == (iota((depth, depth), 1) // 8)
        high, low = pieces(jnp.where(same, spread_z, 0.0))
        wz[0], wz[1] = high, low
        outer_x = jnp.where(iota((8, 64), 1) // 8 == iota((8, 64), 0), 1.0, 0.0)
        inner_y = jnp.where(iota((8, 64), 1) % 8 == iota((8, 64), 0), 1.0, 0.0)

        def expand(matrix, hot):
            left = lax.dot_general(hot, matrix, (((0,), (0,)), ((), ())), precision=HIGH, preferred_element_type=F32)
            return lax.dot_general(left, hot, (((1,), (0,)), ((), ())), precision=HIGH, preferred_element_type=F32)

        same_y = iota((64, 64), 0) % 8 == iota((64, 64), 1) % 8
        same_x = iota((64, 64), 0) // 8 == iota((64, 64), 1) // 8
        mixed = jnp.where(same_y, expand(rigidity[0], outer_x), 0.0) + jnp.where(same_x, expand(rigidity[1], inner_y), 0.0)
        high, low = pieces(mixed)
        wxy[...] = jnp.concatenate([high, high, low], axis=1)

        def second(r, carry):
            d_max, d_min, o_sum = carry
            w = weight[r]
            b_y = jnp.where((y_at % 8 == 7) & (y_at < width - 1), 0.5 * (w + pltpu.roll(w, width - 1, 0)), 0.0)
            b_low = pltpu.roll(b_y, 1, 0)
            uy[r] = b_y
            ly[r] = b_low
            pair = b_y + b_low
            b_z = jnp.where((z_at % 8 == 7) & (z_at < depth - 1), 0.5 * (w + pltpu.roll(w, depth - 1, 1)), 0.0)
            b_low = pltpu.roll(b_z, 1, 1)
            uz[r] = b_z
            lz[r] = b_low
            pair = pair + b_z + b_low
            d = storage[r] + pair
            diag[r] = d
            square = root[r] * root[r]
            whole = d + square * trace
            o = pair + square * off
            return jnp.maximum(d_max, fold(whole, jnp.max)), jnp.minimum(d_min, fold(whole, jnp.min)), o_sum + fold(o, jnp.sum)

        write_stats(*lax.fori_loop(0, rows, second, start))

    def near_start(which, height):
        for o, (peer, where) in enumerate(near_peers):
            pltpu.make_async_remote_copy(
                near_slots.at[which, low_id, pl.ds(0, height)],
                near_slots.at[which, low_id, pl.ds(0, height)],
                near_send.at[which, o],
                near_recv.at[which, low_id],
                device_id=where,
                device_id_type=MESH,
            ).start()

    def near_wait(which, height):
        for o, (peer, where) in enumerate(near_peers):
            copy = pltpu.make_async_remote_copy(
                near_slots.at[which, peer, pl.ds(0, height)],
                near_slots.at[which, peer, pl.ds(0, height)],
                near_send.at[which, o],
                near_recv.at[which, peer],
                device_id=where,
                device_id_type=MESH,
            )
            copy.wait_recv()
            copy.wait_send()

    def far_start(which, height):
        for o, (peer, where) in enumerate(far_peers):
            pltpu.make_async_remote_copy(
                far_slots.at[which, high_id, pl.ds(0, height)],
                far_slots.at[which, high_id, pl.ds(0, height)],
                far_send.at[which, o],
                far_recv.at[which, high_id],
                device_id=where,
                device_id_type=MESH,
            ).start()

    def far_wait(which, height):
        for o, (peer, where) in enumerate(far_peers):
            copy = pltpu.make_async_remote_copy(
                far_slots.at[which, peer, pl.ds(0, height)],
                far_slots.at[which, peer, pl.ds(0, height)],
                far_send.at[which, o],
                far_recv.at[which, peer],
                device_id=where,
                device_id_type=MESH,
            )
            copy.wait_recv()
            copy.wait_send()

    def merge_stats(tiles):
        lane = iota((8, 128), 1)
        most, summed = tiles[0], tiles[0]
        for tile in tiles[1:]:
            most, summed = jnp.maximum(most, tile), summed + tile
        return jnp.where(lane == 2, summed, most)

    near_start(0, 8)

    l_forcing.wait()

    part_rows = width // PARTS

    def halo_up(k, j):
        span = pl.ds(j * part_rows, part_rows)
        at = RAW.get(k, k)
        return pltpu.make_async_remote_copy(
            basis.at[at, rows, span],
            basis.at[at, 0, span],
            halo_send.at[k, 0, j],
            halo_recv.at[k, 0, j],
            device_id=up,
            device_id_type=MESH,
        )

    def halo_down(k, j):
        span = pl.ds(j * part_rows, part_rows)
        at = RAW.get(k, k)
        return pltpu.make_async_remote_copy(
            basis.at[at, 1, span],
            basis.at[at, rows + 1, span],
            halo_send.at[k, 1, j],
            halo_recv.at[k, 1, j],
            device_id=down,
            device_id_type=MESH,
        )

    def send_halos(k, j):
        @pl.when(has_up)
        def _():
            halo_up(k, j).start()

        @pl.when(has_down)
        def _():
            halo_down(k, j).start()

    @pl.when(fluid)
    def _():
        pltpu.make_async_remote_copy(
            picked, walls, contact_send.at[0], contact_recv.at[groups - 1], device_id=(groups - 1, brick), device_id_type=MESH
        ).wait_recv()

    @pl.when(solid)
    def _():
        for g in range(groups - 1):
            pltpu.make_async_remote_copy(
                picked, nears.at[g], contact_send.at[g], contact_recv.at[g], device_id=(g, brick), device_id_type=MESH
            ).wait_recv()
        walls[...] = nears[0] + nears[1] + nears[2] - picked[...]

    heat = factor[...] * walls[0:lines]
    extra = spread(jnp.where(solid, heat, heat * owned)).reshape(rows, width, depth)
    basis[0, 1 : rows + 1] = forcing[...] + extra
    for j in range(PARTS):
        send_halos(0, j)

    @pl.when(at_bottom)
    def _():
        gx[0] = jnp.zeros(plane, F32)

    @pl.when(fluid & has_down)
    def _():
        coef_a.wait_recv()
        coef_g.wait_recv()
        diag[0] = diag[0] + ax[0]

    @pl.when(solid & has_down)
    def _():
        coef_up.wait_recv()
        gx[0] = 0.5 * (weight_low[...] + weight[0])
        diag[0] = diag[0] + gx[0]

    @pl.when(solid & has_up)
    def _():
        coef_down.wait_recv()
        ax[rows] = 0.5 * (weight[rows - 1] + weight_up[...])
        diag[rows - 1] = diag[rows - 1] + ax[rows]

    @pl.when(solid & at_top)
    def _():
        ax[rows] = jnp.zeros(plane, F32)

    def gram_row(k):
        def body(r, accs):
            accs = list(accs)
            for j in range(width // 8):
                span = slice(8 * j, 8 * j + 8)
                mine = basis[k, r + 1, span, :]
                for i in range(k + 1):
                    other = mine if i == k else basis[i, r + 1, span, :]
                    accs[i] = accs[i] + mine * other
            return tuple(accs)

        accs = lax.fori_loop(0, rows, body, tuple(jnp.zeros((8, depth), F32) for _ in range(k + 1)))
        row, lane = iota((16, 128), 0), iota((16, 128), 1)
        tile = jnp.zeros((16, 128), F32) if k == 0 else gram_tile[...]
        for i in range(k + 1):
            spot = ((row == i) & (lane == k)) | ((row == k) & (lane == i))
            tile = jnp.where(spot, total(accs[i]), tile)
        gram_tile[...] = tile

    def local(r, v):
        return (
            diag[r] * v
            - uy[r] * pltpu.roll(v, width - 1, 0)
            - ly[r] * pltpu.roll(v, 1, 0)
            - uz[r] * pltpu.roll(v, depth - 1, 1)
            - lz[r] * pltpu.roll(v, 1, 1)
        )

    def apply(k, scale):
        at, to = (RAW.get(k, k), RAW[k + 1]) if scale is None else (k, k + 1)

        def keep(r, q):
            if scale is None:
                basis[to, r + 1] = q
            else:
                basis[to, r + 1] = scale * q - basis[k - 1, r + 1]

        @pl.when(fluid)
        def _():
            def middle(r, carry):
                v = basis[at, r + 1]
                keep(r, local(r, v) - gx[r] * basis[at, r] - ax[r + 1] * basis[at, r + 2])
                return carry

            keep(0, local(0, basis[at, 1]) - ax[1] * basis[at, 2])
            keep(rows - 1, local(rows - 1, basis[at, rows]) - gx[rows - 1] * basis[at, rows - 1])
            lax.fori_loop(1, rows - 1, middle, 0)

        @pl.when(solid)
        def _():
            for e in range(width // 8):
                u = (root[:, 8 * e : 8 * e + 8, :] * basis[at, 1 : rows + 1, 8 * e : 8 * e + 8, :]).reshape(64, depth)
                high, low = pieces(u)
                uh[e], ul[e] = high, low
                stiff[e] = dot(wxy[...], jnp.concatenate([high, low, high], axis=0), ((1,), (0,)))
            high, low = uh[...].reshape(cells, depth), ul[...].reshape(cells, depth)
            along = dot(high, wz[0], ((1,), (0,))) + dot(low, wz[0], ((1,), (0,))) + dot(high, wz[1], ((1,), (0,)))
            stiff[...] = stiff[...] + along.reshape(width // 8, 64, depth)

            def each(r, carry):
                force = stiff[:, pl.ds(r * 8, 8), :].reshape(width, depth)
                keep(r, local(r, basis[at, r + 1]) + root[r] * force)
                return carry

            lax.fori_loop(0, rows, each, 0)

    def finish(k, scale, mix=None):
        at, to = RAW.get(k, k), (RAW[k + 1] if scale is None else k + 1)
        for j in range(PARTS):
            span = slice(j * part_rows, (j + 1) * part_rows)

            @pl.when(has_down)
            def _():
                halo_up(k, j).wait_recv()

            @pl.when(has_up)
            def _():
                halo_down(k, j).wait_recv()

            for own, halo, coef in ((1, 0, gx.at[0]), (rows, rows + 1, ax.at[rows])):
                value = basis[at, halo, span]
                if mix is not None:
                    value = mix[0] * value + mix[1] * basis[RAW[1], halo, span] + mix[2] * basis[0, halo, span]
                value = coef[span] * value
                if scale is not None:
                    value = scale * value
                basis[to, own, span] = basis[to, own, span] - value
            if k + 1 < ITERS:
                send_halos(k + 1, j)

    apply(0, None)
    near_wait(0, 8)
    far_slots[0, high_id, 0:8] = merge_stats([near_slots[0, i, 0:8] for i in range(inner)])
    far_start(0, 8)
    finish(0, None)
    apply(1, None)
    gram_row(0)
    finish(1, None)
    far_wait(0, 8)
    split = (groups - 1) * outer

    def interval(tiles, count):
        stats = merge_stats(tiles)
        mean = stats[0:1, 2:3] * (1.0 / count)
        high = stats[0:1, 0:1] + 0.25 * mean
        low = jnp.maximum(-stats[0:1, 1:2] - 0.5 * mean, 0.0)
        return 0.5 * (high + low), 0.5 * (high - low)

    c_fluid, e_fluid = interval([far_slots[0, i, 0:8] for i in range(split)], float((groups - 1) * bricks * cells * depth))
    c_solid, e_solid = interval([far_slots[0, i, 0:8] for i in range(split, n_far)], float(bricks * cells * depth))
    center = jnp.where(solid, c_solid, c_fluid)
    inv_e = 1.0 / jnp.where(solid, e_solid, e_fluid)
    scale = 2.0 * inv_e

    mix = (scale * inv_e, -2.0 * scale * center * inv_e, scale * inv_e * center * center - 1.0)

    def convert(r, carry):
        zero, one, two = basis[0, r + 1], basis[RAW[1], r + 1], basis[RAW[2], r + 1]
        basis[1, r + 1] = (one - center * zero) * inv_e
        basis[2, r + 1] = mix[0] * two + mix[1] * one + mix[2] * zero
        diag[r] = diag[r] - center
        return carry

    lax.fori_loop(0, rows, convert, 0)
    for k in range(2, ITERS):
        apply(k, scale)
        if k == 2:
            gram_row(1)
        gram_row(k)
        finish(k, scale, mix if k == 2 else None)
    gram_row(ITERS)

    near_slots[1, low_id] = gram_tile[...]
    near_start(1, 16)
    near_wait(1, 16)
    summed = near_slots[1, 0]
    for i in range(1, inner):
        summed = summed + near_slots[1, i]
    far_slots[1, high_id] = summed
    far_start(1, 16)
    far_wait(1, 16)
    gram_fluid = far_slots[1, 0]
    for i in range(1, split):
        gram_fluid = gram_fluid + far_slots[1, i]
    gram_solid = far_slots[1, split]
    for i in range(split + 1, n_far):
        gram_solid = gram_solid + far_slots[1, i]
    y_fluid, ok_fluid = projected(gram_fluid, c_fluid / e_fluid, True)
    y_solid, ok_solid = projected(gram_solid, c_solid / e_solid, False)
    coeffs = jnp.where(solid, y_solid, y_fluid) * inv_e
    flag[0] = jnp.max(ok_fluid * ok_solid).astype(jnp.int32)
    weights = [coeffs[k : k + 1, :1] for k in range(ITERS)]

    def combine(r, carry):
        acc = weights[0] * basis[0, r + 1]
        for k in range(1, ITERS):
            acc = acc + weights[k] * basis[k, r + 1]
        out[r] = acc
        pltpu.make_async_copy(out.at[r], out_hbm.at[r], store_sem.at[r]).start()
        return carry

    lax.fori_loop(0, rows, combine, 0)

    @pl.when(solid)
    def _():
        for g in range(groups - 1):
            wall_copy(g).wait_send()

    @pl.when(fluid)
    def _():
        near_copy.wait_send()

    @pl.when(fluid & has_up)
    def _():
        coef_a.wait_send()
        coef_g.wait_send()

    @pl.when(solid & has_up)
    def _():
        coef_up.wait_send()

    @pl.when(solid & has_down)
    def _():
        coef_down.wait_send()

    for k in range(ITERS):
        for j in range(PARTS):

            @pl.when(has_up)
            def _():
                halo_up(k, j).wait_send()

            @pl.when(has_down)
            def _():
                halo_down(k, j).wait_send()

    for r in range(rows):
        pltpu.make_async_copy(out.at[r], out_hbm.at[r], store_sem.at[r]).wait()


def handed_on(result):
    rows = result.shape[0]

    def body(source, target, held, in_sem, out_sem):
        ins = [pltpu.make_async_copy(source.at[i], held.at[i], in_sem.at[i]) for i in range(rows)]
        outs = [pltpu.make_async_copy(held.at[i], target.at[i], out_sem.at[i]) for i in range(rows)]
        for copy in ins:
            copy.start()
        for arrived, copy in zip(ins, outs):
            arrived.wait()
            copy.start()
        for copy in outs:
            copy.wait()

    return pl.pallas_call(
        body,
        out_shape=jax.ShapeDtypeStruct(result.shape, result.dtype),
        in_specs=[pl.BlockSpec(memory_space=pl.ANY)],
        out_specs=pl.BlockSpec(memory_space=pl.ANY),
        scratch_shapes=[pltpu.VMEM(result.shape, F32), pltpu.SemaphoreType.DMA((rows,)), pltpu.SemaphoreType.DMA((rows,))],
        name="handed_on",
    )(result)


def shards(*arguments):
    groups, bricks = lax.axis_size("group"), lax.axis_size("brick")
    forcing = arguments[0]
    rows, width, depth = slab = forcing.shape
    lines = arguments[8].shape[0]
    points = lines * 128
    n_far = groups * (bricks // 8)
    vm = pltpu.VMEM
    scratch = (
        [vm(slab, F32)] * 3
        + [vm((3,) + slab, F32)] * 2
        + [vm(slab, F32)] * 2
        + [vm((3, 8, 8), F32)]
        + [vm((lines, 128), jnp.int32)] * 3
        + [vm((lines, 128), F32)]
        + [vm((ITERS + 3, rows + 2, width, depth), F32)]
        + [vm((rows + 1, width, depth), F32)] * 2
        + [vm(slab, F32)] * 5
        + [vm((width // 8, 64, depth), F32)]
        + [vm((width // 8, 64, depth), BF16)] * 2
        + [vm((2, depth, depth), BF16), vm((64, 192), BF16)]
        + [vm((width, depth), F32)] * 2
        + [vm((rows * width, points), BF16), vm((depth, points), BF16)]
        + [vm((8, 128), F32)] * 2
        + [vm((groups - 1, 8, 128), F32)]
        + [vm((16, 128), F32), vm((2, 8, 16, 128), F32), vm((2, n_far, 16, 128), F32)]
        + [vm(slab, F32)]
    )
    dma = pltpu.SemaphoreType.DMA
    semaphores = [
        dma((12,)),
        dma((rows,)),
        dma((ITERS, 2, PARTS)),
        dma((ITERS, 2, PARTS)),
        dma((2,)),
        dma((2,)),
        dma((groups,)),
        dma((groups,)),
        dma((2, 8)),
        dma((2, 8)),
        dma((2, n_far)),
        dma((2, n_far)),
    ]
    result, flag = pl.pallas_call(
        functools.partial(kernel, groups, bricks),
        out_shape=(jax.ShapeDtypeStruct(slab, F32), jax.ShapeDtypeStruct((1,), jnp.int32)),
        in_specs=[pl.BlockSpec(memory_space=pl.ANY)] * 12,
        out_specs=(pl.BlockSpec(memory_space=pl.ANY), pl.BlockSpec(memory_space=pltpu.SMEM)),
        scratch_shapes=scratch + semaphores,
        compiler_params=pltpu.CompilerParams(collective_id=0, has_side_effects=True, vmem_limit_bytes=56 * 2**20),
        name="coupled",
    )(*arguments)
    return lax.cond(flag[0] > 0, lambda: handed_on(result), lambda: iterated(*arguments))


def solution(mesh):
    return jax.shard_map(
        shards,
        mesh=mesh,
        in_specs=(
            P(("group", "brick"), None, None),
            P(("group", "brick"), None, None),
            P(("group", "brick"), None, None),
            P(None, ("group", "brick"), None, None),
            P(None, ("group", "brick"), None, None),
            P(("group", "brick"), None, None),
            P(("group", "brick"), None, None),
            P(),
            P("brick", None),
            P("brick", None),
            P("brick", None),
            P("brick", None),
        ),
        out_specs=P(("group", "brick"), None, None),
        check_vma=False,
    )
```

```python
import functools

import jax
import jax.numpy as jnp
from jax import lax
from jax.experimental import pallas as pl
from jax.experimental.pallas import tpu as pltpu
from jax.sharding import PartitionSpec as P

ITERS = 8


HIGH = lax.Precision.HIGHEST


def passed_along(value, axis, steps):
    count = lax.axis_size(axis)
    leading, last = (max(0, -steps), min(count, count - steps))
    return lax.ppermute(value, axis, [(source, source + steps) for source in range(leading, last)])


def extended(cells, sides, width):
    for axis, dim in sides:
        count = lax.axis_size(axis)
        ends = count - 1
        head = lax.slice_in_dim(cells, 0, width, axis=dim)
        tail = lax.slice_in_dim(cells, cells.shape[dim] - width, cells.shape[dim], axis=dim)
        cells = jnp.concatenate(
            [
                lax.ppermute(tail, axis, [(i, (i + 1) % count) for i in range(ends)]),
                cells,
                lax.ppermute(head, axis, [((i + 1) % count, i) for i in range(ends)]),
            ],
            axis=dim,
        )
    return cells


def shift_next(v, axis):
    size = v.shape[axis]
    inner = lax.slice_in_dim(v, 1, size, axis=axis)
    zero = jnp.zeros_like(lax.slice_in_dim(v, 0, 1, axis=axis))
    return jnp.concatenate([inner, zero], axis=axis)


def shift_prev(v, axis):
    size = v.shape[axis]
    inner = lax.slice_in_dim(v, 0, size - 1, axis=axis)
    zero = jnp.zeros_like(lax.slice_in_dim(v, 0, 1, axis=axis))
    return jnp.concatenate([zero, inner], axis=axis)


def open_faces(shape, axis):
    index = lax.broadcasted_iota(jnp.int32, shape, axis)
    return (index < shape[axis] - 1).astype(jnp.float32)


def element_faces(shape, axis, nodes):
    index = lax.broadcasted_iota(jnp.int32, shape, axis)
    inside = (index % nodes == nodes - 1) & (index < shape[axis] - 1)
    return inside.astype(jnp.float32)


def stiffness_apply(u, rigidity_matrix):
    nodes = rigidity_matrix.shape[1]
    rows, width, depth = u.shape
    block = min(depth, 128)
    along_x = jnp.einsum("pq,qyz->pyz", rigidity_matrix[0], u, precision=HIGH)
    split_y = u.reshape(rows, width // nodes, nodes, depth)
    along_y = jnp.einsum("pq,xeqz->xepz", rigidity_matrix[1], split_y, precision=HIGH).reshape(
        rows, width, depth
    )
    wide = jnp.kron(jnp.eye(block // nodes, dtype=jnp.float32), rigidity_matrix[2])
    split_z = u.reshape(rows, width, depth // block, block)
    along_z = jnp.einsum("xyeq,pq->xyep", split_z, wide, precision=HIGH).reshape(rows, width, depth)
    return along_x + along_y + along_z


def least_squares(hess, beta):
    gram = jnp.dot(hess.T, hess, precision=HIGH)
    lower = jnp.linalg.cholesky(gram)
    right = (beta * hess[0])[:, None]
    middle = lax.linalg.triangular_solve(lower, right, left_side=True, lower=True)
    coeffs = lax.linalg.triangular_solve(
        lower, middle, left_side=True, lower=True, transpose_a=True
    )
    return coeffs[:, 0]


def iterated(
    forcing_vector,
    thermal_iterate,
    storage_over_step,
    opening_shares,
    flow_speed,
    diffusivity_root,
    sanction_weight,
    rigidity_matrix,
    contact_fluid_part,
    contact_fluid_volume,
    contact_solid_vertex,
    exchange_rate_factor,
):
    groups = lax.axis_size("group")
    bricks = lax.axis_size("brick")
    group_id = lax.axis_index("group")
    brick_id = lax.axis_index("brick")
    solid = group_id == groups - 1
    solid_flag = solid.astype(jnp.float32)
    fluid_flag = 1.0 - solid_flag
    rows, width, depth = forcing_vector.shape
    nodes = rigidity_matrix.shape[1]
    device = group_id * bricks + brick_id
    first_solid = (groups - 1) * bricks
    unrolled_array = thermal_iterate.reshape(-1)
    owned = (contact_fluid_part == group_id).astype(jnp.float32)
    target = jnp.where(solid, contact_solid_vertex, contact_fluid_volume).reshape(-1)
    picked = unrolled_array[target].reshape(contact_solid_vertex.shape)
    wall, near = lax.psum((picked * solid_flag, picked * owned * fluid_flag), "group")
    extra_rhs = jnp.where(
        solid, exchange_rate_factor * (near - wall), exchange_rate_factor * wall * owned
    )
    extra_diag = exchange_rate_factor * owned * fluid_flag
    rhs = (
        forcing_vector.reshape(-1)
        .at[target]
        .add(extra_rhs.reshape(-1))
        .reshape(forcing_vector.shape)
    )
    fluid_diag = (
        storage_over_step.reshape(-1)
        .at[target]
        .add(extra_diag.reshape(-1))
        .reshape(forcing_vector.shape)
    )
    shape = (rows, width, depth)
    global_row = device * rows + lax.broadcasted_iota(jnp.int32, shape, 0)
    face_x = opening_shares[0] * (global_row != first_solid * rows - 1).astype(jnp.float32)
    face_y = opening_shares[1] * open_faces(shape, 1)
    face_z = opening_shares[2] * open_faces(shape, 2)
    rims = passed_along(
        jnp.stack([face_x[-1], flow_speed[0][-1], sanction_weight[-1]]), ("group", "brick"), 1
    )
    face_low = rims[0]
    speed_low = rims[1]
    weight_low = rims[2]
    pair_low = 0.5 * (weight_low + sanction_weight[0]) * (device != first_solid).astype(jnp.float32)
    pair_up = passed_along(pair_low, "brick", -1)
    pair_y = (
        0.5 * (sanction_weight + shift_next(sanction_weight, 1)) * element_faces(shape, 1, nodes)
    )
    pair_z = (
        0.5 * (sanction_weight + shift_next(sanction_weight, 2)) * element_faces(shape, 2, nodes)
    )
    local_square = jnp.sum(rhs * rhs)
    solution = jnp.zeros_like(rhs)
    resid = rhs
    columns = []
    fluid_square, solid_square = lax.psum(
        (local_square * fluid_flag, local_square * solid_flag), ("group", "brick")
    )
    beta = jnp.sqrt(fluid_square)
    basis = [rhs / beta]
    direction = rhs
    norm_now = solid_square
    for step in range(ITERS):
        vector = jnp.where(solid, direction, basis[step])
        padded = extended(vector, ((("group", "brick"), 0),), 1)
        below = padded[0]
        above = padded[-1]

        def fluid_branch(unused):
            following = jnp.concatenate([vector[1:], above[None]], axis=0)
            flux_x = face_x * ((1.0 + flow_speed[0]) * vector - following)
            flux_low = face_low * ((1.0 + speed_low) * below - vector[0])
            out = (
                fluid_diag * vector
                + flux_x
                - jnp.concatenate([flux_low[None], flux_x[:-1]], axis=0)
            )
            flux_y = face_y * ((1.0 + flow_speed[1]) * vector - shift_next(vector, 1))
            flux_z = face_z * ((1.0 + flow_speed[2]) * vector - shift_next(vector, 2))
            return out + flux_y - shift_prev(flux_y, 1) + flux_z - shift_prev(flux_z, 2)

        def solid_branch(unused):
            out = storage_over_step * vector + diffusivity_root * stiffness_apply(
                diffusivity_root * vector, rigidity_matrix
            )
            jump_up = pair_up * (vector[-1] - above)
            jump_low = pair_low * (below - vector[0])
            out = out.at[0].add(-jump_low).at[rows - 1].add(jump_up)
            jump_y = pair_y * (vector - shift_next(vector, 1))
            jump_z = pair_z * (vector - shift_next(vector, 2))
            return out + jump_y - shift_prev(jump_y, 1) + jump_z - shift_prev(jump_z, 2)

        image = lax.cond(solid, solid_branch, fluid_branch, 0)
        inner = jnp.stack([jnp.sum(basis[j] * image) for j in range(step + 1)])
        heights, curvature = lax.psum(
            (inner * fluid_flag, jnp.sum(direction * image) * solid_flag), ("group", "brick")
        )
        fresh = image
        for j in range(step + 1):
            fresh = fresh - heights[j] * basis[j]
        alpha = norm_now / curvature
        solution = solution + alpha * direction
        resid = resid - alpha * image
        fresh_square, norm_next = lax.psum(
            (jnp.sum(fresh * fresh) * fluid_flag, jnp.sum(resid * resid) * solid_flag),
            ("group", "brick"),
        )
        length = jnp.sqrt(fresh_square)
        basis.append(fresh / length)
        columns.append(
            jnp.concatenate([heights, length[None], jnp.zeros((ITERS - 1 - step,), jnp.float32)])
        )
        direction = resid + norm_next / norm_now * direction
        norm_now = norm_next
    coeffs = least_squares(jnp.stack(columns, axis=1), beta)
    fluid_new = jnp.zeros_like(rhs)
    for step in range(ITERS):
        fluid_new = fluid_new + coeffs[step] * basis[step]
    return jnp.where(solid, solution, fluid_new)


F32 = jnp.float32
BF16 = jnp.bfloat16
MESH = pl.DeviceIdType.MESH
PIVOT_LEAST = 1e-3
REFINE_MOST = 3e-4
PARTS = 4
RAW = {1: ITERS + 1, 2: ITERS + 2}
DEEP = (3, 5)
SKIP = tuple(k + 1 for k in DEEP)


def iota(shape, dim):
    return lax.broadcasted_iota(jnp.int32, shape, dim)


def pieces(x):
    high = x.astype(BF16)
    return high, (x - high.astype(F32)).astype(BF16)


def total(x):
    return jnp.sum(jnp.sum(x, axis=0, keepdims=True), axis=1, keepdims=True)


def greatest(x):
    return jnp.max(jnp.max(x, axis=0, keepdims=True), axis=1, keepdims=True)


def dot(a, b, dims):
    return lax.dot_general(a, b, ((dims[0], dims[1]), ((), ())), preferred_element_type=F32)


def shift_rows(x, gamma):
    size = x.shape[0]
    after = pltpu.roll(x, size - 1, 0)
    row = iota(x.shape, 0)
    out = gamma * x + 0.5 * (pltpu.roll(x, 1, 0) + after) + jnp.where(row == 0, 0.5 * after, 0.0)
    return jnp.where(row < ITERS, out, 0.0)


def shift_lanes(x, gamma):
    size = x.shape[1]
    after = pltpu.roll(x, size - 1, 1)
    lane = iota(x.shape, 1)
    out = gamma * x + 0.5 * (pltpu.roll(x, 1, 1) + after) + jnp.where(lane == 0, 0.5 * after, 0.0)
    return jnp.where(lane < ITERS, out, 0.0)


def projected(gram, gamma, fluid):
    shape = gram.shape
    row, lane = iota(shape, 0), iota(shape, 1)
    wide = shift_lanes(gram, gamma)
    if fluid:
        normal, right = shift_rows(wide, gamma), shift_rows(gram, gamma)
    else:
        normal, right = jnp.where(row < ITERS, wide, 0.0), jnp.where(row < ITERS, gram, 0.0)
    table = jnp.where(lane < ITERS, normal, 0.0)
    table = jnp.where((lane == row + 8) & (row < ITERS), 1.0, table)
    table = jnp.where(lane == 16, pltpu.roll(right, 16, 1), table)
    margin = None
    for k in range(ITERS):
        pivot = table[k : k + 1, k : k + 1]
        spare = pivot - PIVOT_LEAST * normal[k : k + 1, k : k + 1]
        margin = spare if margin is None else jnp.minimum(margin, spare)
        scaled = table[k : k + 1, :] * (1.0 / pivot)
        column = jnp.where(row[:, :1] == k, 0.0, table[:, k : k + 1])
        table = jnp.where(row == k, scaled, table - column * scaled)
    coeffs = jnp.broadcast_to(table[:, 16:17], shape)
    inverse = jnp.where(lane < ITERS, pltpu.roll(table, shape[1] - 8, 1), 0.0)
    applied = gamma * coeffs + 0.5 * (pltpu.roll(coeffs, 1, 0) + pltpu.roll(coeffs, shape[0] - 1, 0))
    applied = applied + jnp.where(row == 1, 0.5 * pltpu.roll(coeffs, 1, 0), 0.0)
    rest = jnp.where(row == 0, 1.0, 0.0) - applied
    image = jnp.broadcast_to(jnp.sum(gram * rest, axis=0, keepdims=True), shape)
    image = shift_lanes(image, gamma) if fluid else jnp.where(lane < ITERS, image, 0.0)
    change = jnp.sum(inverse * image, axis=1, keepdims=True)
    coeffs = coeffs[:, :1] + change
    size = jnp.sum(jnp.abs(coeffs), axis=0, keepdims=True)
    moved = jnp.sum(jnp.abs(change), axis=0, keepdims=True)
    good = (margin > 0.0) & (moved < REFINE_MOST * size)
    return coeffs, jnp.where(good, 1.0, 0.0)


def ring_far(step, size):
    return min(step, size - step)


def kernel(
    groups,
    bricks,
    forcing_hbm,
    thermal_hbm,
    storage_hbm,
    opening_hbm,
    flow_hbm,
    root_hbm,
    weight_hbm,
    rigidity_hbm,
    part_hbm,
    volume_hbm,
    vertex_hbm,
    factor_hbm,
    out_hbm,
    flag,
    thermal,
    forcing,
    storage,
    opening,
    flow,
    root,
    weight,
    rigidity,
    part,
    volume,
    vertex,
    factor,
    basis,
    ax,
    gx,
    diag,
    uy,
    ly,
    uz,
    lz,
    stiff,
    uh,
    ul,
    wz,
    wxy,
    weight_low,
    weight_up,
    row_hot,
    col_hot,
    picked,
    walls,
    nears,
    gram_tile,
    near_slots,
    far_slots,
    out,
    second,
    ghost,
    ghost_diag,
    load_sem,
    store_sem,
    halo_send,
    halo_recv,
    coef_send,
    coef_recv,
    contact_send,
    contact_recv,
    near_send,
    near_recv,
    far_send,
    far_recv,
    deep_send,
    deep_recv,
    ghost_send,
    ghost_recv,
):
    group = lax.axis_index("group")
    brick = lax.axis_index("brick")
    rows, width, depth = forcing.shape
    plane = (width, depth)
    cells = rows * width
    solid = group == groups - 1
    fluid = group != groups - 1
    inner, outer = 8, bricks // 8
    low_id = lax.rem(brick, inner)
    high_id = group * outer + brick // inner
    n_far = groups * outer
    at_top = (brick == bricks - 1) & (group >= groups - 2)
    at_bottom = (brick == 0) & ((group == 0) | (group == groups - 1))
    has_up, has_down = jnp.logical_not(at_top), jnp.logical_not(at_bottom)
    far_up = (brick == bricks - 1) & (group < groups - 2)
    far_down = (brick == 0) & (group > 0) & fluid
    device = group * bricks + brick
    up_id = lax.rem(device + 1, groups * bricks)
    down_id = lax.rem(device + groups * bricks - 1, groups * bricks)
    up = (up_id // bricks, lax.rem(up_id, bricks))
    down = (down_id // bricks, lax.rem(down_id, bricks))

    names = [
        (vertex_hbm, vertex),
        (volume_hbm, volume),
        (thermal_hbm, thermal),
        (part_hbm, part),
        (factor_hbm, factor),
        (opening_hbm, opening),
        (flow_hbm, flow),
        (storage_hbm, storage),
        (weight_hbm, weight),
        (root_hbm, root),
        (rigidity_hbm, rigidity),
        (forcing_hbm, forcing),
    ]
    loads = [pltpu.make_async_copy(s, d, load_sem.at[i]) for i, (s, d) in enumerate(names)]
    for load in loads:
        load.start()
    (l_vertex, l_volume, l_thermal, l_part, l_factor, l_opening, l_flow, l_storage, l_weight, l_root, l_rigid, l_forcing) = loads

    plane_id = brick // inner
    near_peers, far_peers = [], []
    for dz, dc in sorted(((a, b) for a in range(inner // 2) for b in range(2)), key=lambda at: -ring_far(at[0], inner // 2)):
        if dz or dc:
            peer = lax.rem(low_id // 2 + dz, inner // 2) * 2 + lax.rem(low_id + dc, 2)
            near_peers.append((peer, (group, plane_id * inner + peer)))
    steps = sorted(
        ((a, b) for a in range(groups) for b in range(outer)), key=lambda at: -ring_far(at[0], groups) - ring_far(at[1], outer)
    )
    for dx, dy in steps:
        if dx or dy:
            x_id, y_id = lax.rem(group + dx, groups), lax.rem(plane_id + dy, outer)
            far_peers.append((x_id * outer + y_id, (x_id, y_id * inner + low_id)))

    barrier = pltpu.get_barrier_semaphore()
    for peer, where in far_peers + near_peers:
        pl.semaphore_signal(barrier, inc=1, device_id=where, device_id_type=MESH)

    @pl.when(has_up)
    def _():
        pl.semaphore_signal(barrier, inc=1, device_id=up, device_id_type=MESH)

    @pl.when(has_down)
    def _():
        pl.semaphore_signal(barrier, inc=1, device_id=down, device_id_type=MESH)

    @pl.when(at_bottom)
    def _():
        for k in range(ITERS):
            basis[RAW.get(k, k), 0] = jnp.zeros(plane, F32)

    @pl.when(at_top)
    def _():
        for k in range(ITERS):
            basis[RAW.get(k, k), rows + 1] = jnp.zeros(plane, F32)

    l_vertex.wait()
    l_volume.wait()
    target = jnp.where(solid, vertex[...], volume[...])
    cell_row, cell_col = target >> 8, target & 255
    lines = target.shape[0]
    points = lines * 128
    for j in range(lines):
        span = pl.ds(j * 128, 128)
        row_hot[:, span] = jnp.where(iota((cells, 128), 0) == cell_row[j : j + 1], 1.0, 0.0).astype(BF16)
        col_hot[:, span] = jnp.where(iota((depth, 128), 0) == cell_col[j : j + 1], 1.0, 0.0).astype(BF16)
    l_thermal.wait()
    high, low = pieces(thermal[...].reshape(cells, depth))
    hot = row_hot[...]
    found = dot(high, hot, ((0,), (0,))) + dot(low, hot, ((0,), (0,)))
    value = jnp.sum(found * col_hot[...].astype(F32), axis=0, keepdims=True)
    value = jnp.concatenate([value[:, j * 128 : (j + 1) * 128] for j in range(lines)], axis=0)
    l_part.wait()
    l_factor.wait()
    owned = jnp.where(part[...] == group, 1.0, 0.0)
    picked[0:lines] = jnp.where(solid, value, value * owned)
    picked[lines:] = jnp.zeros((8 - lines, 128), F32)

    pl.semaphore_wait(barrier, inner - 1 + n_far - 1 + has_up.astype(jnp.int32) + has_down.astype(jnp.int32))

    def wall_copy(g):
        return pltpu.make_async_remote_copy(
            picked, walls, contact_send.at[g], contact_recv.at[groups - 1], device_id=(g, brick), device_id_type=MESH
        )

    near_copy = pltpu.make_async_remote_copy(
        picked, nears.at[group], contact_send.at[0], contact_recv.at[group], device_id=(groups - 1, brick), device_id_type=MESH
    )

    @pl.when(solid)
    def _():
        for g in range(groups - 1):
            wall_copy(g).start()

    @pl.when(fluid)
    def _():
        near_copy.start()

    l_opening.wait()
    l_flow.wait()
    l_weight.wait()
    coef_a = pltpu.make_async_remote_copy(
        ax.at[rows], ax.at[0], coef_send.at[0], coef_recv.at[0], device_id=up, device_id_type=MESH
    )
    coef_g = pltpu.make_async_remote_copy(
        gx.at[rows], gx.at[0], coef_send.at[1], coef_recv.at[1], device_id=up, device_id_type=MESH
    )
    coef_up = pltpu.make_async_remote_copy(
        weight.at[rows - 1], weight_low, coef_send.at[0], coef_recv.at[0], device_id=up, device_id_type=MESH
    )
    coef_down = pltpu.make_async_remote_copy(
        weight.at[0], weight_up, coef_send.at[1], coef_recv.at[1], device_id=down, device_id_type=MESH
    )

    @pl.when(fluid)
    def _():
        last = jnp.where(at_top, 0.0, opening[0, rows - 1])
        ax[rows] = last
        gx[rows] = last * (1.0 + flow[0, rows - 1])

    @pl.when(fluid & has_up)
    def _():
        coef_a.start()
        coef_g.start()

    @pl.when(solid & has_up)
    def _():
        coef_up.start()

    @pl.when(solid & has_down)
    def _():
        coef_down.start()

    l_storage.wait()
    l_root.wait()
    l_rigid.wait()

    def spread(values):
        flat = jnp.concatenate([values[j : j + 1] for j in range(lines)], axis=1)
        high, low = pieces(flat)
        cols = col_hot[...].astype(F32)
        return dot(row_hot[...], (cols * high.astype(F32)).astype(BF16), ((1,), (1,))) + dot(
            row_hot[...], (cols * low.astype(F32)).astype(BF16), ((1,), (1,))
        )

    def fold(x, op):
        y = x.reshape(width // 8, 8, depth)
        return op(y, axis=0)

    y_at, z_at = iota(plane, 0), iota(plane, 1)

    def write_stats(d_max, d_min, o_sum):
        lane = iota((8, 128), 1)
        tile = jnp.where(lane == 0, greatest(d_max), jnp.where(lane == 1, greatest(-d_min), jnp.where(lane == 2, total(o_sum), 0.0)))
        near_slots[0, low_id, 0:8] = tile

    start = (jnp.full((8, depth), -1e30, F32), jnp.full((8, depth), 1e30, F32), jnp.zeros((8, depth), F32))

    @pl.when(fluid)
    def _():
        extra = spread(factor[...] * owned).reshape(rows, width, depth)
        storage[...] = storage[...] + extra

        def second(r, carry):
            d_max, d_min, o_sum = carry
            a_y = jnp.where(y_at == width - 1, 0.0, opening[1, r])
            g_y = a_y * (1.0 + flow[1, r])
            g_low = pltpu.roll(g_y, 1, 0)
            uy[r] = a_y
            ly[r] = g_low
            a_x = jnp.where(at_top & (r == rows - 1), 0.0, opening[0, r])
            g_x = a_x * (1.0 + flow[0, r])

            @pl.when(r < rows - 1)
            def _():
                ax[r + 1] = a_x
                gx[r + 1] = g_x

            d = storage[r] + g_x + g_y + pltpu.roll(a_y, 1, 0)
            o = a_x + g_x + a_y + g_low
            a_z = jnp.where(z_at == depth - 1, 0.0, opening[2, r])
            g_z = a_z * (1.0 + flow[2, r])
            g_low = pltpu.roll(g_z, 1, 1)
            uz[r] = a_z
            lz[r] = g_low
            d = d + g_z + pltpu.roll(a_z, 1, 1)
            o = o + a_z + g_low
            d = d + jnp.where(r == 0, 0.0, opening[0, jnp.maximum(r - 1, 0)])
            diag[r] = d
            return jnp.maximum(d_max, fold(d, jnp.max)), jnp.minimum(d_min, fold(d, jnp.min)), o_sum + fold(o, jnp.sum)

        write_stats(*lax.fori_loop(0, rows, second, start))

    @pl.when(solid)
    def _():
        eye = iota((8, 8), 0) == iota((8, 8), 1)
        both = rigidity[0] + rigidity[1] + rigidity[2]
        size = jnp.abs(rigidity[0]) + jnp.abs(rigidity[1]) + jnp.abs(rigidity[2])
        trace = total(jnp.where(eye, both, 0.0)) * (1.0 / 8)
        off = total(jnp.where(eye, 0.0, size)) * (1.0 / 8)
        block_z = jnp.where(iota((8, depth), 1) % 8 == iota((8, depth), 0), 1.0, 0.0)
        spread_z = lax.dot_general(
            lax.dot_general(block_z, rigidity[2], (((0,), (1,)), ((), ())), precision=HIGH, preferred_element_type=F32),
            block_z,
            (((1,), (0,)), ((), ())),
            precision=HIGH,
            preferred_element_type=F32,
        )
        same = (iota((depth, depth), 0) // 8) == (iota((depth, depth), 1) // 8)
        high, low = pieces(jnp.where(same, spread_z, 0.0))
        wz[0], wz[1] = high, low
        outer_x = jnp.where(iota((8, 64), 1) // 8 == iota((8, 64), 0), 1.0, 0.0)
        inner_y = jnp.where(iota((8, 64), 1) % 8 == iota((8, 64), 0), 1.0, 0.0)

        def expand(matrix, hot):
            left = lax.dot_general(hot, matrix, (((0,), (0,)), ((), ())), precision=HIGH, preferred_element_type=F32)
            return lax.dot_general(left, hot, (((1,), (0,)), ((), ())), precision=HIGH, preferred_element_type=F32)

        same_y = iota((64, 64), 0) % 8 == iota((64, 64), 1) % 8
        same_x = iota((64, 64), 0) // 8 == iota((64, 64), 1) // 8
        mixed = jnp.where(same_y, expand(rigidity[0], outer_x), 0.0) + jnp.where(same_x, expand(rigidity[1], inner_y), 0.0)
        high, low = pieces(mixed)
        wxy[...] = jnp.concatenate([high, high, low], axis=1)

        def second(r, carry):
            d_max, d_min, o_sum = carry
            w = weight[r]
            b_y = jnp.where((y_at % 8 == 7) & (y_at < width - 1), 0.5 * (w + pltpu.roll(w, width - 1, 0)), 0.0)
            b_low = pltpu.roll(b_y, 1, 0)
            uy[r] = b_y
            ly[r] = b_low
            pair = b_y + b_low
            b_z = jnp.where((z_at % 8 == 7) & (z_at < depth - 1), 0.5 * (w + pltpu.roll(w, depth - 1, 1)), 0.0)
            b_low = pltpu.roll(b_z, 1, 1)
            uz[r] = b_z
            lz[r] = b_low
            pair = pair + b_z + b_low
            d = storage[r] + pair
            diag[r] = d
            square = root[r] * root[r]
            whole = d + square * trace
            o = pair + square * off
            return jnp.maximum(d_max, fold(whole, jnp.max)), jnp.minimum(d_min, fold(whole, jnp.min)), o_sum + fold(o, jnp.sum)

        write_stats(*lax.fori_loop(0, rows, second, start))

    def near_start(which, height):
        for o, (peer, where) in enumerate(near_peers):
            pltpu.make_async_remote_copy(
                near_slots.at[which, low_id, pl.ds(0, height)],
                near_slots.at[which, low_id, pl.ds(0, height)],
                near_send.at[which, o],
                near_recv.at[which, low_id],
                device_id=where,
                device_id_type=MESH,
            ).start()

    def near_wait(which, height):
        for o, (peer, where) in enumerate(near_peers):
            copy = pltpu.make_async_remote_copy(
                near_slots.at[which, peer, pl.ds(0, height)],
                near_slots.at[which, peer, pl.ds(0, height)],
                near_send.at[which, o],
                near_recv.at[which, peer],
                device_id=where,
                device_id_type=MESH,
            )
            copy.wait_recv()
            copy.wait_send()

    def far_start(which, height):
        for o, (peer, where) in enumerate(far_peers):
            pltpu.make_async_remote_copy(
                far_slots.at[which, high_id, pl.ds(0, height)],
                far_slots.at[which, high_id, pl.ds(0, height)],
                far_send.at[which, o],
                far_recv.at[which, high_id],
                device_id=where,
                device_id_type=MESH,
            ).start()

    def far_wait(which, height):
        for o, (peer, where) in enumerate(far_peers):
            copy = pltpu.make_async_remote_copy(
                far_slots.at[which, peer, pl.ds(0, height)],
                far_slots.at[which, peer, pl.ds(0, height)],
                far_send.at[which, o],
                far_recv.at[which, peer],
                device_id=where,
                device_id_type=MESH,
            )
            copy.wait_recv()
            copy.wait_send()

    def merge_stats(tiles):
        lane = iota((8, 128), 1)
        most, summed = tiles[0], tiles[0]
        for tile in tiles[1:]:
            most, summed = jnp.maximum(most, tile), summed + tile
        return jnp.where(lane == 2, summed, most)

    near_start(0, 8)

    l_forcing.wait()

    part_rows = width // PARTS

    def halo_up(k, j):
        span = pl.ds(j * part_rows, part_rows)
        at = RAW.get(k, k)
        return pltpu.make_async_remote_copy(
            basis.at[at, rows, span],
            basis.at[at, 0, span],
            halo_send.at[k, 0, j],
            halo_recv.at[k, 0, j],
            device_id=up,
            device_id_type=MESH,
        )

    def halo_down(k, j):
        span = pl.ds(j * part_rows, part_rows)
        at = RAW.get(k, k)
        return pltpu.make_async_remote_copy(
            basis.at[at, 1, span],
            basis.at[at, rows + 1, span],
            halo_send.at[k, 1, j],
            halo_recv.at[k, 1, j],
            device_id=down,
            device_id_type=MESH,
        )

    def linked(k):
        if k in SKIP:
            return has_up & jnp.logical_not(far_up), has_down & jnp.logical_not(far_down)
        return has_up, has_down

    def send_halos(k, j):
        to_up, to_down = linked(k)

        @pl.when(to_up)
        def _():
            halo_up(k, j).start()

        @pl.when(to_down)
        def _():
            halo_down(k, j).start()

    def deep_up(i):
        return pltpu.make_async_remote_copy(
            basis.at[DEEP[i], rows - 1], second.at[0, i], deep_send.at[i, 0], deep_recv.at[i, 0], device_id=up, device_id_type=MESH
        )

    def deep_down(i):
        return pltpu.make_async_remote_copy(
            basis.at[DEEP[i], 2], second.at[1, i], deep_send.at[i, 1], deep_recv.at[i, 1], device_id=down, device_id_type=MESH
        )

    def ghost_up(i):
        source = (ghost_diag.at[0], uy.at[rows - 1], ly.at[rows - 1], uz.at[rows - 1], lz.at[rows - 1], gx.at[rows - 1])[i]
        return pltpu.make_async_remote_copy(
            source, ghost.at[0, i], ghost_send.at[0, i], ghost_recv.at[0, i], device_id=up, device_id_type=MESH
        )

    def ghost_down(i):
        source = (ghost_diag.at[1], uy.at[0], ly.at[0], uz.at[0], lz.at[0], ax.at[1])[i]
        return pltpu.make_async_remote_copy(
            source, ghost.at[1, i], ghost_send.at[1, i], ghost_recv.at[1, i], device_id=down, device_id_type=MESH
        )

    def send_deep(i):
        @pl.when(far_up)
        def _():
            deep_up(i).start()

        @pl.when(far_down)
        def _():
            deep_down(i).start()

    @pl.when(fluid)
    def _():
        pltpu.make_async_remote_copy(
            picked, walls, contact_send.at[0], contact_recv.at[groups - 1], device_id=(groups - 1, brick), device_id_type=MESH
        ).wait_recv()

    @pl.when(solid)
    def _():
        for g in range(groups - 1):
            pltpu.make_async_remote_copy(
                picked, nears.at[g], contact_send.at[g], contact_recv.at[g], device_id=(g, brick), device_id_type=MESH
            ).wait_recv()
        walls[...] = nears[0] + nears[1] + nears[2] - picked[...]

    heat = factor[...] * walls[0:lines]
    extra = spread(jnp.where(solid, heat, heat * owned)).reshape(rows, width, depth)
    basis[0, 1 : rows + 1] = forcing[...] + extra
    for j in range(PARTS):
        send_halos(0, j)

    @pl.when(at_bottom)
    def _():
        gx[0] = jnp.zeros(plane, F32)

    @pl.when(fluid & has_down)
    def _():
        coef_a.wait_recv()
        coef_g.wait_recv()
        diag[0] = diag[0] + ax[0]

    @pl.when(solid & has_down)
    def _():
        coef_up.wait_recv()
        gx[0] = 0.5 * (weight_low[...] + weight[0])
        diag[0] = diag[0] + gx[0]

    @pl.when(solid & has_up)
    def _():
        coef_down.wait_recv()
        ax[rows] = 0.5 * (weight[rows - 1] + weight_up[...])
        diag[rows - 1] = diag[rows - 1] + ax[rows]

    @pl.when(solid & at_top)
    def _():
        ax[rows] = jnp.zeros(plane, F32)

    def gram_row(k):
        def body(r, accs):
            accs = list(accs)
            for j in range(width // 8):
                span = slice(8 * j, 8 * j + 8)
                mine = basis[k, r + 1, span, :]
                for i in range(k + 1):
                    other = mine if i == k else basis[i, r + 1, span, :]
                    accs[i] = accs[i] + mine * other
            return tuple(accs)

        accs = lax.fori_loop(0, rows, body, tuple(jnp.zeros((8, depth), F32) for _ in range(k + 1)))
        row, lane = iota((16, 128), 0), iota((16, 128), 1)
        tile = jnp.zeros((16, 128), F32) if k == 0 else gram_tile[...]
        for i in range(k + 1):
            spot = ((row == i) & (lane == k)) | ((row == k) & (lane == i))
            tile = jnp.where(spot, total(accs[i]), tile)
        gram_tile[...] = tile

    def local(r, v):
        return (
            diag[r] * v
            - uy[r] * pltpu.roll(v, width - 1, 0)
            - ly[r] * pltpu.roll(v, 1, 0)
            - uz[r] * pltpu.roll(v, depth - 1, 1)
            - lz[r] * pltpu.roll(v, 1, 1)
        )

    def apply(k, scale):
        at, to = (RAW.get(k, k), RAW[k + 1]) if scale is None else (k, k + 1)

        def keep(r, q):
            if scale is None:
                basis[to, r + 1] = q
            else:
                basis[to, r + 1] = scale * q - basis[k - 1, r + 1]

        @pl.when(fluid)
        def _():
            def middle(r, carry):
                v = basis[at, r + 1]
                keep(r, local(r, v) - gx[r] * basis[at, r] - ax[r + 1] * basis[at, r + 2])
                return carry

            keep(0, local(0, basis[at, 1]) - ax[1] * basis[at, 2])
            keep(rows - 1, local(rows - 1, basis[at, rows]) - gx[rows - 1] * basis[at, rows - 1])
            lax.fori_loop(1, rows - 1, middle, 0)

        @pl.when(solid)
        def _():
            for e in range(width // 8):
                u = (root[:, 8 * e : 8 * e + 8, :] * basis[at, 1 : rows + 1, 8 * e : 8 * e + 8, :]).reshape(64, depth)
                high, low = pieces(u)
                uh[e], ul[e] = high, low
                stiff[e] = dot(wxy[...], jnp.concatenate([high, low, high], axis=0), ((1,), (0,)))
            high, low = uh[...].reshape(cells, depth), ul[...].reshape(cells, depth)
            along = dot(high, wz[0], ((1,), (0,))) + dot(low, wz[0], ((1,), (0,))) + dot(high, wz[1], ((1,), (0,)))
            stiff[...] = stiff[...] + along.reshape(width // 8, 64, depth)

            def each(r, carry):
                force = stiff[:, pl.ds(r * 8, 8), :].reshape(width, depth)
                keep(r, local(r, basis[at, r + 1]) + root[r] * force)
                return carry

            lax.fori_loop(0, rows, each, 0)

    def finish(k, scale, mix=None):
        at, to = RAW.get(k, k), (RAW[k + 1] if scale is None else k + 1)
        for j in range(PARTS):
            span = slice(j * part_rows, (j + 1) * part_rows)

            from_up, from_down = linked(k)

            @pl.when(from_down)
            def _():
                halo_up(k, j).wait_recv()

            @pl.when(from_up)
            def _():
                halo_down(k, j).wait_recv()

            for own, halo, coef in ((1, 0, gx.at[0]), (rows, rows + 1, ax.at[rows])):
                value = basis[at, halo, span]
                if mix is not None:
                    value = mix[0] * value + mix[1] * basis[RAW[1], halo, span] + mix[2] * basis[0, halo, span]
                    basis[k, halo, span] = value
                value = coef[span] * value
                if scale is not None:
                    value = scale * value
                basis[to, own, span] = basis[to, own, span] - value
            if k + 1 < ITERS:
                send_halos(k + 1, j)

    def extend(i):
        k = DEEP[i]

        def row(side, near, halo, inward):
            v = basis[k, halo]
            q = (
                (ghost[side, 0] - center) * v
                - ghost[side, 1] * pltpu.roll(v, width - 1, 0)
                - ghost[side, 2] * pltpu.roll(v, 1, 0)
                - ghost[side, 3] * pltpu.roll(v, depth - 1, 1)
                - ghost[side, 4] * pltpu.roll(v, 1, 1)
                - ghost[side, 5] * second[side, i]
                - inward * basis[k, near]
            )
            basis[k + 1, halo] = scale * q - basis[k - 1, halo]

        @pl.when(far_down)
        def _():
            deep_up(i).wait_recv()
            if i == 0:
                for n in range(6):
                    ghost_up(n).wait_recv()
            row(0, 1, 0, ax[0])

        @pl.when(far_up)
        def _():
            deep_down(i).wait_recv()
            if i == 0:
                for n in range(6):
                    ghost_down(n).wait_recv()
            row(1, rows, rows + 1, gx[rows])

    apply(0, None)
    near_wait(0, 8)
    far_slots[0, high_id, 0:8] = merge_stats([near_slots[0, i, 0:8] for i in range(inner)])
    far_start(0, 8)
    finish(0, None)

    @pl.when(far_up)
    def _():
        ghost_diag[0] = diag[rows - 1]
        for n in range(6):
            ghost_up(n).start()

    @pl.when(far_down)
    def _():
        ghost_diag[1] = diag[0]
        for n in range(6):
            ghost_down(n).start()

    apply(1, None)
    gram_row(0)
    finish(1, None)
    far_wait(0, 8)
    split = (groups - 1) * outer

    def interval(tiles, count):
        stats = merge_stats(tiles)
        mean = stats[0:1, 2:3] * (1.0 / count)
        high = stats[0:1, 0:1] + 0.25 * mean
        low = jnp.maximum(-stats[0:1, 1:2] - 0.5 * mean, 0.0)
        return 0.5 * (high + low), 0.5 * (high - low)

    c_fluid, e_fluid = interval([far_slots[0, i, 0:8] for i in range(split)], float((groups - 1) * bricks * cells * depth))
    c_solid, e_solid = interval([far_slots[0, i, 0:8] for i in range(split, n_far)], float(bricks * cells * depth))
    center = jnp.where(solid, c_solid, c_fluid)
    inv_e = 1.0 / jnp.where(solid, e_solid, e_fluid)
    scale = 2.0 * inv_e

    mix = (scale * inv_e, -2.0 * scale * center * inv_e, scale * inv_e * center * center - 1.0)

    def convert(r, carry):
        zero, one, two = basis[0, r + 1], basis[RAW[1], r + 1], basis[RAW[2], r + 1]
        basis[1, r + 1] = (one - center * zero) * inv_e
        basis[2, r + 1] = mix[0] * two + mix[1] * one + mix[2] * zero
        diag[r] = diag[r] - center
        return carry

    lax.fori_loop(0, rows, convert, 0)
    for k in range(2, ITERS):
        apply(k, scale)
        if k + 1 in DEEP:
            send_deep(DEEP.index(k + 1))
        if k == 2:
            gram_row(1)
        gram_row(k)
        finish(k, scale, mix if k == 2 else None)
        if k in DEEP:
            extend(DEEP.index(k))
    gram_row(ITERS)

    near_slots[1, low_id] = gram_tile[...]
    near_start(1, 16)
    near_wait(1, 16)
    summed = near_slots[1, 0]
    for i in range(1, inner):
        summed = summed + near_slots[1, i]
    far_slots[1, high_id] = summed
    far_start(1, 16)
    far_wait(1, 16)
    gram_fluid = far_slots[1, 0]
    for i in range(1, split):
        gram_fluid = gram_fluid + far_slots[1, i]
    gram_solid = far_slots[1, split]
    for i in range(split + 1, n_far):
        gram_solid = gram_solid + far_slots[1, i]
    y_fluid, ok_fluid = projected(gram_fluid, c_fluid / e_fluid, True)
    y_solid, ok_solid = projected(gram_solid, c_solid / e_solid, False)
    coeffs = jnp.where(solid, y_solid, y_fluid) * inv_e
    flag[0] = jnp.max(ok_fluid * ok_solid).astype(jnp.int32)
    weights = [coeffs[k : k + 1, :1] for k in range(ITERS)]

    def combine(r, carry):
        acc = weights[0] * basis[0, r + 1]
        for k in range(1, ITERS):
            acc = acc + weights[k] * basis[k, r + 1]
        out[r] = acc
        pltpu.make_async_copy(out.at[r], out_hbm.at[r], store_sem.at[r]).start()
        return carry

    lax.fori_loop(0, rows, combine, 0)

    @pl.when(solid)
    def _():
        for g in range(groups - 1):
            wall_copy(g).wait_send()

    @pl.when(fluid)
    def _():
        near_copy.wait_send()

    @pl.when(fluid & has_up)
    def _():
        coef_a.wait_send()
        coef_g.wait_send()

    @pl.when(solid & has_up)
    def _():
        coef_up.wait_send()

    @pl.when(solid & has_down)
    def _():
        coef_down.wait_send()

    @pl.when(far_up)
    def _():
        for n in range(6):
            ghost_up(n).wait_send()
        for i in range(len(DEEP)):
            deep_up(i).wait_send()

    @pl.when(far_down)
    def _():
        for n in range(6):
            ghost_down(n).wait_send()
        for i in range(len(DEEP)):
            deep_down(i).wait_send()

    for k in range(ITERS):
        sent_up, sent_down = linked(k)
        for j in range(PARTS):

            @pl.when(sent_up)
            def _():
                halo_up(k, j).wait_send()

            @pl.when(sent_down)
            def _():
                halo_down(k, j).wait_send()

    for r in range(rows):
        pltpu.make_async_copy(out.at[r], out_hbm.at[r], store_sem.at[r]).wait()


def handed_on(result):
    rows = result.shape[0]

    def body(source, target, held, in_sem, out_sem):
        ins = [pltpu.make_async_copy(source.at[i], held.at[i], in_sem.at[i]) for i in range(rows)]
        outs = [pltpu.make_async_copy(held.at[i], target.at[i], out_sem.at[i]) for i in range(rows)]
        for copy in ins:
            copy.start()
        for arrived, copy in zip(ins, outs):
            arrived.wait()
            copy.start()
        for copy in outs:
            copy.wait()

    return pl.pallas_call(
        body,
        out_shape=jax.ShapeDtypeStruct(result.shape, result.dtype),
        in_specs=[pl.BlockSpec(memory_space=pl.ANY)],
        out_specs=pl.BlockSpec(memory_space=pl.ANY),
        scratch_shapes=[pltpu.VMEM(result.shape, F32), pltpu.SemaphoreType.DMA((rows,)), pltpu.SemaphoreType.DMA((rows,))],
        name="handed_on",
    )(result)


def shards(*arguments):
    groups, bricks = lax.axis_size("group"), lax.axis_size("brick")
    forcing = arguments[0]
    rows, width, depth = slab = forcing.shape
    lines = arguments[8].shape[0]
    points = lines * 128
    n_far = groups * (bricks // 8)
    vm = pltpu.VMEM
    scratch = (
        [vm(slab, F32)] * 3
        + [vm((3,) + slab, F32)] * 2
        + [vm(slab, F32)] * 2
        + [vm((3, 8, 8), F32)]
        + [vm((lines, 128), jnp.int32)] * 3
        + [vm((lines, 128), F32)]
        + [vm((ITERS + 3, rows + 2, width, depth), F32)]
        + [vm((rows + 1, width, depth), F32)] * 2
        + [vm(slab, F32)] * 5
        + [vm((width // 8, 64, depth), F32)]
        + [vm((width // 8, 64, depth), BF16)] * 2
        + [vm((2, depth, depth), BF16), vm((64, 192), BF16)]
        + [vm((width, depth), F32)] * 2
        + [vm((rows * width, points), BF16), vm((depth, points), BF16)]
        + [vm((8, 128), F32)] * 2
        + [vm((groups - 1, 8, 128), F32)]
        + [vm((16, 128), F32), vm((2, 8, 16, 128), F32), vm((2, n_far, 16, 128), F32)]
        + [vm(slab, F32)]
        + [vm((2, len(DEEP), width, depth), F32), vm((2, 6, width, depth), F32), vm((2, width, depth), F32)]
    )
    dma = pltpu.SemaphoreType.DMA
    semaphores = [
        dma((12,)),
        dma((rows,)),
        dma((ITERS, 2, PARTS)),
        dma((ITERS, 2, PARTS)),
        dma((2,)),
        dma((2,)),
        dma((groups,)),
        dma((groups,)),
        dma((2, 8)),
        dma((2, 8)),
        dma((2, n_far)),
        dma((2, n_far)),
        dma((len(DEEP), 2)),
        dma((len(DEEP), 2)),
        dma((2, 6)),
        dma((2, 6)),
    ]
    result, flag = pl.pallas_call(
        functools.partial(kernel, groups, bricks),
        out_shape=(jax.ShapeDtypeStruct(slab, F32), jax.ShapeDtypeStruct((1,), jnp.int32)),
        in_specs=[pl.BlockSpec(memory_space=pl.ANY)] * 12,
        out_specs=(pl.BlockSpec(memory_space=pl.ANY), pl.BlockSpec(memory_space=pltpu.SMEM)),
        scratch_shapes=scratch + semaphores,
        compiler_params=pltpu.CompilerParams(collective_id=0, has_side_effects=True, vmem_limit_bytes=56 * 2**20),
        name="coupled",
    )(*arguments)
    return lax.cond(flag[0] > 0, lambda: handed_on(result), lambda: iterated(*arguments))


def solution(mesh):
    return jax.shard_map(
        shards,
        mesh=mesh,
        in_specs=(
            P(("group", "brick"), None, None),
            P(("group", "brick"), None, None),
            P(("group", "brick"), None, None),
            P(None, ("group", "brick"), None, None),
            P(None, ("group", "brick"), None, None),
            P(("group", "brick"), None, None),
            P(("group", "brick"), None, None),
            P(),
            P("brick", None),
            P("brick", None),
            P("brick", None),
            P("brick", None),
        ),
        out_specs=P(("group", "brick"), None, None),
        check_vma=False,
    )
```

```python
import functools

import jax
import jax.numpy as jnp
from jax import lax
from jax.experimental import pallas as pl
from jax.experimental.pallas import tpu as pltpu
from jax.sharding import PartitionSpec as P

ITERS = 8


HIGH = lax.Precision.HIGHEST


def passed_along(value, axis, steps):
    count = lax.axis_size(axis)
    leading, last = (max(0, -steps), min(count, count - steps))
    return lax.ppermute(value, axis, [(source, source + steps) for source in range(leading, last)])


def extended(cells, sides, width):
    for axis, dim in sides:
        count = lax.axis_size(axis)
        ends = count - 1
        head = lax.slice_in_dim(cells, 0, width, axis=dim)
        tail = lax.slice_in_dim(cells, cells.shape[dim] - width, cells.shape[dim], axis=dim)
        cells = jnp.concatenate(
            [
                lax.ppermute(tail, axis, [(i, (i + 1) % count) for i in range(ends)]),
                cells,
                lax.ppermute(head, axis, [((i + 1) % count, i) for i in range(ends)]),
            ],
            axis=dim,
        )
    return cells


def shift_next(v, axis):
    size = v.shape[axis]
    inner = lax.slice_in_dim(v, 1, size, axis=axis)
    zero = jnp.zeros_like(lax.slice_in_dim(v, 0, 1, axis=axis))
    return jnp.concatenate([inner, zero], axis=axis)


def shift_prev(v, axis):
    size = v.shape[axis]
    inner = lax.slice_in_dim(v, 0, size - 1, axis=axis)
    zero = jnp.zeros_like(lax.slice_in_dim(v, 0, 1, axis=axis))
    return jnp.concatenate([zero, inner], axis=axis)


def open_faces(shape, axis):
    index = lax.broadcasted_iota(jnp.int32, shape, axis)
    return (index < shape[axis] - 1).astype(jnp.float32)


def element_faces(shape, axis, nodes):
    index = lax.broadcasted_iota(jnp.int32, shape, axis)
    inside = (index % nodes == nodes - 1) & (index < shape[axis] - 1)
    return inside.astype(jnp.float32)


def stiffness_apply(u, rigidity_matrix):
    nodes = rigidity_matrix.shape[1]
    rows, width, depth = u.shape
    block = min(depth, 128)
    along_x = jnp.einsum("pq,qyz->pyz", rigidity_matrix[0], u, precision=HIGH)
    split_y = u.reshape(rows, width // nodes, nodes, depth)
    along_y = jnp.einsum("pq,xeqz->xepz", rigidity_matrix[1], split_y, precision=HIGH).reshape(
        rows, width, depth
    )
    wide = jnp.kron(jnp.eye(block // nodes, dtype=jnp.float32), rigidity_matrix[2])
    split_z = u.reshape(rows, width, depth // block, block)
    along_z = jnp.einsum("xyeq,pq->xyep", split_z, wide, precision=HIGH).reshape(rows, width, depth)
    return along_x + along_y + along_z


def least_squares(hess, beta):
    gram = jnp.dot(hess.T, hess, precision=HIGH)
    lower = jnp.linalg.cholesky(gram)
    right = (beta * hess[0])[:, None]
    middle = lax.linalg.triangular_solve(lower, right, left_side=True, lower=True)
    coeffs = lax.linalg.triangular_solve(
        lower, middle, left_side=True, lower=True, transpose_a=True
    )
    return coeffs[:, 0]


def iterated(
    forcing_vector,
    thermal_iterate,
    storage_over_step,
    opening_shares,
    flow_speed,
    diffusivity_root,
    sanction_weight,
    rigidity_matrix,
    contact_fluid_part,
    contact_fluid_volume,
    contact_solid_vertex,
    exchange_rate_factor,
):
    groups = lax.axis_size("group")
    bricks = lax.axis_size("brick")
    group_id = lax.axis_index("group")
    brick_id = lax.axis_index("brick")
    solid = group_id == groups - 1
    solid_flag = solid.astype(jnp.float32)
    fluid_flag = 1.0 - solid_flag
    rows, width, depth = forcing_vector.shape
    nodes = rigidity_matrix.shape[1]
    device = group_id * bricks + brick_id
    first_solid = (groups - 1) * bricks
    unrolled_array = thermal_iterate.reshape(-1)
    owned = (contact_fluid_part == group_id).astype(jnp.float32)
    target = jnp.where(solid, contact_solid_vertex, contact_fluid_volume).reshape(-1)
    picked = unrolled_array[target].reshape(contact_solid_vertex.shape)
    wall, near = lax.psum((picked * solid_flag, picked * owned * fluid_flag), "group")
    extra_rhs = jnp.where(
        solid, exchange_rate_factor * (near - wall), exchange_rate_factor * wall * owned
    )
    extra_diag = exchange_rate_factor * owned * fluid_flag
    rhs = (
        forcing_vector.reshape(-1)
        .at[target]
        .add(extra_rhs.reshape(-1))
        .reshape(forcing_vector.shape)
    )
    fluid_diag = (
        storage_over_step.reshape(-1)
        .at[target]
        .add(extra_diag.reshape(-1))
        .reshape(forcing_vector.shape)
    )
    shape = (rows, width, depth)
    global_row = device * rows + lax.broadcasted_iota(jnp.int32, shape, 0)
    face_x = opening_shares[0] * (global_row != first_solid * rows - 1).astype(jnp.float32)
    face_y = opening_shares[1] * open_faces(shape, 1)
    face_z = opening_shares[2] * open_faces(shape, 2)
    rims = passed_along(
        jnp.stack([face_x[-1], flow_speed[0][-1], sanction_weight[-1]]), ("group", "brick"), 1
    )
    face_low = rims[0]
    speed_low = rims[1]
    weight_low = rims[2]
    pair_low = 0.5 * (weight_low + sanction_weight[0]) * (device != first_solid).astype(jnp.float32)
    pair_up = passed_along(pair_low, "brick", -1)
    pair_y = (
        0.5 * (sanction_weight + shift_next(sanction_weight, 1)) * element_faces(shape, 1, nodes)
    )
    pair_z = (
        0.5 * (sanction_weight + shift_next(sanction_weight, 2)) * element_faces(shape, 2, nodes)
    )
    local_square = jnp.sum(rhs * rhs)
    solution = jnp.zeros_like(rhs)
    resid = rhs
    columns = []
    fluid_square, solid_square = lax.psum(
        (local_square * fluid_flag, local_square * solid_flag), ("group", "brick")
    )
    beta = jnp.sqrt(fluid_square)
    basis = [rhs / beta]
    direction = rhs
    norm_now = solid_square
    for step in range(ITERS):
        vector = jnp.where(solid, direction, basis[step])
        padded = extended(vector, ((("group", "brick"), 0),), 1)
        below = padded[0]
        above = padded[-1]

        def fluid_branch(unused):
            following = jnp.concatenate([vector[1:], above[None]], axis=0)
            flux_x = face_x * ((1.0 + flow_speed[0]) * vector - following)
            flux_low = face_low * ((1.0 + speed_low) * below - vector[0])
            out = (
                fluid_diag * vector
                + flux_x
                - jnp.concatenate([flux_low[None], flux_x[:-1]], axis=0)
            )
            flux_y = face_y * ((1.0 + flow_speed[1]) * vector - shift_next(vector, 1))
            flux_z = face_z * ((1.0 + flow_speed[2]) * vector - shift_next(vector, 2))
            return out + flux_y - shift_prev(flux_y, 1) + flux_z - shift_prev(flux_z, 2)

        def solid_branch(unused):
            out = storage_over_step * vector + diffusivity_root * stiffness_apply(
                diffusivity_root * vector, rigidity_matrix
            )
            jump_up = pair_up * (vector[-1] - above)
            jump_low = pair_low * (below - vector[0])
            out = out.at[0].add(-jump_low).at[rows - 1].add(jump_up)
            jump_y = pair_y * (vector - shift_next(vector, 1))
            jump_z = pair_z * (vector - shift_next(vector, 2))
            return out + jump_y - shift_prev(jump_y, 1) + jump_z - shift_prev(jump_z, 2)

        image = lax.cond(solid, solid_branch, fluid_branch, 0)
        inner = jnp.stack([jnp.sum(basis[j] * image) for j in range(step + 1)])
        heights, curvature = lax.psum(
            (inner * fluid_flag, jnp.sum(direction * image) * solid_flag), ("group", "brick")
        )
        fresh = image
        for j in range(step + 1):
            fresh = fresh - heights[j] * basis[j]
        alpha = norm_now / curvature
        solution = solution + alpha * direction
        resid = resid - alpha * image
        fresh_square, norm_next = lax.psum(
            (jnp.sum(fresh * fresh) * fluid_flag, jnp.sum(resid * resid) * solid_flag),
            ("group", "brick"),
        )
        length = jnp.sqrt(fresh_square)
        basis.append(fresh / length)
        columns.append(
            jnp.concatenate([heights, length[None], jnp.zeros((ITERS - 1 - step,), jnp.float32)])
        )
        direction = resid + norm_next / norm_now * direction
        norm_now = norm_next
    coeffs = least_squares(jnp.stack(columns, axis=1), beta)
    fluid_new = jnp.zeros_like(rhs)
    for step in range(ITERS):
        fluid_new = fluid_new + coeffs[step] * basis[step]
    return jnp.where(solid, solution, fluid_new)


F32 = jnp.float32
BF16 = jnp.bfloat16
MESH = pl.DeviceIdType.MESH
PIVOT_LEAST = 1e-4
REFINE_MOST = 4e-3
PARTS = 4
SIDE = ITERS + 1
RAW = {1: ITERS + 1, 2: ITERS + 2}
DEEP = (0, 1, 2, 4, 6)
SKIP = (3, 5, 7)


def iota(shape, dim):
    return lax.broadcasted_iota(jnp.int32, shape, dim)


def pieces(x):
    high = x.astype(BF16)
    return high, (x - high.astype(F32)).astype(BF16)


def total(x):
    return jnp.sum(jnp.sum(x, axis=0, keepdims=True), axis=1, keepdims=True)


def greatest(x):
    return jnp.max(jnp.max(x, axis=0, keepdims=True), axis=1, keepdims=True)


def dot(a, b, dims):
    return lax.dot_general(a, b, ((dims[0], dims[1]), ((), ())), preferred_element_type=F32)


def shift_rows(x, gamma):
    size = x.shape[0]
    after = pltpu.roll(x, size - 1, 0)
    row = iota(x.shape, 0)
    out = gamma * x + 0.5 * (pltpu.roll(x, 1, 0) + after) + jnp.where(row == 0, 0.5 * after, 0.0)
    return jnp.where(row < ITERS, out, 0.0)


def shift_lanes(x, gamma):
    size = x.shape[1]
    after = pltpu.roll(x, size - 1, 1)
    lane = iota(x.shape, 1)
    out = gamma * x + 0.5 * (pltpu.roll(x, 1, 1) + after) + jnp.where(lane == 0, 0.5 * after, 0.0)
    return jnp.where(lane < ITERS, out, 0.0)


def projected(flat, gamma, fluid):
    shape = (16, 128)
    row, lane = iota(shape, 0), iota(shape, 1)
    gram = jnp.zeros(shape, F32)
    for i in range(SIDE):
        line = flat if i == 0 else pltpu.roll(flat, 128 - SIDE * i, 1)
        gram = jnp.where((row == i) & (lane < SIDE), line, gram)
    wide = shift_lanes(gram, gamma)
    if fluid:
        normal, right = shift_rows(wide, gamma), shift_rows(gram, gamma)
    else:
        normal, right = jnp.where(row < ITERS, wide, 0.0), jnp.where(row < ITERS, gram, 0.0)
    table = jnp.where(lane < ITERS, normal, 0.0)
    table = jnp.where((lane == row + 8) & (row < ITERS), 1.0, table)
    table = jnp.where(lane == 16, pltpu.roll(right, 16, 1), table)
    margin = None
    for k in range(ITERS):
        pivot = table[k : k + 1, k : k + 1]
        spare = pivot - PIVOT_LEAST * normal[k : k + 1, k : k + 1]
        margin = spare if margin is None else jnp.minimum(margin, spare)
        scaled = table[k : k + 1, :] * (1.0 / pivot)
        column = jnp.where(row[:, :1] == k, 0.0, table[:, k : k + 1])
        table = jnp.where(row == k, scaled, table - column * scaled)
    coeffs = jnp.broadcast_to(table[:, 16:17], shape)
    inverse = jnp.where(lane < ITERS, pltpu.roll(table, shape[1] - 8, 1), 0.0)
    applied = gamma * coeffs + 0.5 * (pltpu.roll(coeffs, 1, 0) + pltpu.roll(coeffs, shape[0] - 1, 0))
    applied = applied + jnp.where(row == 1, 0.5 * pltpu.roll(coeffs, 1, 0), 0.0)
    rest = jnp.where(row == 0, 1.0, 0.0) - applied
    image = jnp.broadcast_to(jnp.sum(gram * rest, axis=0, keepdims=True), shape)
    image = shift_lanes(image, gamma) if fluid else jnp.where(lane < ITERS, image, 0.0)
    change = jnp.sum(inverse * image, axis=1, keepdims=True)
    coeffs = coeffs[:, :1] + change
    size = jnp.sum(jnp.abs(coeffs), axis=0, keepdims=True)
    moved = jnp.sum(jnp.abs(change), axis=0, keepdims=True)
    good = (margin > 0.0) & (moved < REFINE_MOST * size)
    return coeffs, jnp.where(good, 1.0, 0.0)


def ring_far(step, size):
    return min(step, size - step)


def kernel(
    groups,
    bricks,
    forcing_hbm,
    thermal_hbm,
    storage_hbm,
    opening_hbm,
    flow_hbm,
    root_hbm,
    weight_hbm,
    rigidity_hbm,
    part_hbm,
    volume_hbm,
    vertex_hbm,
    factor_hbm,
    out,
    flag,
    thermal,
    forcing,
    storage,
    opening,
    flow,
    root,
    weight,
    rigidity,
    part,
    volume,
    vertex,
    factor,
    basis,
    ax,
    gx,
    diag,
    uy,
    ly,
    uz,
    lz,
    stiff,
    uh,
    ul,
    wz,
    wxy,
    weight_low,
    weight_up,
    row_hot,
    col_hot,
    picked,
    walls,
    nears,
    gram_tile,
    near_slots,
    far_slots,
    second,
    ghost,
    ghost_diag,
    load_sem,
    halo_send,
    halo_recv,
    coef_send,
    coef_recv,
    contact_send,
    contact_recv,
    near_send,
    near_recv,
    far_send,
    far_recv,
    deep_send,
    deep_recv,
    ghost_send,
    ghost_recv,
):
    group = lax.axis_index("group")
    brick = lax.axis_index("brick")
    rows, width, depth = forcing.shape
    plane = (width, depth)
    cells = rows * width
    solid = group == groups - 1
    fluid = group != groups - 1
    inner, outer = 8, bricks // 8
    low_id = lax.rem(brick, inner)
    high_id = group * outer + brick // inner
    n_far = groups * outer
    at_top = (brick == bricks - 1) & (group >= groups - 2)
    at_bottom = (brick == 0) & ((group == 0) | (group == groups - 1))
    has_up, has_down = jnp.logical_not(at_top), jnp.logical_not(at_bottom)
    far_up = (brick == bricks - 1) & (group < groups - 2)
    far_down = (brick == 0) & (group > 0) & fluid
    device = group * bricks + brick
    up_id = lax.rem(device + 1, groups * bricks)
    down_id = lax.rem(device + groups * bricks - 1, groups * bricks)
    up = (up_id // bricks, lax.rem(up_id, bricks))
    down = (down_id // bricks, lax.rem(down_id, bricks))

    names = [
        (vertex_hbm, vertex),
        (volume_hbm, volume),
        (thermal_hbm, thermal),
        (part_hbm, part),
        (factor_hbm, factor),
        (opening_hbm, opening),
        (flow_hbm, flow),
        (storage_hbm, storage),
        (weight_hbm, weight),
        (root_hbm, root),
        (rigidity_hbm, rigidity),
        (forcing_hbm, forcing),
    ]
    loads = [pltpu.make_async_copy(s, d, load_sem.at[i]) for i, (s, d) in enumerate(names)]
    for load in loads:
        load.start()
    (l_vertex, l_volume, l_thermal, l_part, l_factor, l_opening, l_flow, l_storage, l_weight, l_root, l_rigid, l_forcing) = loads

    plane_id = brick // inner
    near_peers, far_peers = [], []
    for dz, dc in sorted(((a, b) for a in range(inner // 2) for b in range(2)), key=lambda at: -ring_far(at[0], inner // 2)):
        if dz or dc:
            peer = lax.rem(low_id // 2 + dz, inner // 2) * 2 + lax.rem(low_id + dc, 2)
            near_peers.append((peer, (group, plane_id * inner + peer)))
    steps = sorted(
        ((a, b) for a in range(groups) for b in range(outer)), key=lambda at: -ring_far(at[0], groups) - ring_far(at[1], outer)
    )
    for dx, dy in steps:
        if dx or dy:
            x_id, y_id = lax.rem(group + dx, groups), lax.rem(plane_id + dy, outer)
            far_peers.append((x_id * outer + y_id, (x_id, y_id * inner + low_id)))

    barrier = pltpu.get_barrier_semaphore()
    for peer, where in far_peers + near_peers:
        pl.semaphore_signal(barrier, inc=1, device_id=where, device_id_type=MESH)

    @pl.when(has_up)
    def _():
        pl.semaphore_signal(barrier, inc=1, device_id=up, device_id_type=MESH)

    @pl.when(has_down)
    def _():
        pl.semaphore_signal(barrier, inc=1, device_id=down, device_id_type=MESH)

    @pl.when(at_bottom)
    def _():
        for k in range(ITERS):
            basis[RAW.get(k, k), 0] = jnp.zeros(plane, F32)

    @pl.when(at_top)
    def _():
        for k in range(ITERS):
            basis[RAW.get(k, k), rows + 1] = jnp.zeros(plane, F32)

    l_vertex.wait()
    l_volume.wait()
    target = jnp.where(solid, vertex[...], volume[...])
    cell_row, cell_col = target >> 8, target & 255
    lines = target.shape[0]
    points = lines * 128
    for j in range(lines):
        span = pl.ds(j * 128, 128)
        row_hot[:, span] = jnp.where(iota((cells, 128), 0) == cell_row[j : j + 1], 1.0, 0.0).astype(BF16)
        col_hot[:, span] = jnp.where(iota((depth, 128), 0) == cell_col[j : j + 1], 1.0, 0.0).astype(BF16)
    l_thermal.wait()
    high, low = pieces(thermal[...].reshape(cells, depth))
    hot = row_hot[...]
    found = dot(high, hot, ((0,), (0,))) + dot(low, hot, ((0,), (0,)))
    value = jnp.sum(found * col_hot[...].astype(F32), axis=0, keepdims=True)
    value = jnp.concatenate([value[:, j * 128 : (j + 1) * 128] for j in range(lines)], axis=0)
    l_part.wait()
    l_factor.wait()
    owned = jnp.where(part[...] == group, 1.0, 0.0)
    picked[0:lines] = jnp.where(solid, value, value * owned)
    picked[lines:] = jnp.zeros((8 - lines, 128), F32)

    pl.semaphore_wait(barrier, inner - 1 + n_far - 1 + has_up.astype(jnp.int32) + has_down.astype(jnp.int32))

    def wall_copy(g):
        return pltpu.make_async_remote_copy(
            picked, walls, contact_send.at[g], contact_recv.at[groups - 1], device_id=(g, brick), device_id_type=MESH
        )

    near_copy = pltpu.make_async_remote_copy(
        picked, nears.at[group], contact_send.at[0], contact_recv.at[group], device_id=(groups - 1, brick), device_id_type=MESH
    )

    @pl.when(solid)
    def _():
        for g in range(groups - 1):
            wall_copy(g).start()

    @pl.when(fluid)
    def _():
        near_copy.start()

    l_opening.wait()
    l_flow.wait()
    l_weight.wait()
    coef_a = pltpu.make_async_remote_copy(
        ax.at[rows], ax.at[0], coef_send.at[0], coef_recv.at[0], device_id=up, device_id_type=MESH
    )
    coef_g = pltpu.make_async_remote_copy(
        gx.at[rows], gx.at[0], coef_send.at[1], coef_recv.at[1], device_id=up, device_id_type=MESH
    )
    coef_up = pltpu.make_async_remote_copy(
        weight.at[rows - 1], weight_low, coef_send.at[0], coef_recv.at[0], device_id=up, device_id_type=MESH
    )
    coef_down = pltpu.make_async_remote_copy(
        weight.at[0], weight_up, coef_send.at[1], coef_recv.at[1], device_id=down, device_id_type=MESH
    )

    @pl.when(fluid)
    def _():
        last = jnp.where(at_top, 0.0, opening[0, rows - 1])
        ax[rows] = last
        gx[rows] = last * (1.0 + flow[0, rows - 1])

    @pl.when(fluid & has_up)
    def _():
        coef_a.start()
        coef_g.start()

    @pl.when(solid & has_up)
    def _():
        coef_up.start()

    @pl.when(solid & has_down)
    def _():
        coef_down.start()

    l_storage.wait()
    l_root.wait()
    l_rigid.wait()

    def spread(values):
        flat = jnp.concatenate([values[j : j + 1] for j in range(lines)], axis=1)
        high, low = pieces(flat)
        cols = col_hot[...].astype(F32)
        return dot(row_hot[...], (cols * high.astype(F32)).astype(BF16), ((1,), (1,))) + dot(
            row_hot[...], (cols * low.astype(F32)).astype(BF16), ((1,), (1,))
        )

    def fold(x, op):
        y = x.reshape(width // 8, 8, depth)
        return op(y, axis=0)

    y_at, z_at = iota(plane, 0), iota(plane, 1)

    def write_stats(d_max, d_min, o_sum):
        lane = iota((1, 128), 1)
        tile = jnp.where(lane == 0, greatest(d_max), jnp.where(lane == 1, greatest(-d_min), jnp.where(lane == 2, total(o_sum), 0.0)))
        near_slots[0, low_id] = tile

    start = (jnp.full((8, depth), -1e30, F32), jnp.full((8, depth), 1e30, F32), jnp.zeros((8, depth), F32))

    @pl.when(fluid)
    def _():
        extra = spread(factor[...] * owned).reshape(rows, width, depth)
        storage[...] = storage[...] + extra

        def second(r, carry):
            d_max, d_min, o_sum = carry
            a_y = jnp.where(y_at == width - 1, 0.0, opening[1, r])
            g_y = a_y * (1.0 + flow[1, r])
            g_low = pltpu.roll(g_y, 1, 0)
            uy[r] = a_y
            ly[r] = g_low
            a_x = jnp.where(at_top & (r == rows - 1), 0.0, opening[0, r])
            g_x = a_x * (1.0 + flow[0, r])

            @pl.when(r < rows - 1)
            def _():
                ax[r + 1] = a_x
                gx[r + 1] = g_x

            d = storage[r] + g_x + g_y + pltpu.roll(a_y, 1, 0)
            o = a_x + g_x + a_y + g_low
            a_z = jnp.where(z_at == depth - 1, 0.0, opening[2, r])
            g_z = a_z * (1.0 + flow[2, r])
            g_low = pltpu.roll(g_z, 1, 1)
            uz[r] = a_z
            lz[r] = g_low
            d = d + g_z + pltpu.roll(a_z, 1, 1)
            o = o + a_z + g_low
            d = d + jnp.where(r == 0, 0.0, opening[0, jnp.maximum(r - 1, 0)])
            diag[r] = d
            return jnp.maximum(d_max, fold(d, jnp.max)), jnp.minimum(d_min, fold(d, jnp.min)), o_sum + fold(o, jnp.sum)

        write_stats(*lax.fori_loop(0, rows, second, start))

    @pl.when(solid)
    def _():
        eye = iota((8, 8), 0) == iota((8, 8), 1)
        both = rigidity[0] + rigidity[1] + rigidity[2]
        size = jnp.abs(rigidity[0]) + jnp.abs(rigidity[1]) + jnp.abs(rigidity[2])
        trace = total(jnp.where(eye, both, 0.0)) * (1.0 / 8)
        off = total(jnp.where(eye, 0.0, size)) * (1.0 / 8)
        block_z = jnp.where(iota((8, depth), 1) % 8 == iota((8, depth), 0), 1.0, 0.0)
        spread_z = lax.dot_general(
            lax.dot_general(block_z, rigidity[2], (((0,), (1,)), ((), ())), precision=HIGH, preferred_element_type=F32),
            block_z,
            (((1,), (0,)), ((), ())),
            precision=HIGH,
            preferred_element_type=F32,
        )
        same = (iota((depth, depth), 0) // 8) == (iota((depth, depth), 1) // 8)
        high, low = pieces(jnp.where(same, spread_z, 0.0))
        wz[0], wz[1] = high, low
        outer_x = jnp.where(iota((8, 64), 1) // 8 == iota((8, 64), 0), 1.0, 0.0)
        inner_y = jnp.where(iota((8, 64), 1) % 8 == iota((8, 64), 0), 1.0, 0.0)

        def expand(matrix, hot):
            left = lax.dot_general(hot, matrix, (((0,), (0,)), ((), ())), precision=HIGH, preferred_element_type=F32)
            return lax.dot_general(left, hot, (((1,), (0,)), ((), ())), precision=HIGH, preferred_element_type=F32)

        same_y = iota((64, 64), 0) % 8 == iota((64, 64), 1) % 8
        same_x = iota((64, 64), 0) // 8 == iota((64, 64), 1) // 8
        mixed = jnp.where(same_y, expand(rigidity[0], outer_x), 0.0) + jnp.where(same_x, expand(rigidity[1], inner_y), 0.0)
        high, low = pieces(mixed)
        wxy[...] = jnp.concatenate([high, high, low], axis=1)

        def second(r, carry):
            d_max, d_min, o_sum = carry
            w = weight[r]
            b_y = jnp.where((y_at % 8 == 7) & (y_at < width - 1), 0.5 * (w + pltpu.roll(w, width - 1, 0)), 0.0)
            b_low = pltpu.roll(b_y, 1, 0)
            uy[r] = b_y
            ly[r] = b_low
            pair = b_y + b_low
            b_z = jnp.where((z_at % 8 == 7) & (z_at < depth - 1), 0.5 * (w + pltpu.roll(w, depth - 1, 1)), 0.0)
            b_low = pltpu.roll(b_z, 1, 1)
            uz[r] = b_z
            lz[r] = b_low
            pair = pair + b_z + b_low
            d = storage[r] + pair
            diag[r] = d
            square = root[r] * root[r]
            whole = d + square * trace
            o = pair + square * off
            return jnp.maximum(d_max, fold(whole, jnp.max)), jnp.minimum(d_min, fold(whole, jnp.min)), o_sum + fold(o, jnp.sum)

        write_stats(*lax.fori_loop(0, rows, second, start))

    def near_start(which):
        for o, (peer, where) in enumerate(near_peers):
            pltpu.make_async_remote_copy(
                near_slots.at[which, low_id],
                near_slots.at[which, low_id],
                near_send.at[which, o],
                near_recv.at[which, low_id],
                device_id=where,
                device_id_type=MESH,
            ).start()

    def near_wait(which):
        for o, (peer, where) in enumerate(near_peers):
            copy = pltpu.make_async_remote_copy(
                near_slots.at[which, peer],
                near_slots.at[which, peer],
                near_send.at[which, o],
                near_recv.at[which, peer],
                device_id=where,
                device_id_type=MESH,
            )
            copy.wait_recv()
            copy.wait_send()

    def far_start(which):
        for o, (peer, where) in enumerate(far_peers):
            pltpu.make_async_remote_copy(
                far_slots.at[which, high_id],
                far_slots.at[which, high_id],
                far_send.at[which, o],
                far_recv.at[which, high_id],
                device_id=where,
                device_id_type=MESH,
            ).start()

    def far_wait(which):
        for o, (peer, where) in enumerate(far_peers):
            copy = pltpu.make_async_remote_copy(
                far_slots.at[which, peer],
                far_slots.at[which, peer],
                far_send.at[which, o],
                far_recv.at[which, peer],
                device_id=where,
                device_id_type=MESH,
            )
            copy.wait_recv()
            copy.wait_send()

    def merge_stats(tiles):
        lane = iota((1, 128), 1)
        most, summed = tiles[0], tiles[0]
        for tile in tiles[1:]:
            most, summed = jnp.maximum(most, tile), summed + tile
        return jnp.where(lane == 2, summed, most)

    near_start(0)

    l_forcing.wait()

    part_rows = width // PARTS

    def halo_up(k, j):
        span = pl.ds(j * part_rows, part_rows)
        at = RAW.get(k, k)
        return pltpu.make_async_remote_copy(
            basis.at[at, rows, span],
            basis.at[at, 0, span],
            halo_send.at[k, 0, j],
            halo_recv.at[k, 0, j],
            device_id=up,
            device_id_type=MESH,
        )

    def halo_down(k, j):
        span = pl.ds(j * part_rows, part_rows)
        at = RAW.get(k, k)
        return pltpu.make_async_remote_copy(
            basis.at[at, 1, span],
            basis.at[at, rows + 1, span],
            halo_send.at[k, 1, j],
            halo_recv.at[k, 1, j],
            device_id=down,
            device_id_type=MESH,
        )

    def linked(k):
        if k in SKIP:
            return has_up & jnp.logical_not(far_up), has_down & jnp.logical_not(far_down)
        return has_up, has_down

    def send_halos(k, j):
        to_up, to_down = linked(k)

        @pl.when(to_up)
        def _():
            halo_up(k, j).start()

        @pl.when(to_down)
        def _():
            halo_down(k, j).start()

    def deep_up(i):
        return pltpu.make_async_remote_copy(
            basis.at[RAW.get(DEEP[i], DEEP[i]), rows - 1], second.at[0, i], deep_send.at[i, 0], deep_recv.at[i, 0], device_id=up, device_id_type=MESH
        )

    def deep_down(i):
        return pltpu.make_async_remote_copy(
            basis.at[RAW.get(DEEP[i], DEEP[i]), 2], second.at[1, i], deep_send.at[i, 1], deep_recv.at[i, 1], device_id=down, device_id_type=MESH
        )

    def ghost_up(i):
        source = (ghost_diag.at[0], uy.at[rows - 1], ly.at[rows - 1], uz.at[rows - 1], lz.at[rows - 1], gx.at[rows - 1])[i]
        return pltpu.make_async_remote_copy(
            source, ghost.at[0, i], ghost_send.at[0, i], ghost_recv.at[0, i], device_id=up, device_id_type=MESH
        )

    def ghost_down(i):
        source = (ghost_diag.at[1], uy.at[0], ly.at[0], uz.at[0], lz.at[0], ax.at[1])[i]
        return pltpu.make_async_remote_copy(
            source, ghost.at[1, i], ghost_send.at[1, i], ghost_recv.at[1, i], device_id=down, device_id_type=MESH
        )

    def send_deep(i):
        @pl.when(far_up)
        def _():
            deep_up(i).start()

        @pl.when(far_down)
        def _():
            deep_down(i).start()

    @pl.when(fluid)
    def _():
        pltpu.make_async_remote_copy(
            picked, walls, contact_send.at[0], contact_recv.at[groups - 1], device_id=(groups - 1, brick), device_id_type=MESH
        ).wait_recv()

    @pl.when(solid)
    def _():
        for g in range(groups - 1):
            pltpu.make_async_remote_copy(
                picked, nears.at[g], contact_send.at[g], contact_recv.at[g], device_id=(g, brick), device_id_type=MESH
            ).wait_recv()
        walls[...] = nears[0] + nears[1] + nears[2] - picked[...]

    heat = factor[...] * walls[0:lines]
    extra = spread(jnp.where(solid, heat, heat * owned)).reshape(rows, width, depth)
    basis[0, 1 : rows + 1] = forcing[...] + extra
    for j in range(PARTS):
        send_halos(0, j)
    send_deep(0)

    @pl.when(at_bottom)
    def _():
        gx[0] = jnp.zeros(plane, F32)

    @pl.when(fluid & has_down)
    def _():
        coef_a.wait_recv()
        coef_g.wait_recv()
        diag[0] = diag[0] + ax[0]

    @pl.when(solid & has_down)
    def _():
        coef_up.wait_recv()
        gx[0] = 0.5 * (weight_low[...] + weight[0])
        diag[0] = diag[0] + gx[0]

    @pl.when(solid & has_up)
    def _():
        coef_down.wait_recv()
        ax[rows] = 0.5 * (weight[rows - 1] + weight_up[...])
        diag[rows - 1] = diag[rows - 1] + ax[rows]

    @pl.when(solid & at_top)
    def _():
        ax[rows] = jnp.zeros(plane, F32)

    def gram_row(k):
        def body(r, accs):
            accs = list(accs)
            for j in range(width // 8):
                span = slice(8 * j, 8 * j + 8)
                mine = basis[k, r + 1, span, :]
                for i in range(k + 1):
                    other = mine if i == k else basis[i, r + 1, span, :]
                    accs[i] = accs[i] + mine * other
            return tuple(accs)

        accs = lax.fori_loop(0, rows, body, tuple(jnp.zeros((8, depth), F32) for _ in range(k + 1)))
        lane = iota((1, 128), 1)
        tile = jnp.zeros((1, 128), F32) if k == 0 else gram_tile[...]
        for i in range(k + 1):
            spot = (lane == i * SIDE + k) | (lane == k * SIDE + i)
            tile = jnp.where(spot, total(accs[i]), tile)
        gram_tile[...] = tile

    def local(r, v):
        return (
            diag[r] * v
            - uy[r] * pltpu.roll(v, width - 1, 0)
            - ly[r] * pltpu.roll(v, 1, 0)
            - uz[r] * pltpu.roll(v, depth - 1, 1)
            - lz[r] * pltpu.roll(v, 1, 1)
        )

    def apply(k, scale):
        at, to = (RAW.get(k, k), RAW[k + 1]) if scale is None else (k, k + 1)

        def keep(r, q):
            if scale is None:
                basis[to, r + 1] = q
            else:
                basis[to, r + 1] = scale * q - basis[k - 1, r + 1]

        @pl.when(fluid)
        def _():
            def middle(r, carry):
                v = basis[at, r + 1]
                keep(r, local(r, v) - gx[r] * basis[at, r] - ax[r + 1] * basis[at, r + 2])
                return carry

            keep(0, local(0, basis[at, 1]) - ax[1] * basis[at, 2])
            keep(rows - 1, local(rows - 1, basis[at, rows]) - gx[rows - 1] * basis[at, rows - 1])
            lax.fori_loop(1, rows - 1, middle, 0)

        @pl.when(solid)
        def _():
            for e in range(width // 8):
                u = (root[:, 8 * e : 8 * e + 8, :] * basis[at, 1 : rows + 1, 8 * e : 8 * e + 8, :]).reshape(64, depth)
                high, low = pieces(u)
                uh[e], ul[e] = high, low
                stiff[e] = dot(wxy[...], jnp.concatenate([high, low, high], axis=0), ((1,), (0,)))
            high, low = uh[...].reshape(cells, depth), ul[...].reshape(cells, depth)
            along = dot(high, wz[0], ((1,), (0,))) + dot(low, wz[0], ((1,), (0,))) + dot(high, wz[1], ((1,), (0,)))
            stiff[...] = stiff[...] + along.reshape(width // 8, 64, depth)

            def each(r, carry):
                force = stiff[:, pl.ds(r * 8, 8), :].reshape(width, depth)
                keep(r, local(r, basis[at, r + 1]) + root[r] * force)
                return carry

            lax.fori_loop(0, rows, each, 0)

    def finish(k, scale, mix=None):
        at, to = RAW.get(k, k), (RAW[k + 1] if scale is None else k + 1)
        for j in range(PARTS):
            span = slice(j * part_rows, (j + 1) * part_rows)

            from_up, from_down = linked(k)

            @pl.when(from_down)
            def _():
                halo_up(k, j).wait_recv()

            @pl.when(from_up)
            def _():
                halo_down(k, j).wait_recv()

            for own, halo, coef in ((1, 0, gx.at[0]), (rows, rows + 1, ax.at[rows])):
                value = basis[at, halo, span]
                if mix is not None:
                    value = mix[0] * value + mix[1] * basis[RAW[1], halo, span] + mix[2] * basis[0, halo, span]
                    basis[k, halo, span] = value
                value = coef[span] * value
                if scale is not None:
                    value = scale * value
                basis[to, own, span] = basis[to, own, span] - value
            if k + 1 < ITERS:
                send_halos(k + 1, j)

    def extend(i):
        k = DEEP[i]
        fresh = range(i + 1) if k == 2 else (i,)

        def row(side, near, halo, inward):
            v = basis[k, halo]
            if k == 2:
                outer_row = mix[0] * second[side, 2] + mix[1] * second[side, 1] + mix[2] * second[side, 0]
                older = (basis[RAW[1], halo] - center * basis[0, halo]) * inv_e
            else:
                outer_row, older = second[side, i], basis[k - 1, halo]
            q = (
                (ghost[side, 0] - center) * v
                - ghost[side, 1] * pltpu.roll(v, width - 1, 0)
                - ghost[side, 2] * pltpu.roll(v, 1, 0)
                - ghost[side, 3] * pltpu.roll(v, depth - 1, 1)
                - ghost[side, 4] * pltpu.roll(v, 1, 1)
                - ghost[side, 5] * outer_row
                - inward * basis[k, near]
            )
            basis[k + 1, halo] = scale * q - older

        @pl.when(far_down)
        def _():
            for n in fresh:
                deep_up(n).wait_recv()
            if k == 2:
                for n in range(6):
                    ghost_up(n).wait_recv()
            row(0, 1, 0, ax[0])

        @pl.when(far_up)
        def _():
            for n in fresh:
                deep_down(n).wait_recv()
            if k == 2:
                for n in range(6):
                    ghost_down(n).wait_recv()
            row(1, rows, rows + 1, gx[rows])

    apply(0, None)
    send_deep(1)
    near_wait(0)
    far_slots[0, high_id] = merge_stats([near_slots[0, i] for i in range(inner)])
    far_start(0)
    finish(0, None)

    @pl.when(far_up)
    def _():
        ghost_diag[0] = diag[rows - 1]
        for n in range(6):
            ghost_up(n).start()

    @pl.when(far_down)
    def _():
        ghost_diag[1] = diag[0]
        for n in range(6):
            ghost_down(n).start()

    apply(1, None)
    send_deep(2)
    gram_row(0)
    finish(1, None)
    far_wait(0)
    split = (groups - 1) * outer

    def interval(tiles, count, of_most, of_mean):
        stats = merge_stats(tiles)
        mean = stats[0:1, 2:3] * (1.0 / count)
        high = of_most * stats[0:1, 0:1] + of_mean * mean
        low = jnp.maximum(-stats[0:1, 1:2] - 0.5 * mean, 0.0)
        return 0.5 * (high + low), 0.5 * (high - low)

    c_fluid, e_fluid = interval([far_slots[0, i] for i in range(split)], float((groups - 1) * bricks * cells * depth), 0.9, 0.1)
    c_solid, e_solid = interval([far_slots[0, i] for i in range(split, n_far)], float(bricks * cells * depth), 0.97, 0.25)
    center = jnp.where(solid, c_solid, c_fluid)
    inv_e = 1.0 / jnp.where(solid, e_solid, e_fluid)
    scale = 2.0 * inv_e

    mix = (scale * inv_e, -2.0 * scale * center * inv_e, scale * inv_e * center * center - 1.0)

    def convert(r, carry):
        zero, one, two = basis[0, r + 1], basis[RAW[1], r + 1], basis[RAW[2], r + 1]
        basis[1, r + 1] = (one - center * zero) * inv_e
        basis[2, r + 1] = mix[0] * two + mix[1] * one + mix[2] * zero
        diag[r] = diag[r] - center
        return carry

    lax.fori_loop(0, rows, convert, 0)
    for k in range(2, ITERS):
        apply(k, scale)
        if k + 1 in DEEP:
            send_deep(DEEP.index(k + 1))
        if k == 2:
            gram_row(1)
        gram_row(k)
        finish(k, scale, mix if k == 2 else None)
        if k + 1 in SKIP:
            extend(DEEP.index(k))
    gram_row(ITERS)

    near_slots[1, low_id] = gram_tile[...]
    near_start(1)
    near_wait(1)
    summed = near_slots[1, 0]
    for i in range(1, inner):
        summed = summed + near_slots[1, i]
    far_slots[1, high_id] = summed
    far_start(1)
    far_wait(1)
    gram_fluid = far_slots[1, 0]
    for i in range(1, split):
        gram_fluid = gram_fluid + far_slots[1, i]
    gram_solid = far_slots[1, split]
    for i in range(split + 1, n_far):
        gram_solid = gram_solid + far_slots[1, i]
    y_fluid, ok_fluid = projected(gram_fluid, c_fluid / e_fluid, True)
    y_solid, ok_solid = projected(gram_solid, c_solid / e_solid, False)
    coeffs = jnp.where(solid, y_solid, y_fluid) * inv_e
    flag[0] = jnp.max(ok_fluid * ok_solid).astype(jnp.int32)
    weights = [coeffs[k : k + 1, :1] for k in range(ITERS)]

    def combine(r, carry):
        acc = weights[0] * basis[0, r + 1]
        for k in range(1, ITERS):
            acc = acc + weights[k] * basis[k, r + 1]
        out[r] = acc
        return carry

    lax.fori_loop(0, rows, combine, 0)

    @pl.when(solid)
    def _():
        for g in range(groups - 1):
            wall_copy(g).wait_send()

    @pl.when(fluid)
    def _():
        near_copy.wait_send()

    @pl.when(fluid & has_up)
    def _():
        coef_a.wait_send()
        coef_g.wait_send()

    @pl.when(solid & has_up)
    def _():
        coef_up.wait_send()

    @pl.when(solid & has_down)
    def _():
        coef_down.wait_send()

    @pl.when(far_up)
    def _():
        for n in range(6):
            ghost_up(n).wait_send()
        for i in range(len(DEEP)):
            deep_up(i).wait_send()

    @pl.when(far_down)
    def _():
        for n in range(6):
            ghost_down(n).wait_send()
        for i in range(len(DEEP)):
            deep_down(i).wait_send()

    for k in range(ITERS):
        sent_up, sent_down = linked(k)
        for j in range(PARTS):

            @pl.when(sent_up)
            def _():
                halo_up(k, j).wait_send()

            @pl.when(sent_down)
            def _():
                halo_down(k, j).wait_send()


def handed_on(result):
    def body(source, target, sem):
        copy = pltpu.make_async_copy(source, target, sem)
        copy.start()
        copy.wait()

    return pl.pallas_call(
        body,
        out_shape=jax.ShapeDtypeStruct(result.shape, result.dtype),
        in_specs=[pl.BlockSpec(memory_space=pltpu.VMEM)],
        out_specs=pl.BlockSpec(memory_space=pl.ANY),
        scratch_shapes=[pltpu.SemaphoreType.DMA],
        name="handed_on",
    )(pltpu.with_memory_space_constraint(result, pltpu.VMEM))


def shards(*arguments):
    groups, bricks = lax.axis_size("group"), lax.axis_size("brick")
    forcing = arguments[0]
    rows, width, depth = slab = forcing.shape
    lines = arguments[8].shape[0]
    points = lines * 128
    n_far = groups * (bricks // 8)
    vm = pltpu.VMEM
    scratch = (
        [vm(slab, F32)] * 3
        + [vm((3,) + slab, F32)] * 2
        + [vm(slab, F32)] * 2
        + [vm((3, 8, 8), F32)]
        + [vm((lines, 128), jnp.int32)] * 3
        + [vm((lines, 128), F32)]
        + [vm((ITERS + 3, rows + 2, width, depth), F32)]
        + [vm((rows + 1, width, depth), F32)] * 2
        + [vm(slab, F32)] * 5
        + [vm((width // 8, 64, depth), F32)]
        + [vm((width // 8, 64, depth), BF16)] * 2
        + [vm((2, depth, depth), BF16), vm((64, 192), BF16)]
        + [vm((width, depth), F32)] * 2
        + [vm((rows * width, points), BF16), vm((depth, points), BF16)]
        + [vm((8, 128), F32)] * 2
        + [vm((groups - 1, 8, 128), F32)]
        + [vm((1, 128), F32), vm((2, 8, 1, 128), F32), vm((2, n_far, 1, 128), F32)]
        + [vm((2, len(DEEP), width, depth), F32), vm((2, 6, width, depth), F32), vm((2, width, depth), F32)]
    )
    dma = pltpu.SemaphoreType.DMA
    semaphores = [
        dma((12,)),
        dma((ITERS, 2, PARTS)),
        dma((ITERS, 2, PARTS)),
        dma((2,)),
        dma((2,)),
        dma((groups,)),
        dma((groups,)),
        dma((2, 8)),
        dma((2, 8)),
        dma((2, n_far)),
        dma((2, n_far)),
        dma((len(DEEP), 2)),
        dma((len(DEEP), 2)),
        dma((2, 6)),
        dma((2, 6)),
    ]
    result, flag = pl.pallas_call(
        functools.partial(kernel, groups, bricks),
        out_shape=(pltpu.VMEM(slab, F32), jax.ShapeDtypeStruct((1,), jnp.int32)),
        in_specs=[pl.BlockSpec(memory_space=pl.ANY)] * 12,
        out_specs=(pl.BlockSpec(memory_space=pltpu.VMEM), pl.BlockSpec(memory_space=pltpu.SMEM)),
        scratch_shapes=scratch + semaphores,
        compiler_params=pltpu.CompilerParams(collective_id=0, has_side_effects=True, vmem_limit_bytes=56 * 2**20),
        name="coupled",
    )(*arguments)
    return lax.cond(flag[0] > 0, lambda: handed_on(result), lambda: iterated(*arguments))


def solution(mesh):
    return jax.shard_map(
        shards,
        mesh=mesh,
        in_specs=(
            P(("group", "brick"), None, None),
            P(("group", "brick"), None, None),
            P(("group", "brick"), None, None),
            P(None, ("group", "brick"), None, None),
            P(None, ("group", "brick"), None, None),
            P(("group", "brick"), None, None),
            P(("group", "brick"), None, None),
            P(),
            P("brick", None),
            P("brick", None),
            P("brick", None),
            P("brick", None),
        ),
        out_specs=P(("group", "brick"), None, None),
        check_vma=False,
    )
```

```python
import functools

import jax
import jax.numpy as jnp
from jax import lax
from jax.experimental import pallas as pl
from jax.experimental.pallas import tpu as pltpu
from jax.sharding import PartitionSpec as P

ITERS = 8


HIGH = lax.Precision.HIGHEST


def passed_along(value, axis, steps):
    count = lax.axis_size(axis)
    leading, last = (max(0, -steps), min(count, count - steps))
    return lax.ppermute(value, axis, [(source, source + steps) for source in range(leading, last)])


def extended(cells, sides, width):
    for axis, dim in sides:
        count = lax.axis_size(axis)
        ends = count - 1
        head = lax.slice_in_dim(cells, 0, width, axis=dim)
        tail = lax.slice_in_dim(cells, cells.shape[dim] - width, cells.shape[dim], axis=dim)
        cells = jnp.concatenate(
            [
                lax.ppermute(tail, axis, [(i, (i + 1) % count) for i in range(ends)]),
                cells,
                lax.ppermute(head, axis, [((i + 1) % count, i) for i in range(ends)]),
            ],
            axis=dim,
        )
    return cells


def shift_next(v, axis):
    size = v.shape[axis]
    inner = lax.slice_in_dim(v, 1, size, axis=axis)
    zero = jnp.zeros_like(lax.slice_in_dim(v, 0, 1, axis=axis))
    return jnp.concatenate([inner, zero], axis=axis)


def shift_prev(v, axis):
    size = v.shape[axis]
    inner = lax.slice_in_dim(v, 0, size - 1, axis=axis)
    zero = jnp.zeros_like(lax.slice_in_dim(v, 0, 1, axis=axis))
    return jnp.concatenate([zero, inner], axis=axis)


def open_faces(shape, axis):
    index = lax.broadcasted_iota(jnp.int32, shape, axis)
    return (index < shape[axis] - 1).astype(jnp.float32)


def element_faces(shape, axis, nodes):
    index = lax.broadcasted_iota(jnp.int32, shape, axis)
    inside = (index % nodes == nodes - 1) & (index < shape[axis] - 1)
    return inside.astype(jnp.float32)


def stiffness_apply(u, rigidity_matrix):
    nodes = rigidity_matrix.shape[1]
    rows, width, depth = u.shape
    block = min(depth, 128)
    along_x = jnp.einsum("pq,qyz->pyz", rigidity_matrix[0], u, precision=HIGH)
    split_y = u.reshape(rows, width // nodes, nodes, depth)
    along_y = jnp.einsum("pq,xeqz->xepz", rigidity_matrix[1], split_y, precision=HIGH).reshape(
        rows, width, depth
    )
    wide = jnp.kron(jnp.eye(block // nodes, dtype=jnp.float32), rigidity_matrix[2])
    split_z = u.reshape(rows, width, depth // block, block)
    along_z = jnp.einsum("xyeq,pq->xyep", split_z, wide, precision=HIGH).reshape(rows, width, depth)
    return along_x + along_y + along_z


def least_squares(hess, beta):
    gram = jnp.dot(hess.T, hess, precision=HIGH)
    lower = jnp.linalg.cholesky(gram)
    right = (beta * hess[0])[:, None]
    middle = lax.linalg.triangular_solve(lower, right, left_side=True, lower=True)
    coeffs = lax.linalg.triangular_solve(
        lower, middle, left_side=True, lower=True, transpose_a=True
    )
    return coeffs[:, 0]


def iterated(
    forcing_vector,
    thermal_iterate,
    storage_over_step,
    opening_shares,
    flow_speed,
    diffusivity_root,
    sanction_weight,
    rigidity_matrix,
    contact_fluid_part,
    contact_fluid_volume,
    contact_solid_vertex,
    exchange_rate_factor,
):
    groups = lax.axis_size("group")
    bricks = lax.axis_size("brick")
    group_id = lax.axis_index("group")
    brick_id = lax.axis_index("brick")
    solid = group_id == groups - 1
    solid_flag = solid.astype(jnp.float32)
    fluid_flag = 1.0 - solid_flag
    rows, width, depth = forcing_vector.shape
    nodes = rigidity_matrix.shape[1]
    device = group_id * bricks + brick_id
    first_solid = (groups - 1) * bricks
    unrolled_array = thermal_iterate.reshape(-1)
    owned = (contact_fluid_part == group_id).astype(jnp.float32)
    target = jnp.where(solid, contact_solid_vertex, contact_fluid_volume).reshape(-1)
    picked = unrolled_array[target].reshape(contact_solid_vertex.shape)
    wall, near = lax.psum((picked * solid_flag, picked * owned * fluid_flag), "group")
    extra_rhs = jnp.where(
        solid, exchange_rate_factor * (near - wall), exchange_rate_factor * wall * owned
    )
    extra_diag = exchange_rate_factor * owned * fluid_flag
    rhs = (
        forcing_vector.reshape(-1)
        .at[target]
        .add(extra_rhs.reshape(-1))
        .reshape(forcing_vector.shape)
    )
    fluid_diag = (
        storage_over_step.reshape(-1)
        .at[target]
        .add(extra_diag.reshape(-1))
        .reshape(forcing_vector.shape)
    )
    shape = (rows, width, depth)
    global_row = device * rows + lax.broadcasted_iota(jnp.int32, shape, 0)
    face_x = opening_shares[0] * (global_row != first_solid * rows - 1).astype(jnp.float32)
    face_y = opening_shares[1] * open_faces(shape, 1)
    face_z = opening_shares[2] * open_faces(shape, 2)
    rims = passed_along(
        jnp.stack([face_x[-1], flow_speed[0][-1], sanction_weight[-1]]), ("group", "brick"), 1
    )
    face_low = rims[0]
    speed_low = rims[1]
    weight_low = rims[2]
    pair_low = 0.5 * (weight_low + sanction_weight[0]) * (device != first_solid).astype(jnp.float32)
    pair_up = passed_along(pair_low, "brick", -1)
    pair_y = (
        0.5 * (sanction_weight + shift_next(sanction_weight, 1)) * element_faces(shape, 1, nodes)
    )
    pair_z = (
        0.5 * (sanction_weight + shift_next(sanction_weight, 2)) * element_faces(shape, 2, nodes)
    )
    local_square = jnp.sum(rhs * rhs)
    solution = jnp.zeros_like(rhs)
    resid = rhs
    columns = []
    fluid_square, solid_square = lax.psum(
        (local_square * fluid_flag, local_square * solid_flag), ("group", "brick")
    )
    beta = jnp.sqrt(fluid_square)
    basis = [rhs / beta]
    direction = rhs
    norm_now = solid_square
    for step in range(ITERS):
        vector = jnp.where(solid, direction, basis[step])
        padded = extended(vector, ((("group", "brick"), 0),), 1)
        below = padded[0]
        above = padded[-1]

        def fluid_branch(unused):
            following = jnp.concatenate([vector[1:], above[None]], axis=0)
            flux_x = face_x * ((1.0 + flow_speed[0]) * vector - following)
            flux_low = face_low * ((1.0 + speed_low) * below - vector[0])
            out = (
                fluid_diag * vector
                + flux_x
                - jnp.concatenate([flux_low[None], flux_x[:-1]], axis=0)
            )
            flux_y = face_y * ((1.0 + flow_speed[1]) * vector - shift_next(vector, 1))
            flux_z = face_z * ((1.0 + flow_speed[2]) * vector - shift_next(vector, 2))
            return out + flux_y - shift_prev(flux_y, 1) + flux_z - shift_prev(flux_z, 2)

        def solid_branch(unused):
            out = storage_over_step * vector + diffusivity_root * stiffness_apply(
                diffusivity_root * vector, rigidity_matrix
            )
            jump_up = pair_up * (vector[-1] - above)
            jump_low = pair_low * (below - vector[0])
            out = out.at[0].add(-jump_low).at[rows - 1].add(jump_up)
            jump_y = pair_y * (vector - shift_next(vector, 1))
            jump_z = pair_z * (vector - shift_next(vector, 2))
            return out + jump_y - shift_prev(jump_y, 1) + jump_z - shift_prev(jump_z, 2)

        image = lax.cond(solid, solid_branch, fluid_branch, 0)
        inner = jnp.stack([jnp.sum(basis[j] * image) for j in range(step + 1)])
        heights, curvature = lax.psum(
            (inner * fluid_flag, jnp.sum(direction * image) * solid_flag), ("group", "brick")
        )
        fresh = image
        for j in range(step + 1):
            fresh = fresh - heights[j] * basis[j]
        alpha = norm_now / curvature
        solution = solution + alpha * direction
        resid = resid - alpha * image
        fresh_square, norm_next = lax.psum(
            (jnp.sum(fresh * fresh) * fluid_flag, jnp.sum(resid * resid) * solid_flag),
            ("group", "brick"),
        )
        length = jnp.sqrt(fresh_square)
        basis.append(fresh / length)
        columns.append(
            jnp.concatenate([heights, length[None], jnp.zeros((ITERS - 1 - step,), jnp.float32)])
        )
        direction = resid + norm_next / norm_now * direction
        norm_now = norm_next
    coeffs = least_squares(jnp.stack(columns, axis=1), beta)
    fluid_new = jnp.zeros_like(rhs)
    for step in range(ITERS):
        fluid_new = fluid_new + coeffs[step] * basis[step]
    return jnp.where(solid, solution, fluid_new)


F32 = jnp.float32
BF16 = jnp.bfloat16
MESH = pl.DeviceIdType.MESH
PIVOT_LEAST = 1e-4
REFINE_MOST = 4e-3
PARTS = 4
SIDE = ITERS + 1
RAW = {1: ITERS + 1, 2: ITERS + 2}
DEEP = (0, 1, 2, 4, 6)
SKIP = (3, 5, 7)


def iota(shape, dim):
    return lax.broadcasted_iota(jnp.int32, shape, dim)


def pieces(x):
    high = x.astype(BF16)
    return high, (x - high.astype(F32)).astype(BF16)


def total(x):
    return jnp.sum(jnp.sum(x, axis=0, keepdims=True), axis=1, keepdims=True)


def greatest(x):
    return jnp.max(jnp.max(x, axis=0, keepdims=True), axis=1, keepdims=True)


def dot(a, b, dims):
    return lax.dot_general(a, b, ((dims[0], dims[1]), ((), ())), preferred_element_type=F32)


def shift_rows(x, gamma):
    size = x.shape[0]
    after = pltpu.roll(x, size - 1, 0)
    row = iota(x.shape, 0)
    out = gamma * x + 0.5 * (pltpu.roll(x, 1, 0) + after) + jnp.where(row == 0, 0.5 * after, 0.0)
    return jnp.where(row < ITERS, out, 0.0)


def shift_lanes(x, gamma):
    size = x.shape[1]
    after = pltpu.roll(x, size - 1, 1)
    lane = iota(x.shape, 1)
    out = gamma * x + 0.5 * (pltpu.roll(x, 1, 1) + after) + jnp.where(lane == 0, 0.5 * after, 0.0)
    return jnp.where(lane < ITERS, out, 0.0)


def projected(flat, gamma, fluid):
    shape = (16, 128)
    row, lane = iota(shape, 0), iota(shape, 1)
    gram = jnp.zeros(shape, F32)
    for i in range(SIDE):
        line = flat if i == 0 else pltpu.roll(flat, 128 - SIDE * i, 1)
        gram = jnp.where((row == i) & (lane < SIDE), line, gram)
    wide = shift_lanes(gram, gamma)
    if fluid:
        normal, right = shift_rows(wide, gamma), shift_rows(gram, gamma)
    else:
        normal, right = jnp.where(row < ITERS, wide, 0.0), jnp.where(row < ITERS, gram, 0.0)
    table = jnp.where(lane < ITERS, normal, 0.0)
    table = jnp.where((lane == row + 8) & (row < ITERS), 1.0, table)
    table = jnp.where(lane == 16, pltpu.roll(right, 16, 1), table)
    margin = None
    for k in range(ITERS):
        pivot = table[k : k + 1, k : k + 1]
        spare = pivot - PIVOT_LEAST * normal[k : k + 1, k : k + 1]
        margin = spare if margin is None else jnp.minimum(margin, spare)
        scaled = table[k : k + 1, :] * (1.0 / pivot)
        column = jnp.where(row[:, :1] == k, 0.0, table[:, k : k + 1])
        table = jnp.where(row == k, scaled, table - column * scaled)
    coeffs = jnp.broadcast_to(table[:, 16:17], shape)
    inverse = jnp.where(lane < ITERS, pltpu.roll(table, shape[1] - 8, 1), 0.0)
    applied = gamma * coeffs + 0.5 * (pltpu.roll(coeffs, 1, 0) + pltpu.roll(coeffs, shape[0] - 1, 0))
    applied = applied + jnp.where(row == 1, 0.5 * pltpu.roll(coeffs, 1, 0), 0.0)
    rest = jnp.where(row == 0, 1.0, 0.0) - applied
    image = jnp.broadcast_to(jnp.sum(gram * rest, axis=0, keepdims=True), shape)
    image = shift_lanes(image, gamma) if fluid else jnp.where(lane < ITERS, image, 0.0)
    change = jnp.sum(inverse * image, axis=1, keepdims=True)
    coeffs = coeffs[:, :1] + change
    size = jnp.sum(jnp.abs(coeffs), axis=0, keepdims=True)
    moved = jnp.sum(jnp.abs(change), axis=0, keepdims=True)
    good = (margin > 0.0) & (moved < REFINE_MOST * size)
    return coeffs, jnp.where(good, 1.0, 0.0)


def ring_far(step, size):
    return min(step, size - step)


def kernel(
    groups,
    bricks,
    forcing_hbm,
    thermal_hbm,
    storage_hbm,
    opening_hbm,
    flow_hbm,
    root_hbm,
    weight_hbm,
    rigidity_hbm,
    part_hbm,
    volume_hbm,
    vertex_hbm,
    factor_hbm,
    out,
    flag,
    thermal,
    forcing,
    storage,
    opening,
    flow,
    root,
    weight,
    rigidity,
    part,
    volume,
    vertex,
    factor,
    basis,
    ax,
    gx,
    diag,
    uy,
    ly,
    uz,
    lz,
    stiff,
    uh,
    ul,
    wz,
    wxy,
    weight_low,
    weight_up,
    row_hot,
    col_hot,
    picked,
    walls,
    nears,
    gram_tile,
    near_slots,
    far_slots,
    second,
    ghost,
    ghost_diag,
    load_sem,
    halo_send,
    halo_recv,
    coef_send,
    coef_recv,
    contact_send,
    contact_recv,
    near_send,
    near_recv,
    far_send,
    far_recv,
    deep_send,
    deep_recv,
    ghost_send,
    ghost_recv,
):
    group = lax.axis_index("group")
    brick = lax.axis_index("brick")
    rows, width, depth = forcing.shape
    plane = (width, depth)
    cells = rows * width
    solid = group == groups - 1
    fluid = group != groups - 1
    inner, outer = 8, bricks // 8
    low_id = lax.rem(brick, inner)
    high_id = group * outer + brick // inner
    n_far = groups * outer
    at_top = (brick == bricks - 1) & (group >= groups - 2)
    at_bottom = (brick == 0) & ((group == 0) | (group == groups - 1))
    has_up, has_down = jnp.logical_not(at_top), jnp.logical_not(at_bottom)
    far_up = (brick == bricks - 1) & (group < groups - 2)
    far_down = (brick == 0) & (group > 0) & fluid
    device = group * bricks + brick
    up_id = lax.rem(device + 1, groups * bricks)
    down_id = lax.rem(device + groups * bricks - 1, groups * bricks)
    up = (up_id // bricks, lax.rem(up_id, bricks))
    down = (down_id // bricks, lax.rem(down_id, bricks))

    names = [
        (vertex_hbm, vertex),
        (volume_hbm, volume),
        (thermal_hbm, thermal),
        (part_hbm, part),
        (factor_hbm, factor),
        (opening_hbm, opening),
        (flow_hbm, flow),
        (storage_hbm, storage),
        (weight_hbm, weight),
        (root_hbm, root),
        (rigidity_hbm, rigidity),
        (forcing_hbm, forcing),
    ]
    loads = [pltpu.make_async_copy(s, d, load_sem.at[i]) for i, (s, d) in enumerate(names)]
    for load in loads:
        load.start()
    (l_vertex, l_volume, l_thermal, l_part, l_factor, l_opening, l_flow, l_storage, l_weight, l_root, l_rigid, l_forcing) = loads

    plane_id = brick // inner
    near_peers, far_peers = [], []
    for dz, dc in sorted(((a, b) for a in range(inner // 2) for b in range(2)), key=lambda at: -ring_far(at[0], inner // 2)):
        if dz or dc:
            peer = lax.rem(low_id // 2 + dz, inner // 2) * 2 + lax.rem(low_id + dc, 2)
            near_peers.append((peer, (group, plane_id * inner + peer)))
    steps = sorted(
        ((a, b) for a in range(groups) for b in range(outer)), key=lambda at: -ring_far(at[0], groups) - ring_far(at[1], outer)
    )
    for dx, dy in steps:
        if dx or dy:
            x_id, y_id = lax.rem(group + dx, groups), lax.rem(plane_id + dy, outer)
            far_peers.append((x_id * outer + y_id, (x_id, y_id * inner + low_id)))

    barrier = pltpu.get_barrier_semaphore()
    for peer, where in far_peers + near_peers:
        pl.semaphore_signal(barrier, inc=1, device_id=where, device_id_type=MESH)

    @pl.when(has_up)
    def _():
        pl.semaphore_signal(barrier, inc=1, device_id=up, device_id_type=MESH)

    @pl.when(has_down)
    def _():
        pl.semaphore_signal(barrier, inc=1, device_id=down, device_id_type=MESH)

    @pl.when(at_bottom)
    def _():
        for k in range(ITERS):
            basis[RAW.get(k, k), 0] = jnp.zeros(plane, F32)

    @pl.when(at_top)
    def _():
        for k in range(ITERS):
            basis[RAW.get(k, k), rows + 1] = jnp.zeros(plane, F32)

    l_vertex.wait()
    l_volume.wait()
    target = jnp.where(solid, vertex[...], volume[...])
    cell_row, cell_col = target >> 8, target & 255
    lines = target.shape[0]
    points = lines * 128
    for j in range(lines):
        span = pl.ds(j * 128, 128)
        row_hot[:, span] = jnp.where(iota((cells, 128), 0) == cell_row[j : j + 1], 1.0, 0.0).astype(BF16)
        col_hot[:, span] = jnp.where(iota((depth, 128), 0) == cell_col[j : j + 1], 1.0, 0.0).astype(BF16)
    l_thermal.wait()
    high, low = pieces(thermal[...].reshape(cells, depth))
    hot = row_hot[...]
    found = dot(high, hot, ((0,), (0,))) + dot(low, hot, ((0,), (0,)))
    value = jnp.sum(found * col_hot[...].astype(F32), axis=0, keepdims=True)
    value = jnp.concatenate([value[:, j * 128 : (j + 1) * 128] for j in range(lines)], axis=0)
    l_part.wait()
    l_factor.wait()
    owned = jnp.where(part[...] == group, 1.0, 0.0)
    picked[0:lines] = jnp.where(solid, value, value * owned)
    picked[lines:] = jnp.zeros((8 - lines, 128), F32)

    pl.semaphore_wait(barrier, inner - 1 + n_far - 1 + has_up.astype(jnp.int32) + has_down.astype(jnp.int32))

    def wall_copy(g):
        return pltpu.make_async_remote_copy(
            picked, walls, contact_send.at[g], contact_recv.at[groups - 1], device_id=(g, brick), device_id_type=MESH
        )

    near_copy = pltpu.make_async_remote_copy(
        picked, nears.at[group], contact_send.at[0], contact_recv.at[group], device_id=(groups - 1, brick), device_id_type=MESH
    )

    @pl.when(solid)
    def _():
        for g in range(groups - 1):
            wall_copy(g).start()

    @pl.when(fluid)
    def _():
        near_copy.start()

    l_opening.wait()
    l_flow.wait()
    l_weight.wait()
    coef_a = pltpu.make_async_remote_copy(
        ax.at[rows], ax.at[0], coef_send.at[0], coef_recv.at[0], device_id=up, device_id_type=MESH
    )
    coef_g = pltpu.make_async_remote_copy(
        gx.at[rows], gx.at[0], coef_send.at[1], coef_recv.at[1], device_id=up, device_id_type=MESH
    )
    coef_up = pltpu.make_async_remote_copy(
        weight.at[rows - 1], weight_low, coef_send.at[0], coef_recv.at[0], device_id=up, device_id_type=MESH
    )
    coef_down = pltpu.make_async_remote_copy(
        weight.at[0], weight_up, coef_send.at[1], coef_recv.at[1], device_id=down, device_id_type=MESH
    )

    @pl.when(fluid)
    def _():
        last = jnp.where(at_top, 0.0, opening[0, rows - 1])
        ax[rows] = last
        gx[rows] = last * (1.0 + flow[0, rows - 1])

    @pl.when(fluid & has_up)
    def _():
        coef_a.start()
        coef_g.start()

    @pl.when(solid & has_up)
    def _():
        coef_up.start()

    @pl.when(solid & has_down)
    def _():
        coef_down.start()

    l_storage.wait()
    l_root.wait()
    l_rigid.wait()

    def spread(values):
        flat = jnp.concatenate([values[j : j + 1] for j in range(lines)], axis=1)
        high, low = pieces(flat)
        cols = col_hot[...].astype(F32)
        return dot(row_hot[...], (cols * high.astype(F32)).astype(BF16), ((1,), (1,))) + dot(
            row_hot[...], (cols * low.astype(F32)).astype(BF16), ((1,), (1,))
        )

    def fold(x, op):
        y = x.reshape(width // 8, 8, depth)
        return op(y, axis=0)

    y_at, z_at = iota(plane, 0), iota(plane, 1)

    def write_stats(d_max, d_min, o_sum):
        lane = iota((1, 128), 1)
        tile = jnp.where(lane == 0, greatest(d_max), jnp.where(lane == 1, greatest(-d_min), jnp.where(lane == 2, total(o_sum), 0.0)))
        near_slots[0, low_id] = tile

    start = (jnp.full((8, depth), -1e30, F32), jnp.full((8, depth), 1e30, F32), jnp.zeros((8, depth), F32))

    @pl.when(fluid)
    def _():
        extra = spread(factor[...] * owned).reshape(rows, width, depth)
        storage[...] = storage[...] + extra

        def second(r, carry):
            d_max, d_min, o_sum = carry
            a_y = jnp.where(y_at == width - 1, 0.0, opening[1, r])
            g_y = a_y * (1.0 + flow[1, r])
            g_low = pltpu.roll(g_y, 1, 0)
            uy[r] = a_y
            ly[r] = g_low
            a_x = jnp.where(at_top & (r == rows - 1), 0.0, opening[0, r])
            g_x = a_x * (1.0 + flow[0, r])

            @pl.when(r < rows - 1)
            def _():
                ax[r + 1] = a_x
                gx[r + 1] = g_x

            d = storage[r] + g_x + g_y + pltpu.roll(a_y, 1, 0)
            o = a_x + g_x + a_y + g_low
            a_z = jnp.where(z_at == depth - 1, 0.0, opening[2, r])
            g_z = a_z * (1.0 + flow[2, r])
            g_low = pltpu.roll(g_z, 1, 1)
            uz[r] = a_z
            lz[r] = g_low
            d = d + g_z + pltpu.roll(a_z, 1, 1)
            o = o + a_z + g_low
            d = d + jnp.where(r == 0, 0.0, opening[0, jnp.maximum(r - 1, 0)])
            diag[r] = d
            return jnp.maximum(d_max, fold(d, jnp.max)), jnp.minimum(d_min, fold(d, jnp.min)), o_sum + fold(o, jnp.sum)

        write_stats(*lax.fori_loop(0, rows, second, start))

    @pl.when(solid)
    def _():
        eye = iota((8, 8), 0) == iota((8, 8), 1)
        both = rigidity[0] + rigidity[1] + rigidity[2]
        size = jnp.abs(rigidity[0]) + jnp.abs(rigidity[1]) + jnp.abs(rigidity[2])
        trace = total(jnp.where(eye, both, 0.0)) * (1.0 / 8)
        off = total(jnp.where(eye, 0.0, size)) * (1.0 / 8)
        block_z = jnp.where(iota((8, depth), 1) % 8 == iota((8, depth), 0), 1.0, 0.0)
        spread_z = lax.dot_general(
            lax.dot_general(block_z, rigidity[2], (((0,), (1,)), ((), ())), precision=HIGH, preferred_element_type=F32),
            block_z,
            (((1,), (0,)), ((), ())),
            precision=HIGH,
            preferred_element_type=F32,
        )
        same = (iota((depth, depth), 0) // 8) == (iota((depth, depth), 1) // 8)
        high, low = pieces(jnp.where(same, spread_z, 0.0))
        wz[0], wz[1] = high, low
        outer_x = jnp.where(iota((8, 64), 1) // 8 == iota((8, 64), 0), 1.0, 0.0)
        inner_y = jnp.where(iota((8, 64), 1) % 8 == iota((8, 64), 0), 1.0, 0.0)

        def expand(matrix, hot):
            left = lax.dot_general(hot, matrix, (((0,), (0,)), ((), ())), precision=HIGH, preferred_element_type=F32)
            return lax.dot_general(left, hot, (((1,), (0,)), ((), ())), precision=HIGH, preferred_element_type=F32)

        same_y = iota((64, 64), 0) % 8 == iota((64, 64), 1) % 8
        same_x = iota((64, 64), 0) // 8 == iota((64, 64), 1) // 8
        mixed = jnp.where(same_y, expand(rigidity[0], outer_x), 0.0) + jnp.where(same_x, expand(rigidity[1], inner_y), 0.0)
        high, low = pieces(mixed)
        wxy[...] = jnp.concatenate([high, high, low], axis=1)

        def second(r, carry):
            d_max, d_min, o_sum = carry
            w = weight[r]
            b_y = jnp.where((y_at % 8 == 7) & (y_at < width - 1), 0.5 * (w + pltpu.roll(w, width - 1, 0)), 0.0)
            b_low = pltpu.roll(b_y, 1, 0)
            uy[r] = b_y
            ly[r] = b_low
            pair = b_y + b_low
            b_z = jnp.where((z_at % 8 == 7) & (z_at < depth - 1), 0.5 * (w + pltpu.roll(w, depth - 1, 1)), 0.0)
            b_low = pltpu.roll(b_z, 1, 1)
            uz[r] = b_z
            lz[r] = b_low
            pair = pair + b_z + b_low
            d = storage[r] + pair
            diag[r] = d
            square = root[r] * root[r]
            whole = d + square * trace
            o = pair + square * off
            return jnp.maximum(d_max, fold(whole, jnp.max)), jnp.minimum(d_min, fold(whole, jnp.min)), o_sum + fold(o, jnp.sum)

        write_stats(*lax.fori_loop(0, rows, second, start))

    def near_start(which):
        for o, (peer, where) in enumerate(near_peers):
            pltpu.make_async_remote_copy(
                near_slots.at[which, low_id],
                near_slots.at[which, low_id],
                near_send.at[which, o],
                near_recv.at[which, low_id],
                device_id=where,
                device_id_type=MESH,
            ).start()

    def near_wait(which):
        for o, (peer, where) in enumerate(near_peers):
            copy = pltpu.make_async_remote_copy(
                near_slots.at[which, peer],
                near_slots.at[which, peer],
                near_send.at[which, o],
                near_recv.at[which, peer],
                device_id=where,
                device_id_type=MESH,
            )
            copy.wait_recv()
            copy.wait_send()

    def far_start(which):
        for o, (peer, where) in enumerate(far_peers):
            pltpu.make_async_remote_copy(
                far_slots.at[which, high_id],
                far_slots.at[which, high_id],
                far_send.at[which, o],
                far_recv.at[which, high_id],
                device_id=where,
                device_id_type=MESH,
            ).start()

    def far_wait(which):
        for o, (peer, where) in enumerate(far_peers):
            copy = pltpu.make_async_remote_copy(
                far_slots.at[which, peer],
                far_slots.at[which, peer],
                far_send.at[which, o],
                far_recv.at[which, peer],
                device_id=where,
                device_id_type=MESH,
            )
            copy.wait_recv()
            copy.wait_send()

    def merge_stats(tiles):
        lane = iota((1, 128), 1)
        most, summed = tiles[0], tiles[0]
        for tile in tiles[1:]:
            most, summed = jnp.maximum(most, tile), summed + tile
        return jnp.where(lane == 2, summed, most)

    near_start(0)

    l_forcing.wait()

    part_rows = width // PARTS

    def halo_up(k, j):
        span = pl.ds(j * part_rows, part_rows)
        at = RAW.get(k, k)
        return pltpu.make_async_remote_copy(
            basis.at[at, rows, span],
            basis.at[at, 0, span],
            halo_send.at[k, 0, j],
            halo_recv.at[k, 0, j],
            device_id=up,
            device_id_type=MESH,
        )

    def halo_down(k, j):
        span = pl.ds(j * part_rows, part_rows)
        at = RAW.get(k, k)
        return pltpu.make_async_remote_copy(
            basis.at[at, 1, span],
            basis.at[at, rows + 1, span],
            halo_send.at[k, 1, j],
            halo_recv.at[k, 1, j],
            device_id=down,
            device_id_type=MESH,
        )

    def linked(k):
        if k in SKIP:
            return has_up & jnp.logical_not(far_up), has_down & jnp.logical_not(far_down)
        return has_up, has_down

    def send_halos(k, j):
        to_up, to_down = linked(k)

        @pl.when(to_up)
        def _():
            halo_up(k, j).start()

        @pl.when(to_down)
        def _():
            halo_down(k, j).start()

    def deep_up(i):
        return pltpu.make_async_remote_copy(
            basis.at[RAW.get(DEEP[i], DEEP[i]), rows - 1], second.at[0, i], deep_send.at[i, 0], deep_recv.at[i, 0], device_id=up, device_id_type=MESH
        )

    def deep_down(i):
        return pltpu.make_async_remote_copy(
            basis.at[RAW.get(DEEP[i], DEEP[i]), 2], second.at[1, i], deep_send.at[i, 1], deep_recv.at[i, 1], device_id=down, device_id_type=MESH
        )

    def ghost_up(i):
        source = (ghost_diag.at[0], uy.at[rows - 1], ly.at[rows - 1], uz.at[rows - 1], lz.at[rows - 1], gx.at[rows - 1])[i]
        return pltpu.make_async_remote_copy(
            source, ghost.at[0, i], ghost_send.at[0, i], ghost_recv.at[0, i], device_id=up, device_id_type=MESH
        )

    def ghost_down(i):
        source = (ghost_diag.at[1], uy.at[0], ly.at[0], uz.at[0], lz.at[0], ax.at[1])[i]
        return pltpu.make_async_remote_copy(
            source, ghost.at[1, i], ghost_send.at[1, i], ghost_recv.at[1, i], device_id=down, device_id_type=MESH
        )

    def send_deep(i):
        @pl.when(far_up)
        def _():
            deep_up(i).start()

        @pl.when(far_down)
        def _():
            deep_down(i).start()

    @pl.when(fluid)
    def _():
        pltpu.make_async_remote_copy(
            picked, walls, contact_send.at[0], contact_recv.at[groups - 1], device_id=(groups - 1, brick), device_id_type=MESH
        ).wait_recv()

    @pl.when(solid)
    def _():
        for g in range(groups - 1):
            pltpu.make_async_remote_copy(
                picked, nears.at[g], contact_send.at[g], contact_recv.at[g], device_id=(g, brick), device_id_type=MESH
            ).wait_recv()
        walls[...] = nears[0] + nears[1] + nears[2] - picked[...]

    heat = factor[...] * walls[0:lines]
    extra = spread(jnp.where(solid, heat, heat * owned)).reshape(rows, width, depth)
    basis[0, 1 : rows + 1] = forcing[...] + extra
    for j in range(PARTS):
        send_halos(0, j)
    send_deep(0)

    @pl.when(at_bottom)
    def _():
        gx[0] = jnp.zeros(plane, F32)

    @pl.when(fluid & has_down)
    def _():
        coef_a.wait_recv()
        coef_g.wait_recv()
        diag[0] = diag[0] + ax[0]

    @pl.when(solid & has_down)
    def _():
        coef_up.wait_recv()
        gx[0] = 0.5 * (weight_low[...] + weight[0])
        diag[0] = diag[0] + gx[0]

    @pl.when(solid & has_up)
    def _():
        coef_down.wait_recv()
        ax[rows] = 0.5 * (weight[rows - 1] + weight_up[...])
        diag[rows - 1] = diag[rows - 1] + ax[rows]

    @pl.when(solid & at_top)
    def _():
        ax[rows] = jnp.zeros(plane, F32)

    def gram_sums(k, low, high, accs):
        def body(r, accs):
            accs = list(accs)
            for j in range(width // 8):
                span = slice(8 * j, 8 * j + 8)
                mine = basis[k, r + 1, span, :]
                for i in range(k + 1):
                    other = mine if i == k else basis[i, r + 1, span, :]
                    accs[i] = accs[i] + mine * other
            return tuple(accs)

        return lax.fori_loop(low, high, body, accs)

    def gram_none(k):
        return tuple(jnp.zeros((8, depth), F32) for _ in range(k + 1))

    def gram_keep(k, accs):
        lane = iota((1, 128), 1)
        tile = jnp.zeros((1, 128), F32) if k == 0 else gram_tile[...]
        for i in range(k + 1):
            spot = (lane == i * SIDE + k) | (lane == k * SIDE + i)
            tile = jnp.where(spot, total(accs[i]), tile)
        gram_tile[...] = tile

    def gram_row(k):
        gram_keep(k, gram_sums(k, 0, rows, gram_none(k)))

    def local(r, v):
        return (
            diag[r] * v
            - uy[r] * pltpu.roll(v, width - 1, 0)
            - ly[r] * pltpu.roll(v, 1, 0)
            - uz[r] * pltpu.roll(v, depth - 1, 1)
            - lz[r] * pltpu.roll(v, 1, 1)
        )

    def apply(k, scale):
        at, to = (RAW.get(k, k), RAW[k + 1]) if scale is None else (k, k + 1)

        def keep(r, q):
            if scale is None:
                basis[to, r + 1] = q
            else:
                basis[to, r + 1] = scale * q - basis[k - 1, r + 1]

        @pl.when(fluid)
        def _():
            def middle(r, carry):
                v = basis[at, r + 1]
                keep(r, local(r, v) - gx[r] * basis[at, r] - ax[r + 1] * basis[at, r + 2])
                return carry

            keep(0, local(0, basis[at, 1]) - ax[1] * basis[at, 2])
            keep(rows - 1, local(rows - 1, basis[at, rows]) - gx[rows - 1] * basis[at, rows - 1])
            lax.fori_loop(1, rows - 1, middle, 0)

        @pl.when(solid)
        def _():
            for e in range(width // 8):
                u = (root[:, 8 * e : 8 * e + 8, :] * basis[at, 1 : rows + 1, 8 * e : 8 * e + 8, :]).reshape(64, depth)
                high, low = pieces(u)
                uh[e], ul[e] = high, low
                stiff[e] = dot(wxy[...], jnp.concatenate([high, low, high], axis=0), ((1,), (0,)))
            high, low = uh[...].reshape(cells, depth), ul[...].reshape(cells, depth)
            along = dot(high, wz[0], ((1,), (0,))) + dot(low, wz[0], ((1,), (0,))) + dot(high, wz[1], ((1,), (0,)))
            stiff[...] = stiff[...] + along.reshape(width // 8, 64, depth)

            def each(r, carry):
                force = stiff[:, pl.ds(r * 8, 8), :].reshape(width, depth)
                keep(r, local(r, basis[at, r + 1]) + root[r] * force)
                return carry

            lax.fori_loop(0, rows, each, 0)

    def finish(k, scale, mix=None):
        at, to = RAW.get(k, k), (RAW[k + 1] if scale is None else k + 1)
        for j in range(PARTS):
            span = slice(j * part_rows, (j + 1) * part_rows)

            from_up, from_down = linked(k)

            @pl.when(from_down)
            def _():
                halo_up(k, j).wait_recv()

            @pl.when(from_up)
            def _():
                halo_down(k, j).wait_recv()

            for own, halo, coef in ((1, 0, gx.at[0]), (rows, rows + 1, ax.at[rows])):
                value = basis[at, halo, span]
                if mix is not None:
                    value = mix[0] * value + mix[1] * basis[RAW[1], halo, span] + mix[2] * basis[0, halo, span]
                    basis[k, halo, span] = value
                value = coef[span] * value
                if scale is not None:
                    value = scale * value
                basis[to, own, span] = basis[to, own, span] - value
            if k + 1 < ITERS:
                send_halos(k + 1, j)

    def extend(i):
        k = DEEP[i]
        fresh = range(i + 1) if k == 2 else (i,)

        def row(side, near, halo, inward):
            v = basis[k, halo]
            if k == 2:
                outer_row = mix[0] * second[side, 2] + mix[1] * second[side, 1] + mix[2] * second[side, 0]
                older = (basis[RAW[1], halo] - center * basis[0, halo]) * inv_e
            else:
                outer_row, older = second[side, i], basis[k - 1, halo]
            q = (
                (ghost[side, 0] - center) * v
                - ghost[side, 1] * pltpu.roll(v, width - 1, 0)
                - ghost[side, 2] * pltpu.roll(v, 1, 0)
                - ghost[side, 3] * pltpu.roll(v, depth - 1, 1)
                - ghost[side, 4] * pltpu.roll(v, 1, 1)
                - ghost[side, 5] * outer_row
                - inward * basis[k, near]
            )
            basis[k + 1, halo] = scale * q - older

        @pl.when(far_down)
        def _():
            for n in fresh:
                deep_up(n).wait_recv()
            if k == 2:
                for n in range(6):
                    ghost_up(n).wait_recv()
            row(0, 1, 0, ax[0])

        @pl.when(far_up)
        def _():
            for n in fresh:
                deep_down(n).wait_recv()
            if k == 2:
                for n in range(6):
                    ghost_down(n).wait_recv()
            row(1, rows, rows + 1, gx[rows])

    apply(0, None)
    send_deep(1)
    near_wait(0)
    far_slots[0, high_id] = merge_stats([near_slots[0, i] for i in range(inner)])
    far_start(0)
    finish(0, None)

    @pl.when(far_up)
    def _():
        ghost_diag[0] = diag[rows - 1]
        for n in range(6):
            ghost_up(n).start()

    @pl.when(far_down)
    def _():
        ghost_diag[1] = diag[0]
        for n in range(6):
            ghost_down(n).start()

    apply(1, None)
    send_deep(2)
    gram_row(0)
    finish(1, None)
    far_wait(0)
    split = (groups - 1) * outer

    def interval(tiles, count, of_most, of_mean):
        stats = merge_stats(tiles)
        mean = stats[0:1, 2:3] * (1.0 / count)
        high = of_most * stats[0:1, 0:1] + of_mean * mean
        low = jnp.maximum(-stats[0:1, 1:2] - 0.5 * mean, 0.0)
        return 0.5 * (high + low), 0.5 * (high - low)

    c_fluid, e_fluid = interval([far_slots[0, i] for i in range(split)], float((groups - 1) * bricks * cells * depth), 0.9, 0.1)
    c_solid, e_solid = interval([far_slots[0, i] for i in range(split, n_far)], float(bricks * cells * depth), 0.97, 0.25)
    center = jnp.where(solid, c_solid, c_fluid)
    inv_e = 1.0 / jnp.where(solid, e_solid, e_fluid)
    scale = 2.0 * inv_e

    mix = (scale * inv_e, -2.0 * scale * center * inv_e, scale * inv_e * center * center - 1.0)

    def convert(r, carry):
        zero, one, two = basis[0, r + 1], basis[RAW[1], r + 1], basis[RAW[2], r + 1]
        basis[1, r + 1] = (one - center * zero) * inv_e
        basis[2, r + 1] = mix[0] * two + mix[1] * one + mix[2] * zero
        diag[r] = diag[r] - center
        return carry

    lax.fori_loop(0, rows, convert, 0)
    for k in range(2, ITERS):
        apply(k, scale)
        if k + 1 in DEEP:
            send_deep(DEEP.index(k + 1))
        if k == 2:
            gram_row(1)
        gram_row(k)
        if k + 1 == ITERS:
            last_sums = gram_sums(ITERS, 1, rows - 1, gram_none(ITERS))
        finish(k, scale, mix if k == 2 else None)
        if k + 1 in SKIP:
            extend(DEEP.index(k))
    last_sums = gram_sums(ITERS, rows - 1, rows, gram_sums(ITERS, 0, 1, last_sums))
    gram_keep(ITERS, last_sums)

    near_slots[1, low_id] = gram_tile[...]
    near_start(1)
    near_wait(1)
    summed = near_slots[1, 0]
    for i in range(1, inner):
        summed = summed + near_slots[1, i]
    far_slots[1, high_id] = summed
    far_start(1)

    @pl.when(solid)
    def _():
        for g in range(groups - 1):
            wall_copy(g).wait_send()

    @pl.when(fluid)
    def _():
        near_copy.wait_send()

    @pl.when(fluid & has_up)
    def _():
        coef_a.wait_send()
        coef_g.wait_send()

    @pl.when(solid & has_up)
    def _():
        coef_up.wait_send()

    @pl.when(solid & has_down)
    def _():
        coef_down.wait_send()

    @pl.when(far_up)
    def _():
        for n in range(6):
            ghost_up(n).wait_send()
        for i in range(len(DEEP)):
            deep_up(i).wait_send()

    @pl.when(far_down)
    def _():
        for n in range(6):
            ghost_down(n).wait_send()
        for i in range(len(DEEP)):
            deep_down(i).wait_send()

    for k in range(ITERS):
        sent_up, sent_down = linked(k)
        for j in range(PARTS):

            @pl.when(sent_up)
            def _():
                halo_up(k, j).wait_send()

            @pl.when(sent_down)
            def _():
                halo_down(k, j).wait_send()

    far_wait(1)
    gram_fluid = far_slots[1, 0]
    for i in range(1, split):
        gram_fluid = gram_fluid + far_slots[1, i]
    gram_solid = far_slots[1, split]
    for i in range(split + 1, n_far):
        gram_solid = gram_solid + far_slots[1, i]
    y_fluid, ok_fluid = projected(gram_fluid, c_fluid / e_fluid, True)
    y_solid, ok_solid = projected(gram_solid, c_solid / e_solid, False)
    coeffs = jnp.where(solid, y_solid, y_fluid) * inv_e
    flag[0] = jnp.max(ok_fluid * ok_solid).astype(jnp.int32)
    weights = [coeffs[k : k + 1, :1] for k in range(ITERS)]

    def combine(r, carry):
        acc = weights[0] * basis[0, r + 1]
        for k in range(1, ITERS):
            acc = acc + weights[k] * basis[k, r + 1]
        out[r] = acc
        return carry

    lax.fori_loop(0, rows, combine, 0)


def handed_on(result):
    def body(source, target, sem):
        copy = pltpu.make_async_copy(source, target, sem)
        copy.start()
        copy.wait()

    return pl.pallas_call(
        body,
        out_shape=jax.ShapeDtypeStruct(result.shape, result.dtype),
        in_specs=[pl.BlockSpec(memory_space=pltpu.VMEM)],
        out_specs=pl.BlockSpec(memory_space=pl.ANY),
        scratch_shapes=[pltpu.SemaphoreType.DMA],
        name="handed_on",
    )(pltpu.with_memory_space_constraint(result, pltpu.VMEM))


def shards(*arguments):
    groups, bricks = lax.axis_size("group"), lax.axis_size("brick")
    forcing = arguments[0]
    rows, width, depth = slab = forcing.shape
    lines = arguments[8].shape[0]
    points = lines * 128
    n_far = groups * (bricks // 8)
    vm = pltpu.VMEM
    scratch = (
        [vm(slab, F32)] * 3
        + [vm((3,) + slab, F32)] * 2
        + [vm(slab, F32)] * 2
        + [vm((3, 8, 8), F32)]
        + [vm((lines, 128), jnp.int32)] * 3
        + [vm((lines, 128), F32)]
        + [vm((ITERS + 3, rows + 2, width, depth), F32)]
        + [vm((rows + 1, width, depth), F32)] * 2
        + [vm(slab, F32)] * 5
        + [vm((width // 8, 64, depth), F32)]
        + [vm((width // 8, 64, depth), BF16)] * 2
        + [vm((2, depth, depth), BF16), vm((64, 192), BF16)]
        + [vm((width, depth), F32)] * 2
        + [vm((rows * width, points), BF16), vm((depth, points), BF16)]
        + [vm((8, 128), F32)] * 2
        + [vm((groups - 1, 8, 128), F32)]
        + [vm((1, 128), F32), vm((2, 8, 1, 128), F32), vm((2, n_far, 1, 128), F32)]
        + [vm((2, len(DEEP), width, depth), F32), vm((2, 6, width, depth), F32), vm((2, width, depth), F32)]
    )
    dma = pltpu.SemaphoreType.DMA
    semaphores = [
        dma((12,)),
        dma((ITERS, 2, PARTS)),
        dma((ITERS, 2, PARTS)),
        dma((2,)),
        dma((2,)),
        dma((groups,)),
        dma((groups,)),
        dma((2, 8)),
        dma((2, 8)),
        dma((2, n_far)),
        dma((2, n_far)),
        dma((len(DEEP), 2)),
        dma((len(DEEP), 2)),
        dma((2, 6)),
        dma((2, 6)),
    ]
    result, flag = pl.pallas_call(
        functools.partial(kernel, groups, bricks),
        out_shape=(pltpu.VMEM(slab, F32), jax.ShapeDtypeStruct((1,), jnp.int32)),
        in_specs=[pl.BlockSpec(memory_space=pl.ANY)] * 12,
        out_specs=(pl.BlockSpec(memory_space=pltpu.VMEM), pl.BlockSpec(memory_space=pltpu.SMEM)),
        scratch_shapes=scratch + semaphores,
        compiler_params=pltpu.CompilerParams(collective_id=0, has_side_effects=True, vmem_limit_bytes=56 * 2**20),
        name="coupled",
    )(*arguments)
    return lax.cond(flag[0] > 0, lambda: handed_on(result), lambda: iterated(*arguments))


def solution(mesh):
    return jax.shard_map(
        shards,
        mesh=mesh,
        in_specs=(
            P(("group", "brick"), None, None),
            P(("group", "brick"), None, None),
            P(("group", "brick"), None, None),
            P(None, ("group", "brick"), None, None),
            P(None, ("group", "brick"), None, None),
            P(("group", "brick"), None, None),
            P(("group", "brick"), None, None),
            P(),
            P("brick", None),
            P("brick", None),
            P("brick", None),
            P("brick", None),
        ),
        out_specs=P(("group", "brick"), None, None),
        check_vma=False,
    )
```

```python
import functools

import jax
import jax.numpy as jnp
from jax import lax
from jax.experimental import pallas as pl
from jax.experimental.pallas import tpu as pltpu
from jax.sharding import PartitionSpec as P

ITERS = 8


HIGH = lax.Precision.HIGHEST


def passed_along(value, axis, steps):
    count = lax.axis_size(axis)
    leading, last = (max(0, -steps), min(count, count - steps))
    return lax.ppermute(value, axis, [(source, source + steps) for source in range(leading, last)])


def extended(cells, sides, width):
    for axis, dim in sides:
        count = lax.axis_size(axis)
        ends = count - 1
        head = lax.slice_in_dim(cells, 0, width, axis=dim)
        tail = lax.slice_in_dim(cells, cells.shape[dim] - width, cells.shape[dim], axis=dim)
        cells = jnp.concatenate(
            [
                lax.ppermute(tail, axis, [(i, (i + 1) % count) for i in range(ends)]),
                cells,
                lax.ppermute(head, axis, [((i + 1) % count, i) for i in range(ends)]),
            ],
            axis=dim,
        )
    return cells


def shift_next(v, axis):
    size = v.shape[axis]
    inner = lax.slice_in_dim(v, 1, size, axis=axis)
    zero = jnp.zeros_like(lax.slice_in_dim(v, 0, 1, axis=axis))
    return jnp.concatenate([inner, zero], axis=axis)


def shift_prev(v, axis):
    size = v.shape[axis]
    inner = lax.slice_in_dim(v, 0, size - 1, axis=axis)
    zero = jnp.zeros_like(lax.slice_in_dim(v, 0, 1, axis=axis))
    return jnp.concatenate([zero, inner], axis=axis)


def open_faces(shape, axis):
    index = lax.broadcasted_iota(jnp.int32, shape, axis)
    return (index < shape[axis] - 1).astype(jnp.float32)


def element_faces(shape, axis, nodes):
    index = lax.broadcasted_iota(jnp.int32, shape, axis)
    inside = (index % nodes == nodes - 1) & (index < shape[axis] - 1)
    return inside.astype(jnp.float32)


def stiffness_apply(u, rigidity_matrix):
    nodes = rigidity_matrix.shape[1]
    rows, width, depth = u.shape
    block = min(depth, 128)
    along_x = jnp.einsum("pq,qyz->pyz", rigidity_matrix[0], u, precision=HIGH)
    split_y = u.reshape(rows, width // nodes, nodes, depth)
    along_y = jnp.einsum("pq,xeqz->xepz", rigidity_matrix[1], split_y, precision=HIGH).reshape(
        rows, width, depth
    )
    wide = jnp.kron(jnp.eye(block // nodes, dtype=jnp.float32), rigidity_matrix[2])
    split_z = u.reshape(rows, width, depth // block, block)
    along_z = jnp.einsum("xyeq,pq->xyep", split_z, wide, precision=HIGH).reshape(rows, width, depth)
    return along_x + along_y + along_z


def least_squares(hess, beta):
    gram = jnp.dot(hess.T, hess, precision=HIGH)
    lower = jnp.linalg.cholesky(gram)
    right = (beta * hess[0])[:, None]
    middle = lax.linalg.triangular_solve(lower, right, left_side=True, lower=True)
    coeffs = lax.linalg.triangular_solve(
        lower, middle, left_side=True, lower=True, transpose_a=True
    )
    return coeffs[:, 0]


def iterated(
    forcing_vector,
    thermal_iterate,
    storage_over_step,
    opening_shares,
    flow_speed,
    diffusivity_root,
    sanction_weight,
    rigidity_matrix,
    contact_fluid_part,
    contact_fluid_volume,
    contact_solid_vertex,
    exchange_rate_factor,
):
    groups = lax.axis_size("group")
    bricks = lax.axis_size("brick")
    group_id = lax.axis_index("group")
    brick_id = lax.axis_index("brick")
    solid = group_id == groups - 1
    solid_flag = solid.astype(jnp.float32)
    fluid_flag = 1.0 - solid_flag
    rows, width, depth = forcing_vector.shape
    nodes = rigidity_matrix.shape[1]
    device = group_id * bricks + brick_id
    first_solid = (groups - 1) * bricks
    unrolled_array = thermal_iterate.reshape(-1)
    owned = (contact_fluid_part == group_id).astype(jnp.float32)
    target = jnp.where(solid, contact_solid_vertex, contact_fluid_volume).reshape(-1)
    picked = unrolled_array[target].reshape(contact_solid_vertex.shape)
    wall, near = lax.psum((picked * solid_flag, picked * owned * fluid_flag), "group")
    extra_rhs = jnp.where(
        solid, exchange_rate_factor * (near - wall), exchange_rate_factor * wall * owned
    )
    extra_diag = exchange_rate_factor * owned * fluid_flag
    rhs = (
        forcing_vector.reshape(-1)
        .at[target]
        .add(extra_rhs.reshape(-1))
        .reshape(forcing_vector.shape)
    )
    fluid_diag = (
        storage_over_step.reshape(-1)
        .at[target]
        .add(extra_diag.reshape(-1))
        .reshape(forcing_vector.shape)
    )
    shape = (rows, width, depth)
    global_row = device * rows + lax.broadcasted_iota(jnp.int32, shape, 0)
    face_x = opening_shares[0] * (global_row != first_solid * rows - 1).astype(jnp.float32)
    face_y = opening_shares[1] * open_faces(shape, 1)
    face_z = opening_shares[2] * open_faces(shape, 2)
    rims = passed_along(
        jnp.stack([face_x[-1], flow_speed[0][-1], sanction_weight[-1]]), ("group", "brick"), 1
    )
    face_low = rims[0]
    speed_low = rims[1]
    weight_low = rims[2]
    pair_low = 0.5 * (weight_low + sanction_weight[0]) * (device != first_solid).astype(jnp.float32)
    pair_up = passed_along(pair_low, "brick", -1)
    pair_y = (
        0.5 * (sanction_weight + shift_next(sanction_weight, 1)) * element_faces(shape, 1, nodes)
    )
    pair_z = (
        0.5 * (sanction_weight + shift_next(sanction_weight, 2)) * element_faces(shape, 2, nodes)
    )
    local_square = jnp.sum(rhs * rhs)
    solution = jnp.zeros_like(rhs)
    resid = rhs
    columns = []
    fluid_square, solid_square = lax.psum(
        (local_square * fluid_flag, local_square * solid_flag), ("group", "brick")
    )
    beta = jnp.sqrt(fluid_square)
    basis = [rhs / beta]
    direction = rhs
    norm_now = solid_square
    for step in range(ITERS):
        vector = jnp.where(solid, direction, basis[step])
        padded = extended(vector, ((("group", "brick"), 0),), 1)
        below = padded[0]
        above = padded[-1]

        def fluid_branch(unused):
            following = jnp.concatenate([vector[1:], above[None]], axis=0)
            flux_x = face_x * ((1.0 + flow_speed[0]) * vector - following)
            flux_low = face_low * ((1.0 + speed_low) * below - vector[0])
            out = (
                fluid_diag * vector
                + flux_x
                - jnp.concatenate([flux_low[None], flux_x[:-1]], axis=0)
            )
            flux_y = face_y * ((1.0 + flow_speed[1]) * vector - shift_next(vector, 1))
            flux_z = face_z * ((1.0 + flow_speed[2]) * vector - shift_next(vector, 2))
            return out + flux_y - shift_prev(flux_y, 1) + flux_z - shift_prev(flux_z, 2)

        def solid_branch(unused):
            out = storage_over_step * vector + diffusivity_root * stiffness_apply(
                diffusivity_root * vector, rigidity_matrix
            )
            jump_up = pair_up * (vector[-1] - above)
            jump_low = pair_low * (below - vector[0])
            out = out.at[0].add(-jump_low).at[rows - 1].add(jump_up)
            jump_y = pair_y * (vector - shift_next(vector, 1))
            jump_z = pair_z * (vector - shift_next(vector, 2))
            return out + jump_y - shift_prev(jump_y, 1) + jump_z - shift_prev(jump_z, 2)

        image = lax.cond(solid, solid_branch, fluid_branch, 0)
        inner = jnp.stack([jnp.sum(basis[j] * image) for j in range(step + 1)])
        heights, curvature = lax.psum(
            (inner * fluid_flag, jnp.sum(direction * image) * solid_flag), ("group", "brick")
        )
        fresh = image
        for j in range(step + 1):
            fresh = fresh - heights[j] * basis[j]
        alpha = norm_now / curvature
        solution = solution + alpha * direction
        resid = resid - alpha * image
        fresh_square, norm_next = lax.psum(
            (jnp.sum(fresh * fresh) * fluid_flag, jnp.sum(resid * resid) * solid_flag),
            ("group", "brick"),
        )
        length = jnp.sqrt(fresh_square)
        basis.append(fresh / length)
        columns.append(
            jnp.concatenate([heights, length[None], jnp.zeros((ITERS - 1 - step,), jnp.float32)])
        )
        direction = resid + norm_next / norm_now * direction
        norm_now = norm_next
    coeffs = least_squares(jnp.stack(columns, axis=1), beta)
    fluid_new = jnp.zeros_like(rhs)
    for step in range(ITERS):
        fluid_new = fluid_new + coeffs[step] * basis[step]
    return jnp.where(solid, solution, fluid_new)


F32 = jnp.float32
BF16 = jnp.bfloat16
MESH = pl.DeviceIdType.MESH
PIVOT_LEAST = 1e-4
REFINE_MOST = 4e-3
PARTS = 4
SIDE = ITERS + 1
RAW = {1: ITERS + 1, 2: ITERS + 2}
DEEP = (0, 1, 2, 4, 6)
SKIP = (3, 5, 7)


def iota(shape, dim):
    return lax.broadcasted_iota(jnp.int32, shape, dim)


def pieces(x):
    high = x.astype(BF16)
    return high, (x - high.astype(F32)).astype(BF16)


def total(x):
    return jnp.sum(jnp.sum(x, axis=0, keepdims=True), axis=1, keepdims=True)


def greatest(x):
    return jnp.max(jnp.max(x, axis=0, keepdims=True), axis=1, keepdims=True)


def dot(a, b, dims):
    return lax.dot_general(a, b, ((dims[0], dims[1]), ((), ())), preferred_element_type=F32)


def shift_rows(x, gamma):
    size = x.shape[0]
    after = pltpu.roll(x, size - 1, 0)
    row = iota(x.shape, 0)
    out = gamma * x + 0.5 * (pltpu.roll(x, 1, 0) + after) + jnp.where(row == 0, 0.5 * after, 0.0)
    return jnp.where(row < ITERS, out, 0.0)


def shift_lanes(x, gamma):
    size = x.shape[1]
    after = pltpu.roll(x, size - 1, 1)
    lane = iota(x.shape, 1)
    out = gamma * x + 0.5 * (pltpu.roll(x, 1, 1) + after) + jnp.where(lane == 0, 0.5 * after, 0.0)
    return jnp.where(lane < ITERS, out, 0.0)


def projected(flat, gamma, fluid):
    shape = (16, 128)
    row, lane = iota(shape, 0), iota(shape, 1)
    gram = jnp.zeros(shape, F32)
    for i in range(SIDE):
        line = flat if i == 0 else pltpu.roll(flat, 128 - SIDE * i, 1)
        gram = jnp.where((row == i) & (lane < SIDE), line, gram)
    wide = shift_lanes(gram, gamma)
    if fluid:
        normal, right = shift_rows(wide, gamma), shift_rows(gram, gamma)
    else:
        normal, right = jnp.where(row < ITERS, wide, 0.0), jnp.where(row < ITERS, gram, 0.0)
    table = jnp.where(lane < ITERS, normal, 0.0)
    table = jnp.where((lane == row + 8) & (row < ITERS), 1.0, table)
    table = jnp.where(lane == 16, pltpu.roll(right, 16, 1), table)
    margin = None
    for k in range(ITERS):
        pivot = table[k : k + 1, k : k + 1]
        spare = pivot - PIVOT_LEAST * normal[k : k + 1, k : k + 1]
        margin = spare if margin is None else jnp.minimum(margin, spare)
        scaled = table[k : k + 1, :] * (1.0 / pivot)
        column = jnp.where(row[:, :1] == k, 0.0, table[:, k : k + 1])
        table = jnp.where(row == k, scaled, table - column * scaled)
    coeffs = jnp.broadcast_to(table[:, 16:17], shape)
    inverse = jnp.where(lane < ITERS, pltpu.roll(table, shape[1] - 8, 1), 0.0)
    applied = gamma * coeffs + 0.5 * (pltpu.roll(coeffs, 1, 0) + pltpu.roll(coeffs, shape[0] - 1, 0))
    applied = applied + jnp.where(row == 1, 0.5 * pltpu.roll(coeffs, 1, 0), 0.0)
    rest = jnp.where(row == 0, 1.0, 0.0) - applied
    image = jnp.broadcast_to(jnp.sum(gram * rest, axis=0, keepdims=True), shape)
    image = shift_lanes(image, gamma) if fluid else jnp.where(lane < ITERS, image, 0.0)
    change = jnp.sum(inverse * image, axis=1, keepdims=True)
    coeffs = coeffs[:, :1] + change
    size = jnp.sum(jnp.abs(coeffs), axis=0, keepdims=True)
    moved = jnp.sum(jnp.abs(change), axis=0, keepdims=True)
    good = (margin > 0.0) & (moved < REFINE_MOST * size)
    return coeffs, jnp.where(good, 1.0, 0.0)


def ring_far(step, size):
    return min(step, size - step)


def kernel(
    groups,
    bricks,
    forcing_hbm,
    thermal_hbm,
    storage_hbm,
    opening_hbm,
    flow_hbm,
    root_hbm,
    weight_hbm,
    rigidity_hbm,
    part_hbm,
    volume_hbm,
    vertex_hbm,
    factor_hbm,
    out,
    flag,
    thermal,
    forcing,
    storage,
    opening,
    flow,
    root,
    weight,
    rigidity,
    part,
    volume,
    vertex,
    factor,
    basis,
    ax,
    gx,
    diag,
    uy,
    ly,
    uz,
    lz,
    stiff,
    uh,
    ul,
    wz,
    wxy,
    weight_low,
    weight_up,
    row_hot,
    col_hot,
    picked,
    walls,
    nears,
    gram_tile,
    near_slots,
    far_slots,
    second,
    ghost,
    ghost_diag,
    load_sem,
    halo_send,
    halo_recv,
    coef_send,
    coef_recv,
    contact_send,
    contact_recv,
    near_send,
    near_recv,
    far_send,
    far_recv,
    deep_send,
    deep_recv,
    ghost_send,
    ghost_recv,
):
    group = lax.axis_index("group")
    brick = lax.axis_index("brick")
    rows, width, depth = forcing.shape
    plane = (width, depth)
    cells = rows * width
    solid = group == groups - 1
    fluid = group != groups - 1
    inner, outer = 8, bricks // 8
    low_id = lax.rem(brick, inner)
    high_id = group * outer + brick // inner
    n_far = groups * outer
    at_top = (brick == bricks - 1) & (group >= groups - 2)
    at_bottom = (brick == 0) & ((group == 0) | (group == groups - 1))
    has_up, has_down = jnp.logical_not(at_top), jnp.logical_not(at_bottom)
    far_up = (brick == bricks - 1) & (group < groups - 2)
    far_down = (brick == 0) & (group > 0) & fluid
    device = group * bricks + brick
    up_id = lax.rem(device + 1, groups * bricks)
    down_id = lax.rem(device + groups * bricks - 1, groups * bricks)
    up = (up_id // bricks, lax.rem(up_id, bricks))
    down = (down_id // bricks, lax.rem(down_id, bricks))

    names = [
        (vertex_hbm, vertex),
        (volume_hbm, volume),
        (thermal_hbm, thermal),
        (part_hbm, part),
        (factor_hbm, factor),
        (opening_hbm, opening),
        (flow_hbm, flow),
        (storage_hbm, storage),
        (weight_hbm, weight),
        (root_hbm, root),
        (rigidity_hbm, rigidity),
        (forcing_hbm, forcing),
    ]
    loads = [pltpu.make_async_copy(s, d, load_sem.at[i]) for i, (s, d) in enumerate(names)]
    for load in loads[:3]:
        load.start()
    (l_vertex, l_volume, l_thermal, l_part, l_factor, l_opening, l_flow, l_storage, l_weight, l_root, l_rigid, l_forcing) = loads

    plane_id = brick // inner
    near_peers, far_peers = [], []
    for dz, dc in sorted(((a, b) for a in range(inner // 2) for b in range(2)), key=lambda at: -ring_far(at[0], inner // 2)):
        if dz or dc:
            peer = lax.rem(low_id // 2 + dz, inner // 2) * 2 + lax.rem(low_id + dc, 2)
            near_peers.append((peer, (group, plane_id * inner + peer)))
    steps = sorted(
        ((a, b) for a in range(groups) for b in range(outer)), key=lambda at: -ring_far(at[0], groups) - ring_far(at[1], outer)
    )
    for dx, dy in steps:
        if dx or dy:
            x_id, y_id = lax.rem(group + dx, groups), lax.rem(plane_id + dy, outer)
            far_peers.append((x_id * outer + y_id, (x_id, y_id * inner + low_id)))

    barrier = pltpu.get_barrier_semaphore()
    for peer, where in far_peers + near_peers:
        pl.semaphore_signal(barrier, inc=1, device_id=where, device_id_type=MESH)

    @pl.when(has_up)
    def _():
        pl.semaphore_signal(barrier, inc=1, device_id=up, device_id_type=MESH)

    @pl.when(has_down)
    def _():
        pl.semaphore_signal(barrier, inc=1, device_id=down, device_id_type=MESH)

    for load in loads[3:]:
        load.start()

    @pl.when(at_bottom)
    def _():
        for k in range(ITERS):
            basis[RAW.get(k, k), 0] = jnp.zeros(plane, F32)

    @pl.when(at_top)
    def _():
        for k in range(ITERS):
            basis[RAW.get(k, k), rows + 1] = jnp.zeros(plane, F32)

    l_vertex.wait()
    l_volume.wait()
    target = jnp.where(solid, vertex[...], volume[...])
    cell_row, cell_col = target >> 8, target & 255
    lines = target.shape[0]
    points = lines * 128
    for j in range(lines):
        span = pl.ds(j * 128, 128)
        row_hot[:, span] = jnp.where(iota((cells, 128), 0) == cell_row[j : j + 1], 1.0, 0.0).astype(BF16)
        col_hot[:, span] = jnp.where(iota((depth, 128), 0) == cell_col[j : j + 1], 1.0, 0.0).astype(BF16)
    l_thermal.wait()
    high, low = pieces(thermal[...].reshape(cells, depth))
    hot = row_hot[...]
    found = dot(high, hot, ((0,), (0,))) + dot(low, hot, ((0,), (0,)))
    value = jnp.sum(found * col_hot[...].astype(F32), axis=0, keepdims=True)
    value = jnp.concatenate([value[:, j * 128 : (j + 1) * 128] for j in range(lines)], axis=0)
    l_part.wait()
    l_factor.wait()
    owned = jnp.where(part[...] == group, 1.0, 0.0)
    picked[0:lines] = jnp.where(solid, value, value * owned)
    picked[lines:] = jnp.zeros((8 - lines, 128), F32)

    pl.semaphore_wait(barrier, inner - 1 + n_far - 1 + has_up.astype(jnp.int32) + has_down.astype(jnp.int32))

    def wall_copy(g):
        return pltpu.make_async_remote_copy(
            picked, walls, contact_send.at[g], contact_recv.at[groups - 1], device_id=(g, brick), device_id_type=MESH
        )

    near_copy = pltpu.make_async_remote_copy(
        picked, nears.at[group], contact_send.at[0], contact_recv.at[group], device_id=(groups - 1, brick), device_id_type=MESH
    )

    @pl.when(solid)
    def _():
        for g in range(groups - 1):
            wall_copy(g).start()

    @pl.when(fluid)
    def _():
        near_copy.start()

    l_opening.wait()
    l_flow.wait()
    l_weight.wait()
    coef_a = pltpu.make_async_remote_copy(
        ax.at[rows], ax.at[0], coef_send.at[0], coef_recv.at[0], device_id=up, device_id_type=MESH
    )
    coef_g = pltpu.make_async_remote_copy(
        gx.at[rows], gx.at[0], coef_send.at[1], coef_recv.at[1], device_id=up, device_id_type=MESH
    )
    coef_up = pltpu.make_async_remote_copy(
        weight.at[rows - 1], weight_low, coef_send.at[0], coef_recv.at[0], device_id=up, device_id_type=MESH
    )
    coef_down = pltpu.make_async_remote_copy(
        weight.at[0], weight_up, coef_send.at[1], coef_recv.at[1], device_id=down, device_id_type=MESH
    )

    @pl.when(fluid)
    def _():
        last = jnp.where(at_top, 0.0, opening[0, rows - 1])
        ax[rows] = last
        gx[rows] = last * (1.0 + flow[0, rows - 1])

    @pl.when(fluid & has_up)
    def _():
        coef_a.start()
        coef_g.start()

    @pl.when(solid & has_up)
    def _():
        coef_up.start()

    @pl.when(solid & has_down)
    def _():
        coef_down.start()

    l_storage.wait()
    l_root.wait()
    l_rigid.wait()

    def spread(values):
        flat = jnp.concatenate([values[j : j + 1] for j in range(lines)], axis=1)
        high, low = pieces(flat)
        cols = col_hot[...].astype(F32)
        return dot(row_hot[...], (cols * high.astype(F32)).astype(BF16), ((1,), (1,))) + dot(
            row_hot[...], (cols * low.astype(F32)).astype(BF16), ((1,), (1,))
        )

    def fold(x, op):
        y = x.reshape(width // 8, 8, depth)
        return op(y, axis=0)

    y_at, z_at = iota(plane, 0), iota(plane, 1)

    def write_stats(d_max, d_min, o_sum):
        lane = iota((1, 128), 1)
        tile = jnp.where(lane == 0, greatest(d_max), jnp.where(lane == 1, greatest(-d_min), jnp.where(lane == 2, total(o_sum), 0.0)))
        near_slots[0, low_id] = tile

    start = (jnp.full((8, depth), -1e30, F32), jnp.full((8, depth), 1e30, F32), jnp.zeros((8, depth), F32))

    @pl.when(fluid)
    def _():
        extra = spread(factor[...] * owned).reshape(rows, width, depth)
        storage[...] = storage[...] + extra

        def second(r, carry):
            d_max, d_min, o_sum = carry
            a_y = jnp.where(y_at == width - 1, 0.0, opening[1, r])
            g_y = a_y * (1.0 + flow[1, r])
            g_low = pltpu.roll(g_y, 1, 0)
            uy[r] = a_y
            ly[r] = g_low
            a_x = jnp.where(at_top & (r == rows - 1), 0.0, opening[0, r])
            g_x = a_x * (1.0 + flow[0, r])

            @pl.when(r < rows - 1)
            def _():
                ax[r + 1] = a_x
                gx[r + 1] = g_x

            d = storage[r] + g_x + g_y + pltpu.roll(a_y, 1, 0)
            o = a_x + g_x + a_y + g_low
            a_z = jnp.where(z_at == depth - 1, 0.0, opening[2, r])
            g_z = a_z * (1.0 + flow[2, r])
            g_low = pltpu.roll(g_z, 1, 1)
            uz[r] = a_z
            lz[r] = g_low
            d = d + g_z + pltpu.roll(a_z, 1, 1)
            o = o + a_z + g_low
            d = d + jnp.where(r == 0, 0.0, opening[0, jnp.maximum(r - 1, 0)])
            diag[r] = d
            return jnp.maximum(d_max, fold(d, jnp.max)), jnp.minimum(d_min, fold(d, jnp.min)), o_sum + fold(o, jnp.sum)

        write_stats(*lax.fori_loop(0, rows, second, start))

    @pl.when(solid)
    def _():
        eye = iota((8, 8), 0) == iota((8, 8), 1)
        both = rigidity[0] + rigidity[1] + rigidity[2]
        size = jnp.abs(rigidity[0]) + jnp.abs(rigidity[1]) + jnp.abs(rigidity[2])
        trace = total(jnp.where(eye, both, 0.0)) * (1.0 / 8)
        off = total(jnp.where(eye, 0.0, size)) * (1.0 / 8)
        block_z = jnp.where(iota((8, depth), 1) % 8 == iota((8, depth), 0), 1.0, 0.0)
        spread_z = lax.dot_general(
            lax.dot_general(block_z, rigidity[2], (((0,), (1,)), ((), ())), precision=HIGH, preferred_element_type=F32),
            block_z,
            (((1,), (0,)), ((), ())),
            precision=HIGH,
            preferred_element_type=F32,
        )
        same = (iota((depth, depth), 0) // 8) == (iota((depth, depth), 1) // 8)
        high, low = pieces(jnp.where(same, spread_z, 0.0))
        wz[0], wz[1] = high, low
        outer_x = jnp.where(iota((8, 64), 1) // 8 == iota((8, 64), 0), 1.0, 0.0)
        inner_y = jnp.where(iota((8, 64), 1) % 8 == iota((8, 64), 0), 1.0, 0.0)

        def expand(matrix, hot):
            left = lax.dot_general(hot, matrix, (((0,), (0,)), ((), ())), precision=HIGH, preferred_element_type=F32)
            return lax.dot_general(left, hot, (((1,), (0,)), ((), ())), precision=HIGH, preferred_element_type=F32)

        same_y = iota((64, 64), 0) % 8 == iota((64, 64), 1) % 8
        same_x = iota((64, 64), 0) // 8 == iota((64, 64), 1) // 8
        mixed = jnp.where(same_y, expand(rigidity[0], outer_x), 0.0) + jnp.where(same_x, expand(rigidity[1], inner_y), 0.0)
        high, low = pieces(mixed)
        wxy[...] = jnp.concatenate([high, high, low], axis=1)

        def second(r, carry):
            d_max, d_min, o_sum = carry
            w = weight[r]
            b_y = jnp.where((y_at % 8 == 7) & (y_at < width - 1), 0.5 * (w + pltpu.roll(w, width - 1, 0)), 0.0)
            b_low = pltpu.roll(b_y, 1, 0)
            uy[r] = b_y
            ly[r] = b_low
            pair = b_y + b_low
            b_z = jnp.where((z_at % 8 == 7) & (z_at < depth - 1), 0.5 * (w + pltpu.roll(w, depth - 1, 1)), 0.0)
            b_low = pltpu.roll(b_z, 1, 1)
            uz[r] = b_z
            lz[r] = b_low
            pair = pair + b_z + b_low
            d = storage[r] + pair
            diag[r] = d
            square = root[r] * root[r]
            whole = d + square * trace
            o = pair + square * off
            return jnp.maximum(d_max, fold(whole, jnp.max)), jnp.minimum(d_min, fold(whole, jnp.min)), o_sum + fold(o, jnp.sum)

        write_stats(*lax.fori_loop(0, rows, second, start))

    def near_start(which):
        for o, (peer, where) in enumerate(near_peers):
            pltpu.make_async_remote_copy(
                near_slots.at[which, low_id],
                near_slots.at[which, low_id],
                near_send.at[which, o],
                near_recv.at[which, low_id],
                device_id=where,
                device_id_type=MESH,
            ).start()

    def near_wait(which):
        for o, (peer, where) in enumerate(near_peers):
            copy = pltpu.make_async_remote_copy(
                near_slots.at[which, peer],
                near_slots.at[which, peer],
                near_send.at[which, o],
                near_recv.at[which, peer],
                device_id=where,
                device_id_type=MESH,
            )
            copy.wait_recv()
            copy.wait_send()

    def far_start(which):
        for o, (peer, where) in enumerate(far_peers):
            pltpu.make_async_remote_copy(
                far_slots.at[which, high_id],
                far_slots.at[which, high_id],
                far_send.at[which, o],
                far_recv.at[which, high_id],
                device_id=where,
                device_id_type=MESH,
            ).start()

    def far_wait(which):
        for o, (peer, where) in enumerate(far_peers):
            copy = pltpu.make_async_remote_copy(
                far_slots.at[which, peer],
                far_slots.at[which, peer],
                far_send.at[which, o],
                far_recv.at[which, peer],
                device_id=where,
                device_id_type=MESH,
            )
            copy.wait_recv()
            copy.wait_send()

    def merge_stats(tiles):
        lane = iota((1, 128), 1)
        most, summed = tiles[0], tiles[0]
        for tile in tiles[1:]:
            most, summed = jnp.maximum(most, tile), summed + tile
        return jnp.where(lane == 2, summed, most)

    near_start(0)

    l_forcing.wait()

    part_rows = width // PARTS

    def halo_up(k, j):
        span = pl.ds(j * part_rows, part_rows)
        at = RAW.get(k, k)
        return pltpu.make_async_remote_copy(
            basis.at[at, rows, span],
            basis.at[at, 0, span],
            halo_send.at[k, 0, j],
            halo_recv.at[k, 0, j],
            device_id=up,
            device_id_type=MESH,
        )

    def halo_down(k, j):
        span = pl.ds(j * part_rows, part_rows)
        at = RAW.get(k, k)
        return pltpu.make_async_remote_copy(
            basis.at[at, 1, span],
            basis.at[at, rows + 1, span],
            halo_send.at[k, 1, j],
            halo_recv.at[k, 1, j],
            device_id=down,
            device_id_type=MESH,
        )

    def linked(k):
        if k in SKIP:
            return has_up & jnp.logical_not(far_up), has_down & jnp.logical_not(far_down)
        return has_up, has_down

    def send_halos(k, j):
        to_up, to_down = linked(k)

        @pl.when(to_up)
        def _():
            halo_up(k, j).start()

        @pl.when(to_down)
        def _():
            halo_down(k, j).start()

    def deep_up(i):
        return pltpu.make_async_remote_copy(
            basis.at[RAW.get(DEEP[i], DEEP[i]), rows - 1], second.at[0, i], deep_send.at[i, 0], deep_recv.at[i, 0], device_id=up, device_id_type=MESH
        )

    def deep_down(i):
        return pltpu.make_async_remote_copy(
            basis.at[RAW.get(DEEP[i], DEEP[i]), 2], second.at[1, i], deep_send.at[i, 1], deep_recv.at[i, 1], device_id=down, device_id_type=MESH
        )

    def ghost_up(i):
        source = (ghost_diag.at[0], uy.at[rows - 1], ly.at[rows - 1], uz.at[rows - 1], lz.at[rows - 1], gx.at[rows - 1])[i]
        return pltpu.make_async_remote_copy(
            source, ghost.at[0, i], ghost_send.at[0, i], ghost_recv.at[0, i], device_id=up, device_id_type=MESH
        )

    def ghost_down(i):
        source = (ghost_diag.at[1], uy.at[0], ly.at[0], uz.at[0], lz.at[0], ax.at[1])[i]
        return pltpu.make_async_remote_copy(
            source, ghost.at[1, i], ghost_send.at[1, i], ghost_recv.at[1, i], device_id=down, device_id_type=MESH
        )

    def send_deep(i):
        @pl.when(far_up)
        def _():
            deep_up(i).start()

        @pl.when(far_down)
        def _():
            deep_down(i).start()

    @pl.when(fluid)
    def _():
        pltpu.make_async_remote_copy(
            picked, walls, contact_send.at[0], contact_recv.at[groups - 1], device_id=(groups - 1, brick), device_id_type=MESH
        ).wait_recv()

    @pl.when(solid)
    def _():
        for g in range(groups - 1):
            pltpu.make_async_remote_copy(
                picked, nears.at[g], contact_send.at[g], contact_recv.at[g], device_id=(g, brick), device_id_type=MESH
            ).wait_recv()
        walls[...] = nears[0] + nears[1] + nears[2] - picked[...]

    heat = factor[...] * walls[0:lines]
    extra = spread(jnp.where(solid, heat, heat * owned)).reshape(rows, width, depth)
    basis[0, 1 : rows + 1] = forcing[...] + extra
    for j in range(PARTS):
        send_halos(0, j)
    send_deep(0)

    @pl.when(at_bottom)
    def _():
        gx[0] = jnp.zeros(plane, F32)

    @pl.when(fluid & has_down)
    def _():
        coef_a.wait_recv()
        coef_g.wait_recv()
        diag[0] = diag[0] + ax[0]

    @pl.when(solid & has_down)
    def _():
        coef_up.wait_recv()
        gx[0] = 0.5 * (weight_low[...] + weight[0])
        diag[0] = diag[0] + gx[0]

    @pl.when(solid & has_up)
    def _():
        coef_down.wait_recv()
        ax[rows] = 0.5 * (weight[rows - 1] + weight_up[...])
        diag[rows - 1] = diag[rows - 1] + ax[rows]

    @pl.when(solid & at_top)
    def _():
        ax[rows] = jnp.zeros(plane, F32)

    def gram_sums(k, low, high, accs):
        def body(r, accs):
            accs = list(accs)
            for j in range(width // 8):
                span = slice(8 * j, 8 * j + 8)
                mine = basis[k, r + 1, span, :]
                for i in range(k + 1):
                    other = mine if i == k else basis[i, r + 1, span, :]
                    accs[i] = accs[i] + mine * other
            return tuple(accs)

        return lax.fori_loop(low, high, body, accs)

    def gram_none(k):
        return tuple(jnp.zeros((8, depth), F32) for _ in range(k + 1))

    def gram_keep(k, accs):
        lane = iota((1, 128), 1)
        tile = jnp.zeros((1, 128), F32) if k == 0 else gram_tile[...]
        for i in range(k + 1):
            spot = (lane == i * SIDE + k) | (lane == k * SIDE + i)
            tile = jnp.where(spot, total(accs[i]), tile)
        gram_tile[...] = tile

    def gram_row(k):
        gram_keep(k, gram_sums(k, 0, rows, gram_none(k)))

    def local(r, v):
        return (
            diag[r] * v
            - uy[r] * pltpu.roll(v, width - 1, 0)
            - ly[r] * pltpu.roll(v, 1, 0)
            - uz[r] * pltpu.roll(v, depth - 1, 1)
            - lz[r] * pltpu.roll(v, 1, 1)
        )

    def apply(k, scale):
        at, to = (RAW.get(k, k), RAW[k + 1]) if scale is None else (k, k + 1)

        def keep(r, q):
            if scale is None:
                basis[to, r + 1] = q
            else:
                basis[to, r + 1] = scale * q - basis[k - 1, r + 1]

        @pl.when(fluid)
        def _():
            def middle(r, carry):
                v = basis[at, r + 1]
                keep(r, local(r, v) - gx[r] * basis[at, r] - ax[r + 1] * basis[at, r + 2])
                return carry

            keep(0, local(0, basis[at, 1]) - ax[1] * basis[at, 2])
            keep(rows - 1, local(rows - 1, basis[at, rows]) - gx[rows - 1] * basis[at, rows - 1])
            lax.fori_loop(1, rows - 1, middle, 0)

        @pl.when(solid)
        def _():
            for e in range(width // 8):
                u = (root[:, 8 * e : 8 * e + 8, :] * basis[at, 1 : rows + 1, 8 * e : 8 * e + 8, :]).reshape(64, depth)
                high, low = pieces(u)
                uh[e], ul[e] = high, low
                stiff[e] = dot(wxy[...], jnp.concatenate([high, low, high], axis=0), ((1,), (0,)))
            high, low = uh[...].reshape(cells, depth), ul[...].reshape(cells, depth)
            along = dot(high, wz[0], ((1,), (0,))) + dot(low, wz[0], ((1,), (0,))) + dot(high, wz[1], ((1,), (0,)))
            stiff[...] = stiff[...] + along.reshape(width // 8, 64, depth)

            def each(r, carry):
                force = stiff[:, pl.ds(r * 8, 8), :].reshape(width, depth)
                keep(r, local(r, basis[at, r + 1]) + root[r] * force)
                return carry

            lax.fori_loop(0, rows, each, 0)

    def finish(k, scale, mix=None):
        at, to = RAW.get(k, k), (RAW[k + 1] if scale is None else k + 1)
        for j in range(PARTS):
            span = slice(j * part_rows, (j + 1) * part_rows)

            from_up, from_down = linked(k)

            @pl.when(from_down)
            def _():
                halo_up(k, j).wait_recv()

            @pl.when(from_up)
            def _():
                halo_down(k, j).wait_recv()

            for own, halo, coef in ((1, 0, gx.at[0]), (rows, rows + 1, ax.at[rows])):
                value = basis[at, halo, span]
                if mix is not None:
                    value = mix[0] * value + mix[1] * basis[RAW[1], halo, span] + mix[2] * basis[0, halo, span]
                    basis[k, halo, span] = value
                value = coef[span] * value
                if scale is not None:
                    value = scale * value
                basis[to, own, span] = basis[to, own, span] - value
            if k + 1 < ITERS:
                send_halos(k + 1, j)

    def extend(i):
        k = DEEP[i]
        fresh = range(i + 1) if k == 2 else (i,)

        def row(side, near, halo, inward):
            v = basis[k, halo]
            if k == 2:
                outer_row = mix[0] * second[side, 2] + mix[1] * second[side, 1] + mix[2] * second[side, 0]
                older = (basis[RAW[1], halo] - center * basis[0, halo]) * inv_e
            else:
                outer_row, older = second[side, i], basis[k - 1, halo]
            q = (
                (ghost[side, 0] - center) * v
                - ghost[side, 1] * pltpu.roll(v, width - 1, 0)
                - ghost[side, 2] * pltpu.roll(v, 1, 0)
                - ghost[side, 3] * pltpu.roll(v, depth - 1, 1)
                - ghost[side, 4] * pltpu.roll(v, 1, 1)
                - ghost[side, 5] * outer_row
                - inward * basis[k, near]
            )
            basis[k + 1, halo] = scale * q - older

        @pl.when(far_down)
        def _():
            for n in fresh:
                deep_up(n).wait_recv()
            if k == 2:
                for n in range(6):
                    ghost_up(n).wait_recv()
            row(0, 1, 0, ax[0])

        @pl.when(far_up)
        def _():
            for n in fresh:
                deep_down(n).wait_recv()
            if k == 2:
                for n in range(6):
                    ghost_down(n).wait_recv()
            row(1, rows, rows + 1, gx[rows])

    apply(0, None)
    send_deep(1)
    near_wait(0)
    far_slots[0, high_id] = merge_stats([near_slots[0, i] for i in range(inner)])
    far_start(0)
    finish(0, None)

    @pl.when(far_up)
    def _():
        ghost_diag[0] = diag[rows - 1]
        for n in range(6):
            ghost_up(n).start()

    @pl.when(far_down)
    def _():
        ghost_diag[1] = diag[0]
        for n in range(6):
            ghost_down(n).start()

    apply(1, None)
    send_deep(2)
    gram_row(0)
    finish(1, None)
    far_wait(0)
    split = (groups - 1) * outer

    def interval(tiles, count, of_most, of_mean):
        stats = merge_stats(tiles)
        mean = stats[0:1, 2:3] * (1.0 / count)
        high = of_most * stats[0:1, 0:1] + of_mean * mean
        low = jnp.maximum(-stats[0:1, 1:2] - 0.5 * mean, 0.0)
        return 0.5 * (high + low), 0.5 * (high - low)

    c_fluid, e_fluid = interval([far_slots[0, i] for i in range(split)], float((groups - 1) * bricks * cells * depth), 0.9, 0.1)
    c_solid, e_solid = interval([far_slots[0, i] for i in range(split, n_far)], float(bricks * cells * depth), 0.97, 0.25)
    center = jnp.where(solid, c_solid, c_fluid)
    inv_e = 1.0 / jnp.where(solid, e_solid, e_fluid)
    scale = 2.0 * inv_e

    mix = (scale * inv_e, -2.0 * scale * center * inv_e, scale * inv_e * center * center - 1.0)

    def convert(r, carry):
        zero, one, two = basis[0, r + 1], basis[RAW[1], r + 1], basis[RAW[2], r + 1]
        basis[1, r + 1] = (one - center * zero) * inv_e
        basis[2, r + 1] = mix[0] * two + mix[1] * one + mix[2] * zero
        diag[r] = diag[r] - center
        return carry

    lax.fori_loop(0, rows, convert, 0)
    for k in range(2, ITERS):
        apply(k, scale)
        if k + 1 in DEEP:
            send_deep(DEEP.index(k + 1))
        if k == 2:
            gram_row(1)
        gram_row(k)
        if k + 1 == ITERS:
            last_sums = gram_sums(ITERS, 1, rows - 1, gram_none(ITERS))
        finish(k, scale, mix if k == 2 else None)
        if k + 1 in SKIP:
            extend(DEEP.index(k))
    last_sums = gram_sums(ITERS, rows - 1, rows, gram_sums(ITERS, 0, 1, last_sums))
    gram_keep(ITERS, last_sums)

    near_slots[1, low_id] = gram_tile[...]
    near_start(1)
    near_wait(1)
    summed = near_slots[1, 0]
    for i in range(1, inner):
        summed = summed + near_slots[1, i]
    far_slots[1, high_id] = summed
    far_start(1)

    @pl.when(solid)
    def _():
        for g in range(groups - 1):
            wall_copy(g).wait_send()

    @pl.when(fluid)
    def _():
        near_copy.wait_send()

    @pl.when(fluid & has_up)
    def _():
        coef_a.wait_send()
        coef_g.wait_send()

    @pl.when(solid & has_up)
    def _():
        coef_up.wait_send()

    @pl.when(solid & has_down)
    def _():
        coef_down.wait_send()

    @pl.when(far_up)
    def _():
        for n in range(6):
            ghost_up(n).wait_send()
        for i in range(len(DEEP)):
            deep_up(i).wait_send()

    @pl.when(far_down)
    def _():
        for n in range(6):
            ghost_down(n).wait_send()
        for i in range(len(DEEP)):
            deep_down(i).wait_send()

    for k in range(ITERS):
        sent_up, sent_down = linked(k)
        for j in range(PARTS):

            @pl.when(sent_up)
            def _():
                halo_up(k, j).wait_send()

            @pl.when(sent_down)
            def _():
                halo_down(k, j).wait_send()

    far_wait(1)
    gram_fluid = far_slots[1, 0]
    for i in range(1, split):
        gram_fluid = gram_fluid + far_slots[1, i]
    gram_solid = far_slots[1, split]
    for i in range(split + 1, n_far):
        gram_solid = gram_solid + far_slots[1, i]
    y_fluid, ok_fluid = projected(gram_fluid, c_fluid / e_fluid, True)
    y_solid, ok_solid = projected(gram_solid, c_solid / e_solid, False)
    coeffs = jnp.where(solid, y_solid, y_fluid) * inv_e
    flag[0] = jnp.max(ok_fluid * ok_solid).astype(jnp.int32)
    weights = [coeffs[k : k + 1, :1] for k in range(ITERS)]

    def combine(r, carry):
        acc = weights[0] * basis[0, r + 1]
        for k in range(1, ITERS):
            acc = acc + weights[k] * basis[k, r + 1]
        out[r] = acc
        return carry

    lax.fori_loop(0, rows, combine, 0)


def handed_on(result):
    def body(source, target, sem):
        copy = pltpu.make_async_copy(source, target, sem)
        copy.start()
        copy.wait()

    return pl.pallas_call(
        body,
        out_shape=jax.ShapeDtypeStruct(result.shape, result.dtype),
        in_specs=[pl.BlockSpec(memory_space=pltpu.VMEM)],
        out_specs=pl.BlockSpec(memory_space=pl.ANY),
        scratch_shapes=[pltpu.SemaphoreType.DMA],
        name="handed_on",
    )(pltpu.with_memory_space_constraint(result, pltpu.VMEM))


def shards(*arguments):
    groups, bricks = lax.axis_size("group"), lax.axis_size("brick")
    forcing = arguments[0]
    rows, width, depth = slab = forcing.shape
    lines = arguments[8].shape[0]
    points = lines * 128
    n_far = groups * (bricks // 8)
    vm = pltpu.VMEM
    scratch = (
        [vm(slab, F32)] * 3
        + [vm((3,) + slab, F32)] * 2
        + [vm(slab, F32)] * 2
        + [vm((3, 8, 8), F32)]
        + [vm((lines, 128), jnp.int32)] * 3
        + [vm((lines, 128), F32)]
        + [vm((ITERS + 3, rows + 2, width, depth), F32)]
        + [vm((rows + 1, width, depth), F32)] * 2
        + [vm(slab, F32)] * 5
        + [vm((width // 8, 64, depth), F32)]
        + [vm((width // 8, 64, depth), BF16)] * 2
        + [vm((2, depth, depth), BF16), vm((64, 192), BF16)]
        + [vm((width, depth), F32)] * 2
        + [vm((rows * width, points), BF16), vm((depth, points), BF16)]
        + [vm((8, 128), F32)] * 2
        + [vm((groups - 1, 8, 128), F32)]
        + [vm((1, 128), F32), vm((2, 8, 1, 128), F32), vm((2, n_far, 1, 128), F32)]
        + [vm((2, len(DEEP), width, depth), F32), vm((2, 6, width, depth), F32), vm((2, width, depth), F32)]
    )
    dma = pltpu.SemaphoreType.DMA
    semaphores = [
        dma((12,)),
        dma((ITERS, 2, PARTS)),
        dma((ITERS, 2, PARTS)),
        dma((2,)),
        dma((2,)),
        dma((groups,)),
        dma((groups,)),
        dma((2, 8)),
        dma((2, 8)),
        dma((2, n_far)),
        dma((2, n_far)),
        dma((len(DEEP), 2)),
        dma((len(DEEP), 2)),
        dma((2, 6)),
        dma((2, 6)),
    ]
    result, flag = pl.pallas_call(
        functools.partial(kernel, groups, bricks),
        out_shape=(pltpu.VMEM(slab, F32), jax.ShapeDtypeStruct((1,), jnp.int32)),
        in_specs=[pl.BlockSpec(memory_space=pl.ANY)] * 12,
        out_specs=(pl.BlockSpec(memory_space=pltpu.VMEM), pl.BlockSpec(memory_space=pltpu.SMEM)),
        scratch_shapes=scratch + semaphores,
        compiler_params=pltpu.CompilerParams(collective_id=0, has_side_effects=True, vmem_limit_bytes=56 * 2**20),
        name="coupled",
    )(*arguments)
    return lax.cond(flag[0] > 0, lambda: handed_on(result), lambda: iterated(*arguments))


def solution(mesh):
    return jax.shard_map(
        shards,
        mesh=mesh,
        in_specs=(
            P(("group", "brick"), None, None),
            P(("group", "brick"), None, None),
            P(("group", "brick"), None, None),
            P(None, ("group", "brick"), None, None),
            P(None, ("group", "brick"), None, None),
            P(("group", "brick"), None, None),
            P(("group", "brick"), None, None),
            P(),
            P("brick", None),
            P("brick", None),
            P("brick", None),
            P("brick", None),
        ),
        out_specs=P(("group", "brick"), None, None),
        check_vma=False,
    )
```

```python
import functools

import jax
import jax.numpy as jnp
from jax import lax
from jax.experimental import pallas as pl
from jax.experimental.pallas import tpu as pltpu
from jax.sharding import PartitionSpec as P

ITERS = 8


HIGH = lax.Precision.HIGHEST


def passed_along(value, axis, steps):
    count = lax.axis_size(axis)
    leading, last = (max(0, -steps), min(count, count - steps))
    return lax.ppermute(value, axis, [(source, source + steps) for source in range(leading, last)])


def extended(cells, sides, width):
    for axis, dim in sides:
        count = lax.axis_size(axis)
        ends = count - 1
        head = lax.slice_in_dim(cells, 0, width, axis=dim)
        tail = lax.slice_in_dim(cells, cells.shape[dim] - width, cells.shape[dim], axis=dim)
        cells = jnp.concatenate(
            [
                lax.ppermute(tail, axis, [(i, (i + 1) % count) for i in range(ends)]),
                cells,
                lax.ppermute(head, axis, [((i + 1) % count, i) for i in range(ends)]),
            ],
            axis=dim,
        )
    return cells


def shift_next(v, axis):
    size = v.shape[axis]
    inner = lax.slice_in_dim(v, 1, size, axis=axis)
    zero = jnp.zeros_like(lax.slice_in_dim(v, 0, 1, axis=axis))
    return jnp.concatenate([inner, zero], axis=axis)


def shift_prev(v, axis):
    size = v.shape[axis]
    inner = lax.slice_in_dim(v, 0, size - 1, axis=axis)
    zero = jnp.zeros_like(lax.slice_in_dim(v, 0, 1, axis=axis))
    return jnp.concatenate([zero, inner], axis=axis)


def open_faces(shape, axis):
    index = lax.broadcasted_iota(jnp.int32, shape, axis)
    return (index < shape[axis] - 1).astype(jnp.float32)


def element_faces(shape, axis, nodes):
    index = lax.broadcasted_iota(jnp.int32, shape, axis)
    inside = (index % nodes == nodes - 1) & (index < shape[axis] - 1)
    return inside.astype(jnp.float32)


def stiffness_apply(u, rigidity_matrix):
    nodes = rigidity_matrix.shape[1]
    rows, width, depth = u.shape
    block = min(depth, 128)
    along_x = jnp.einsum("pq,qyz->pyz", rigidity_matrix[0], u, precision=HIGH)
    split_y = u.reshape(rows, width // nodes, nodes, depth)
    along_y = jnp.einsum("pq,xeqz->xepz", rigidity_matrix[1], split_y, precision=HIGH).reshape(
        rows, width, depth
    )
    wide = jnp.kron(jnp.eye(block // nodes, dtype=jnp.float32), rigidity_matrix[2])
    split_z = u.reshape(rows, width, depth // block, block)
    along_z = jnp.einsum("xyeq,pq->xyep", split_z, wide, precision=HIGH).reshape(rows, width, depth)
    return along_x + along_y + along_z


def least_squares(hess, beta):
    gram = jnp.dot(hess.T, hess, precision=HIGH)
    lower = jnp.linalg.cholesky(gram)
    right = (beta * hess[0])[:, None]
    middle = lax.linalg.triangular_solve(lower, right, left_side=True, lower=True)
    coeffs = lax.linalg.triangular_solve(
        lower, middle, left_side=True, lower=True, transpose_a=True
    )
    return coeffs[:, 0]


def iterated(
    forcing_vector,
    thermal_iterate,
    storage_over_step,
    opening_shares,
    flow_speed,
    diffusivity_root,
    sanction_weight,
    rigidity_matrix,
    contact_fluid_part,
    contact_fluid_volume,
    contact_solid_vertex,
    exchange_rate_factor,
):
    groups = lax.axis_size("group")
    bricks = lax.axis_size("brick")
    group_id = lax.axis_index("group")
    brick_id = lax.axis_index("brick")
    solid = group_id == groups - 1
    solid_flag = solid.astype(jnp.float32)
    fluid_flag = 1.0 - solid_flag
    rows, width, depth = forcing_vector.shape
    nodes = rigidity_matrix.shape[1]
    device = group_id * bricks + brick_id
    first_solid = (groups - 1) * bricks
    unrolled_array = thermal_iterate.reshape(-1)
    owned = (contact_fluid_part == group_id).astype(jnp.float32)
    target = jnp.where(solid, contact_solid_vertex, contact_fluid_volume).reshape(-1)
    picked = unrolled_array[target].reshape(contact_solid_vertex.shape)
    wall, near = lax.psum((picked * solid_flag, picked * owned * fluid_flag), "group")
    extra_rhs = jnp.where(
        solid, exchange_rate_factor * (near - wall), exchange_rate_factor * wall * owned
    )
    extra_diag = exchange_rate_factor * owned * fluid_flag
    rhs = (
        forcing_vector.reshape(-1)
        .at[target]
        .add(extra_rhs.reshape(-1))
        .reshape(forcing_vector.shape)
    )
    fluid_diag = (
        storage_over_step.reshape(-1)
        .at[target]
        .add(extra_diag.reshape(-1))
        .reshape(forcing_vector.shape)
    )
    shape = (rows, width, depth)
    global_row = device * rows + lax.broadcasted_iota(jnp.int32, shape, 0)
    face_x = opening_shares[0] * (global_row != first_solid * rows - 1).astype(jnp.float32)
    face_y = opening_shares[1] * open_faces(shape, 1)
    face_z = opening_shares[2] * open_faces(shape, 2)
    rims = passed_along(
        jnp.stack([face_x[-1], flow_speed[0][-1], sanction_weight[-1]]), ("group", "brick"), 1
    )
    face_low = rims[0]
    speed_low = rims[1]
    weight_low = rims[2]
    pair_low = 0.5 * (weight_low + sanction_weight[0]) * (device != first_solid).astype(jnp.float32)
    pair_up = passed_along(pair_low, "brick", -1)
    pair_y = (
        0.5 * (sanction_weight + shift_next(sanction_weight, 1)) * element_faces(shape, 1, nodes)
    )
    pair_z = (
        0.5 * (sanction_weight + shift_next(sanction_weight, 2)) * element_faces(shape, 2, nodes)
    )
    local_square = jnp.sum(rhs * rhs)
    solution = jnp.zeros_like(rhs)
    resid = rhs
    columns = []
    fluid_square, solid_square = lax.psum(
        (local_square * fluid_flag, local_square * solid_flag), ("group", "brick")
    )
    beta = jnp.sqrt(fluid_square)
    basis = [rhs / beta]
    direction = rhs
    norm_now = solid_square
    for step in range(ITERS):
        vector = jnp.where(solid, direction, basis[step])
        padded = extended(vector, ((("group", "brick"), 0),), 1)
        below = padded[0]
        above = padded[-1]

        def fluid_branch(unused):
            following = jnp.concatenate([vector[1:], above[None]], axis=0)
            flux_x = face_x * ((1.0 + flow_speed[0]) * vector - following)
            flux_low = face_low * ((1.0 + speed_low) * below - vector[0])
            out = (
                fluid_diag * vector
                + flux_x
                - jnp.concatenate([flux_low[None], flux_x[:-1]], axis=0)
            )
            flux_y = face_y * ((1.0 + flow_speed[1]) * vector - shift_next(vector, 1))
            flux_z = face_z * ((1.0 + flow_speed[2]) * vector - shift_next(vector, 2))
            return out + flux_y - shift_prev(flux_y, 1) + flux_z - shift_prev(flux_z, 2)

        def solid_branch(unused):
            out = storage_over_step * vector + diffusivity_root * stiffness_apply(
                diffusivity_root * vector, rigidity_matrix
            )
            jump_up = pair_up * (vector[-1] - above)
            jump_low = pair_low * (below - vector[0])
            out = out.at[0].add(-jump_low).at[rows - 1].add(jump_up)
            jump_y = pair_y * (vector - shift_next(vector, 1))
            jump_z = pair_z * (vector - shift_next(vector, 2))
            return out + jump_y - shift_prev(jump_y, 1) + jump_z - shift_prev(jump_z, 2)

        image = lax.cond(solid, solid_branch, fluid_branch, 0)
        inner = jnp.stack([jnp.sum(basis[j] * image) for j in range(step + 1)])
        heights, curvature = lax.psum(
            (inner * fluid_flag, jnp.sum(direction * image) * solid_flag), ("group", "brick")
        )
        fresh = image
        for j in range(step + 1):
            fresh = fresh - heights[j] * basis[j]
        alpha = norm_now / curvature
        solution = solution + alpha * direction
        resid = resid - alpha * image
        fresh_square, norm_next = lax.psum(
            (jnp.sum(fresh * fresh) * fluid_flag, jnp.sum(resid * resid) * solid_flag),
            ("group", "brick"),
        )
        length = jnp.sqrt(fresh_square)
        basis.append(fresh / length)
        columns.append(
            jnp.concatenate([heights, length[None], jnp.zeros((ITERS - 1 - step,), jnp.float32)])
        )
        direction = resid + norm_next / norm_now * direction
        norm_now = norm_next
    coeffs = least_squares(jnp.stack(columns, axis=1), beta)
    fluid_new = jnp.zeros_like(rhs)
    for step in range(ITERS):
        fluid_new = fluid_new + coeffs[step] * basis[step]
    return jnp.where(solid, solution, fluid_new)


F32 = jnp.float32
BF16 = jnp.bfloat16
MESH = pl.DeviceIdType.MESH
PIVOT_LEAST = 1e-4
REFINE_MOST = 4e-3
PARTS = 8
SIDE = ITERS + 1
RAW = {1: ITERS + 1, 2: ITERS + 2}
DEEP = (0, 1, 2, 4, 6)
SKIP = (3, 5, 7)


def iota(shape, dim):
    return lax.broadcasted_iota(jnp.int32, shape, dim)


def pieces(x):
    high = x.astype(BF16)
    return high, (x - high.astype(F32)).astype(BF16)


def total(x):
    return jnp.sum(jnp.sum(x, axis=0, keepdims=True), axis=1, keepdims=True)


def greatest(x):
    return jnp.max(jnp.max(x, axis=0, keepdims=True), axis=1, keepdims=True)


def dot(a, b, dims):
    return lax.dot_general(a, b, ((dims[0], dims[1]), ((), ())), preferred_element_type=F32)


def shift_rows(x, gamma):
    size = x.shape[0]
    after = pltpu.roll(x, size - 1, 0)
    row = iota(x.shape, 0)
    out = gamma * x + 0.5 * (pltpu.roll(x, 1, 0) + after) + jnp.where(row == 0, 0.5 * after, 0.0)
    return jnp.where(row < ITERS, out, 0.0)


def shift_lanes(x, gamma):
    size = x.shape[1]
    after = pltpu.roll(x, size - 1, 1)
    lane = iota(x.shape, 1)
    out = gamma * x + 0.5 * (pltpu.roll(x, 1, 1) + after) + jnp.where(lane == 0, 0.5 * after, 0.0)
    return jnp.where(lane < ITERS, out, 0.0)


def projected(flat, gamma, fluid):
    shape = (16, 128)
    row, lane = iota(shape, 0), iota(shape, 1)
    gram = jnp.zeros(shape, F32)
    for i in range(SIDE):
        line = flat if i == 0 else pltpu.roll(flat, 128 - SIDE * i, 1)
        gram = jnp.where((row == i) & (lane < SIDE), line, gram)
    wide = shift_lanes(gram, gamma)
    if fluid:
        normal, right = shift_rows(wide, gamma), shift_rows(gram, gamma)
    else:
        normal, right = jnp.where(row < ITERS, wide, 0.0), jnp.where(row < ITERS, gram, 0.0)
    table = jnp.where(lane < ITERS, normal, 0.0)
    table = jnp.where((lane == row + 8) & (row < ITERS), 1.0, table)
    table = jnp.where(lane == 16, pltpu.roll(right, 16, 1), table)
    margin = None
    for k in range(ITERS):
        pivot = table[k : k + 1, k : k + 1]
        spare = pivot - PIVOT_LEAST * normal[k : k + 1, k : k + 1]
        margin = spare if margin is None else jnp.minimum(margin, spare)
        scaled = table[k : k + 1, :] * (1.0 / pivot)
        column = jnp.where(row[:, :1] == k, 0.0, table[:, k : k + 1])
        table = jnp.where(row == k, scaled, table - column * scaled)
    coeffs = jnp.broadcast_to(table[:, 16:17], shape)
    inverse = jnp.where(lane < ITERS, pltpu.roll(table, shape[1] - 8, 1), 0.0)
    applied = gamma * coeffs + 0.5 * (pltpu.roll(coeffs, 1, 0) + pltpu.roll(coeffs, shape[0] - 1, 0))
    applied = applied + jnp.where(row == 1, 0.5 * pltpu.roll(coeffs, 1, 0), 0.0)
    rest = jnp.where(row == 0, 1.0, 0.0) - applied
    image = jnp.broadcast_to(jnp.sum(gram * rest, axis=0, keepdims=True), shape)
    image = shift_lanes(image, gamma) if fluid else jnp.where(lane < ITERS, image, 0.0)
    change = jnp.sum(inverse * image, axis=1, keepdims=True)
    coeffs = coeffs[:, :1] + change
    size = jnp.sum(jnp.abs(coeffs), axis=0, keepdims=True)
    moved = jnp.sum(jnp.abs(change), axis=0, keepdims=True)
    good = (margin > 0.0) & (moved < REFINE_MOST * size)
    return coeffs, jnp.where(good, 1.0, 0.0)


def ring_far(step, size):
    return min(step, size - step)


def kernel(
    groups,
    bricks,
    forcing_hbm,
    thermal_hbm,
    storage_hbm,
    opening_hbm,
    flow_hbm,
    root_hbm,
    weight_hbm,
    rigidity_hbm,
    part_hbm,
    volume_hbm,
    vertex_hbm,
    factor_hbm,
    out,
    flag,
    thermal,
    forcing,
    storage,
    opening,
    flow,
    root,
    weight,
    rigidity,
    part,
    volume,
    vertex,
    factor,
    basis,
    ax,
    gx,
    diag,
    uy,
    ly,
    uz,
    lz,
    stiff,
    uh,
    ul,
    wz,
    wxy,
    weight_low,
    weight_up,
    row_hot,
    col_hot,
    picked,
    walls,
    nears,
    gram_tile,
    near_slots,
    far_slots,
    second,
    ghost,
    ghost_diag,
    load_sem,
    halo_send,
    halo_recv,
    coef_send,
    coef_recv,
    contact_send,
    contact_recv,
    near_send,
    near_recv,
    far_send,
    far_recv,
    deep_send,
    deep_recv,
    ghost_send,
    ghost_recv,
):
    group = lax.axis_index("group")
    brick = lax.axis_index("brick")
    rows, width, depth = forcing.shape
    plane = (width, depth)
    cells = rows * width
    solid = group == groups - 1
    fluid = group != groups - 1
    inner, outer = 8, bricks // 8
    low_id = lax.rem(brick, inner)
    high_id = group * outer + brick // inner
    n_far = groups * outer
    at_top = (brick == bricks - 1) & (group >= groups - 2)
    at_bottom = (brick == 0) & ((group == 0) | (group == groups - 1))
    has_up, has_down = jnp.logical_not(at_top), jnp.logical_not(at_bottom)
    far_up = (brick == bricks - 1) & (group < groups - 2)
    far_down = (brick == 0) & (group > 0) & fluid
    device = group * bricks + brick
    up_id = lax.rem(device + 1, groups * bricks)
    down_id = lax.rem(device + groups * bricks - 1, groups * bricks)
    up = (up_id // bricks, lax.rem(up_id, bricks))
    down = (down_id // bricks, lax.rem(down_id, bricks))

    names = [
        (vertex_hbm, vertex),
        (volume_hbm, volume),
        (thermal_hbm, thermal),
        (part_hbm, part),
        (factor_hbm, factor),
        (opening_hbm, opening),
        (flow_hbm, flow),
        (storage_hbm, storage),
        (weight_hbm, weight),
        (root_hbm, root),
        (rigidity_hbm, rigidity),
        (forcing_hbm, forcing),
    ]
    loads = [pltpu.make_async_copy(s, d, load_sem.at[i]) for i, (s, d) in enumerate(names)]
    for load in loads[:3]:
        load.start()
    (l_vertex, l_volume, l_thermal, l_part, l_factor, l_opening, l_flow, l_storage, l_weight, l_root, l_rigid, l_forcing) = loads

    plane_id = brick // inner
    near_peers, far_peers = [], []
    for dz, dc in sorted(((a, b) for a in range(inner // 2) for b in range(2)), key=lambda at: -ring_far(at[0], inner // 2)):
        if dz or dc:
            peer = lax.rem(low_id // 2 + dz, inner // 2) * 2 + lax.rem(low_id + dc, 2)
            near_peers.append((peer, (group, plane_id * inner + peer)))
    steps = sorted(
        ((a, b) for a in range(groups) for b in range(outer)), key=lambda at: -ring_far(at[0], groups) - ring_far(at[1], outer)
    )
    for dx, dy in steps:
        if dx or dy:
            x_id, y_id = lax.rem(group + dx, groups), lax.rem(plane_id + dy, outer)
            far_peers.append((x_id * outer + y_id, (x_id, y_id * inner + low_id)))

    barrier = pltpu.get_barrier_semaphore()
    for peer, where in far_peers + near_peers:
        pl.semaphore_signal(barrier, inc=1, device_id=where, device_id_type=MESH)

    @pl.when(has_up)
    def _():
        pl.semaphore_signal(barrier, inc=1, device_id=up, device_id_type=MESH)

    @pl.when(has_down)
    def _():
        pl.semaphore_signal(barrier, inc=1, device_id=down, device_id_type=MESH)

    for load in loads[3:]:
        load.start()

    @pl.when(at_bottom)
    def _():
        for k in range(ITERS):
            basis[RAW.get(k, k), 0] = jnp.zeros(plane, F32)

    @pl.when(at_top)
    def _():
        for k in range(ITERS):
            basis[RAW.get(k, k), rows + 1] = jnp.zeros(plane, F32)

    l_vertex.wait()
    l_volume.wait()
    target = jnp.where(solid, vertex[...], volume[...])
    cell_row, cell_col = target >> 8, target & 255
    lines = target.shape[0]
    points = lines * 128
    for j in range(lines):
        span = pl.ds(j * 128, 128)
        row_hot[:, span] = jnp.where(iota((cells, 128), 0) == cell_row[j : j + 1], 1.0, 0.0).astype(BF16)
        col_hot[:, span] = jnp.where(iota((depth, 128), 0) == cell_col[j : j + 1], 1.0, 0.0).astype(BF16)
    l_thermal.wait()
    high, low = pieces(thermal[...].reshape(cells, depth))
    hot = row_hot[...]
    found = dot(high, hot, ((0,), (0,))) + dot(low, hot, ((0,), (0,)))
    value = jnp.sum(found * col_hot[...].astype(F32), axis=0, keepdims=True)
    value = jnp.concatenate([value[:, j * 128 : (j + 1) * 128] for j in range(lines)], axis=0)
    l_part.wait()
    l_factor.wait()
    owned = jnp.where(part[...] == group, 1.0, 0.0)
    picked[0:lines] = jnp.where(solid, value, value * owned)
    picked[lines:] = jnp.zeros((8 - lines, 128), F32)

    pl.semaphore_wait(barrier, inner - 1 + n_far - 1 + has_up.astype(jnp.int32) + has_down.astype(jnp.int32))

    def wall_copy(g):
        return pltpu.make_async_remote_copy(
            picked, walls, contact_send.at[g], contact_recv.at[groups - 1], device_id=(g, brick), device_id_type=MESH
        )

    near_copy = pltpu.make_async_remote_copy(
        picked, nears.at[group], contact_send.at[0], contact_recv.at[group], device_id=(groups - 1, brick), device_id_type=MESH
    )

    @pl.when(solid)
    def _():
        for g in range(groups - 1):
            wall_copy(g).start()

    @pl.when(fluid)
    def _():
        near_copy.start()

    l_opening.wait()
    l_flow.wait()
    l_weight.wait()
    coef_a = pltpu.make_async_remote_copy(
        ax.at[rows], ax.at[0], coef_send.at[0], coef_recv.at[0], device_id=up, device_id_type=MESH
    )
    coef_g = pltpu.make_async_remote_copy(
        gx.at[rows], gx.at[0], coef_send.at[1], coef_recv.at[1], device_id=up, device_id_type=MESH
    )
    coef_up = pltpu.make_async_remote_copy(
        weight.at[rows - 1], weight_low, coef_send.at[0], coef_recv.at[0], device_id=up, device_id_type=MESH
    )
    coef_down = pltpu.make_async_remote_copy(
        weight.at[0], weight_up, coef_send.at[1], coef_recv.at[1], device_id=down, device_id_type=MESH
    )

    @pl.when(fluid)
    def _():
        last = jnp.where(at_top, 0.0, opening[0, rows - 1])
        ax[rows] = last
        gx[rows] = last * (1.0 + flow[0, rows - 1])

    @pl.when(fluid & has_up)
    def _():
        coef_a.start()
        coef_g.start()

    @pl.when(solid & has_up)
    def _():
        coef_up.start()

    @pl.when(solid & has_down)
    def _():
        coef_down.start()

    l_storage.wait()
    l_root.wait()
    l_rigid.wait()

    def spread(values):
        flat = jnp.concatenate([values[j : j + 1] for j in range(lines)], axis=1)
        high, low = pieces(flat)
        cols = col_hot[...].astype(F32)
        return dot(row_hot[...], (cols * high.astype(F32)).astype(BF16), ((1,), (1,))) + dot(
            row_hot[...], (cols * low.astype(F32)).astype(BF16), ((1,), (1,))
        )

    def fold(x, op):
        y = x.reshape(width // 8, 8, depth)
        return op(y, axis=0)

    y_at, z_at = iota(plane, 0), iota(plane, 1)

    def write_stats(d_max, d_min, o_sum):
        lane = iota((1, 128), 1)
        tile = jnp.where(lane == 0, greatest(d_max), jnp.where(lane == 1, greatest(-d_min), jnp.where(lane == 2, total(o_sum), 0.0)))
        near_slots[0, low_id] = tile

    start = (jnp.full((8, depth), -1e30, F32), jnp.full((8, depth), 1e30, F32), jnp.zeros((8, depth), F32))

    @pl.when(fluid)
    def _():
        extra = spread(factor[...] * owned).reshape(rows, width, depth)
        storage[...] = storage[...] + extra

        def second(r, carry):
            d_max, d_min, o_sum = carry
            a_y = jnp.where(y_at == width - 1, 0.0, opening[1, r])
            g_y = a_y * (1.0 + flow[1, r])
            g_low = pltpu.roll(g_y, 1, 0)
            uy[r] = a_y
            ly[r] = g_low
            a_x = jnp.where(at_top & (r == rows - 1), 0.0, opening[0, r])
            g_x = a_x * (1.0 + flow[0, r])

            @pl.when(r < rows - 1)
            def _():
                ax[r + 1] = a_x
                gx[r + 1] = g_x

            d = storage[r] + g_x + g_y + pltpu.roll(a_y, 1, 0)
            o = a_x + g_x + a_y + g_low
            a_z = jnp.where(z_at == depth - 1, 0.0, opening[2, r])
            g_z = a_z * (1.0 + flow[2, r])
            g_low = pltpu.roll(g_z, 1, 1)
            uz[r] = a_z
            lz[r] = g_low
            d = d + g_z + pltpu.roll(a_z, 1, 1)
            o = o + a_z + g_low
            d = d + jnp.where(r == 0, 0.0, opening[0, jnp.maximum(r - 1, 0)])
            diag[r] = d
            return jnp.maximum(d_max, fold(d, jnp.max)), jnp.minimum(d_min, fold(d, jnp.min)), o_sum + fold(o, jnp.sum)

        write_stats(*lax.fori_loop(0, rows, second, start))

    @pl.when(solid)
    def _():
        eye = iota((8, 8), 0) == iota((8, 8), 1)
        both = rigidity[0] + rigidity[1] + rigidity[2]
        size = jnp.abs(rigidity[0]) + jnp.abs(rigidity[1]) + jnp.abs(rigidity[2])
        trace = total(jnp.where(eye, both, 0.0)) * (1.0 / 8)
        off = total(jnp.where(eye, 0.0, size)) * (1.0 / 8)
        block_z = jnp.where(iota((8, depth), 1) % 8 == iota((8, depth), 0), 1.0, 0.0)
        spread_z = lax.dot_general(
            lax.dot_general(block_z, rigidity[2], (((0,), (1,)), ((), ())), precision=HIGH, preferred_element_type=F32),
            block_z,
            (((1,), (0,)), ((), ())),
            precision=HIGH,
            preferred_element_type=F32,
        )
        same = (iota((depth, depth), 0) // 8) == (iota((depth, depth), 1) // 8)
        high, low = pieces(jnp.where(same, spread_z, 0.0))
        wz[0], wz[1] = high, low
        outer_x = jnp.where(iota((8, 64), 1) // 8 == iota((8, 64), 0), 1.0, 0.0)
        inner_y = jnp.where(iota((8, 64), 1) % 8 == iota((8, 64), 0), 1.0, 0.0)

        def expand(matrix, hot):
            left = lax.dot_general(hot, matrix, (((0,), (0,)), ((), ())), precision=HIGH, preferred_element_type=F32)
            return lax.dot_general(left, hot, (((1,), (0,)), ((), ())), precision=HIGH, preferred_element_type=F32)

        same_y = iota((64, 64), 0) % 8 == iota((64, 64), 1) % 8
        same_x = iota((64, 64), 0) // 8 == iota((64, 64), 1) // 8
        mixed = jnp.where(same_y, expand(rigidity[0], outer_x), 0.0) + jnp.where(same_x, expand(rigidity[1], inner_y), 0.0)
        high, low = pieces(mixed)
        wxy[...] = jnp.concatenate([high, high, low], axis=1)

        def second(r, carry):
            d_max, d_min, o_sum = carry
            w = weight[r]
            b_y = jnp.where((y_at % 8 == 7) & (y_at < width - 1), 0.5 * (w + pltpu.roll(w, width - 1, 0)), 0.0)
            b_low = pltpu.roll(b_y, 1, 0)
            uy[r] = b_y
            ly[r] = b_low
            pair = b_y + b_low
            b_z = jnp.where((z_at % 8 == 7) & (z_at < depth - 1), 0.5 * (w + pltpu.roll(w, depth - 1, 1)), 0.0)
            b_low = pltpu.roll(b_z, 1, 1)
            uz[r] = b_z
            lz[r] = b_low
            pair = pair + b_z + b_low
            d = storage[r] + pair
            diag[r] = d
            square = root[r] * root[r]
            whole = d + square * trace
            o = pair + square * off
            return jnp.maximum(d_max, fold(whole, jnp.max)), jnp.minimum(d_min, fold(whole, jnp.min)), o_sum + fold(o, jnp.sum)

        write_stats(*lax.fori_loop(0, rows, second, start))

    def near_start(which):
        for o, (peer, where) in enumerate(near_peers):
            pltpu.make_async_remote_copy(
                near_slots.at[which, low_id],
                near_slots.at[which, low_id],
                near_send.at[which, o],
                near_recv.at[which, low_id],
                device_id=where,
                device_id_type=MESH,
            ).start()

    def near_wait(which):
        for o, (peer, where) in enumerate(near_peers):
            copy = pltpu.make_async_remote_copy(
                near_slots.at[which, peer],
                near_slots.at[which, peer],
                near_send.at[which, o],
                near_recv.at[which, peer],
                device_id=where,
                device_id_type=MESH,
            )
            copy.wait_recv()

    def near_sent(which):
        for o, (peer, where) in enumerate(near_peers):
            pltpu.make_async_remote_copy(
                near_slots.at[which, low_id],
                near_slots.at[which, low_id],
                near_send.at[which, o],
                near_recv.at[which, low_id],
                device_id=where,
                device_id_type=MESH,
            ).wait_send()

    def far_start(which):
        for o, (peer, where) in enumerate(far_peers):
            pltpu.make_async_remote_copy(
                far_slots.at[which, high_id],
                far_slots.at[which, high_id],
                far_send.at[which, o],
                far_recv.at[which, high_id],
                device_id=where,
                device_id_type=MESH,
            ).start()

    def far_wait(which):
        for o, (peer, where) in enumerate(far_peers):
            copy = pltpu.make_async_remote_copy(
                far_slots.at[which, peer],
                far_slots.at[which, peer],
                far_send.at[which, o],
                far_recv.at[which, peer],
                device_id=where,
                device_id_type=MESH,
            )
            copy.wait_recv()
            copy.wait_send()

    def merge_stats(tiles):
        lane = iota((1, 128), 1)
        most, summed = tiles[0], tiles[0]
        for tile in tiles[1:]:
            most, summed = jnp.maximum(most, tile), summed + tile
        return jnp.where(lane == 2, summed, most)

    near_start(0)

    l_forcing.wait()

    part_rows = width // PARTS

    def halo_up(k, j):
        span = pl.ds(j * part_rows, part_rows)
        at = RAW.get(k, k)
        return pltpu.make_async_remote_copy(
            basis.at[at, rows, span],
            basis.at[at, 0, span],
            halo_send.at[k, 0, j],
            halo_recv.at[k, 0, j],
            device_id=up,
            device_id_type=MESH,
        )

    def halo_down(k, j):
        span = pl.ds(j * part_rows, part_rows)
        at = RAW.get(k, k)
        return pltpu.make_async_remote_copy(
            basis.at[at, 1, span],
            basis.at[at, rows + 1, span],
            halo_send.at[k, 1, j],
            halo_recv.at[k, 1, j],
            device_id=down,
            device_id_type=MESH,
        )

    def linked(k):
        if k in SKIP:
            return has_up & jnp.logical_not(far_up), has_down & jnp.logical_not(far_down)
        return has_up, has_down

    def send_halos(k, j):
        to_up, to_down = linked(k)

        @pl.when(to_up)
        def _():
            halo_up(k, j).start()

        @pl.when(to_down)
        def _():
            halo_down(k, j).start()

    def deep_up(i):
        return pltpu.make_async_remote_copy(
            basis.at[RAW.get(DEEP[i], DEEP[i]), rows - 1], second.at[0, i], deep_send.at[i, 0], deep_recv.at[i, 0], device_id=up, device_id_type=MESH
        )

    def deep_down(i):
        return pltpu.make_async_remote_copy(
            basis.at[RAW.get(DEEP[i], DEEP[i]), 2], second.at[1, i], deep_send.at[i, 1], deep_recv.at[i, 1], device_id=down, device_id_type=MESH
        )

    def ghost_up(i):
        source = (ghost_diag.at[0], uy.at[rows - 1], ly.at[rows - 1], uz.at[rows - 1], lz.at[rows - 1], gx.at[rows - 1])[i]
        return pltpu.make_async_remote_copy(
            source, ghost.at[0, i], ghost_send.at[0, i], ghost_recv.at[0, i], device_id=up, device_id_type=MESH
        )

    def ghost_down(i):
        source = (ghost_diag.at[1], uy.at[0], ly.at[0], uz.at[0], lz.at[0], ax.at[1])[i]
        return pltpu.make_async_remote_copy(
            source, ghost.at[1, i], ghost_send.at[1, i], ghost_recv.at[1, i], device_id=down, device_id_type=MESH
        )

    def send_deep(i):
        @pl.when(far_up)
        def _():
            deep_up(i).start()

        @pl.when(far_down)
        def _():
            deep_down(i).start()

    @pl.when(fluid)
    def _():
        pltpu.make_async_remote_copy(
            picked, walls, contact_send.at[0], contact_recv.at[groups - 1], device_id=(groups - 1, brick), device_id_type=MESH
        ).wait_recv()

    @pl.when(solid)
    def _():
        for g in range(groups - 1):
            pltpu.make_async_remote_copy(
                picked, nears.at[g], contact_send.at[g], contact_recv.at[g], device_id=(g, brick), device_id_type=MESH
            ).wait_recv()
        walls[...] = nears[0] + nears[1] + nears[2] - picked[...]

    heat = factor[...] * walls[0:lines]
    extra = spread(jnp.where(solid, heat, heat * owned)).reshape(rows, width, depth)
    basis[0, 1 : rows + 1] = forcing[...] + extra
    for j in range(PARTS):
        send_halos(0, j)
    send_deep(0)

    @pl.when(at_bottom)
    def _():
        gx[0] = jnp.zeros(plane, F32)

    @pl.when(fluid & has_down)
    def _():
        coef_a.wait_recv()
        coef_g.wait_recv()
        diag[0] = diag[0] + ax[0]

    @pl.when(solid & has_down)
    def _():
        coef_up.wait_recv()
        gx[0] = 0.5 * (weight_low[...] + weight[0])
        diag[0] = diag[0] + gx[0]

    @pl.when(solid & has_up)
    def _():
        coef_down.wait_recv()
        ax[rows] = 0.5 * (weight[rows - 1] + weight_up[...])
        diag[rows - 1] = diag[rows - 1] + ax[rows]

    @pl.when(solid & at_top)
    def _():
        ax[rows] = jnp.zeros(plane, F32)

    def gram_sums(k, low, high, accs):
        def body(r, accs):
            accs = list(accs)
            for j in range(width // 8):
                span = slice(8 * j, 8 * j + 8)
                mine = basis[k, r + 1, span, :]
                for i in range(k + 1):
                    other = mine if i == k else basis[i, r + 1, span, :]
                    accs[i] = accs[i] + mine * other
            return tuple(accs)

        return lax.fori_loop(low, high, body, accs)

    def gram_none(k):
        return tuple(jnp.zeros((8, depth), F32) for _ in range(k + 1))

    def gram_keep(k, accs):
        lane = iota((1, 128), 1)
        tile = jnp.zeros((1, 128), F32) if k == 0 else gram_tile[...]
        for i in range(k + 1):
            spot = (lane == i * SIDE + k) | (lane == k * SIDE + i)
            tile = jnp.where(spot, total(accs[i]), tile)
        gram_tile[...] = tile

    def gram_row(k):
        gram_keep(k, gram_sums(k, 0, rows, gram_none(k)))

    def local(r, v):
        return (
            diag[r] * v
            - uy[r] * pltpu.roll(v, width - 1, 0)
            - ly[r] * pltpu.roll(v, 1, 0)
            - uz[r] * pltpu.roll(v, depth - 1, 1)
            - lz[r] * pltpu.roll(v, 1, 1)
        )

    def apply(k, scale):
        at, to = (RAW.get(k, k), RAW[k + 1]) if scale is None else (k, k + 1)

        def keep(r, q):
            if scale is None:
                basis[to, r + 1] = q
            else:
                basis[to, r + 1] = scale * q - basis[k - 1, r + 1]

        @pl.when(fluid)
        def _():
            def middle(r, carry):
                v = basis[at, r + 1]
                keep(r, local(r, v) - gx[r] * basis[at, r] - ax[r + 1] * basis[at, r + 2])
                return carry

            keep(0, local(0, basis[at, 1]) - ax[1] * basis[at, 2])
            keep(rows - 1, local(rows - 1, basis[at, rows]) - gx[rows - 1] * basis[at, rows - 1])
            lax.fori_loop(1, rows - 1, middle, 0)

        @pl.when(solid)
        def _():
            for e in range(width // 8):
                u = (root[:, 8 * e : 8 * e + 8, :] * basis[at, 1 : rows + 1, 8 * e : 8 * e + 8, :]).reshape(64, depth)
                high, low = pieces(u)
                uh[e], ul[e] = high, low
                stiff[e] = dot(wxy[...], jnp.concatenate([high, low, high], axis=0), ((1,), (0,)))
            high, low = uh[...].reshape(cells, depth), ul[...].reshape(cells, depth)
            along = dot(high, wz[0], ((1,), (0,))) + dot(low, wz[0], ((1,), (0,))) + dot(high, wz[1], ((1,), (0,)))
            stiff[...] = stiff[...] + along.reshape(width // 8, 64, depth)

            def each(r, carry):
                force = stiff[:, pl.ds(r * 8, 8), :].reshape(width, depth)
                keep(r, local(r, basis[at, r + 1]) + root[r] * force)
                return carry

            lax.fori_loop(0, rows, each, 0)

    def finish(k, scale, mix=None):
        at, to = RAW.get(k, k), (RAW[k + 1] if scale is None else k + 1)
        for j in range(PARTS):
            span = slice(j * part_rows, (j + 1) * part_rows)

            from_up, from_down = linked(k)

            @pl.when(from_down)
            def _():
                halo_up(k, j).wait_recv()

            @pl.when(from_up)
            def _():
                halo_down(k, j).wait_recv()

            for own, halo, coef in ((1, 0, gx.at[0]), (rows, rows + 1, ax.at[rows])):
                value = basis[at, halo, span]
                if mix is not None:
                    value = mix[0] * value + mix[1] * basis[RAW[1], halo, span] + mix[2] * basis[0, halo, span]
                    basis[k, halo, span] = value
                value = coef[span] * value
                if scale is not None:
                    value = scale * value
                basis[to, own, span] = basis[to, own, span] - value
            if k + 1 < ITERS:
                send_halos(k + 1, j)

    def extend(i):
        k = DEEP[i]
        fresh = range(i + 1) if k == 2 else (i,)

        def row(side, near, halo, inward):
            v = basis[k, halo]
            if k == 2:
                outer_row = mix[0] * second[side, 2] + mix[1] * second[side, 1] + mix[2] * second[side, 0]
                older = (basis[RAW[1], halo] - center * basis[0, halo]) * inv_e
            else:
                outer_row, older = second[side, i], basis[k - 1, halo]
            q = (
                (ghost[side, 0] - center) * v
                - ghost[side, 1] * pltpu.roll(v, width - 1, 0)
                - ghost[side, 2] * pltpu.roll(v, 1, 0)
                - ghost[side, 3] * pltpu.roll(v, depth - 1, 1)
                - ghost[side, 4] * pltpu.roll(v, 1, 1)
                - ghost[side, 5] * outer_row
                - inward * basis[k, near]
            )
            basis[k + 1, halo] = scale * q - older

        @pl.when(far_down)
        def _():
            for n in fresh:
                deep_up(n).wait_recv()
            if k == 2:
                for n in range(6):
                    ghost_up(n).wait_recv()
            row(0, 1, 0, ax[0])

        @pl.when(far_up)
        def _():
            for n in fresh:
                deep_down(n).wait_recv()
            if k == 2:
                for n in range(6):
                    ghost_down(n).wait_recv()
            row(1, rows, rows + 1, gx[rows])

    apply(0, None)
    send_deep(1)
    near_wait(0)
    far_slots[0, high_id] = merge_stats([near_slots[0, i] for i in range(inner)])
    far_start(0)
    finish(0, None)

    @pl.when(far_up)
    def _():
        ghost_diag[0] = diag[rows - 1]
        for n in range(6):
            ghost_up(n).start()

    @pl.when(far_down)
    def _():
        ghost_diag[1] = diag[0]
        for n in range(6):
            ghost_down(n).start()

    apply(1, None)
    send_deep(2)
    gram_row(0)
    finish(1, None)
    far_wait(0)
    split = (groups - 1) * outer

    def interval(tiles, count, of_most, of_mean):
        stats = merge_stats(tiles)
        mean = stats[0:1, 2:3] * (1.0 / count)
        high = of_most * stats[0:1, 0:1] + of_mean * mean
        low = jnp.maximum(-stats[0:1, 1:2] - 0.5 * mean, 0.0)
        return 0.5 * (high + low), 0.5 * (high - low)

    c_fluid, e_fluid = interval([far_slots[0, i] for i in range(split)], float((groups - 1) * bricks * cells * depth), 0.9, 0.1)
    c_solid, e_solid = interval([far_slots[0, i] for i in range(split, n_far)], float(bricks * cells * depth), 0.97, 0.25)
    center = jnp.where(solid, c_solid, c_fluid)
    inv_e = 1.0 / jnp.where(solid, e_solid, e_fluid)
    scale = 2.0 * inv_e

    mix = (scale * inv_e, -2.0 * scale * center * inv_e, scale * inv_e * center * center - 1.0)

    def convert(r, carry):
        zero, one, two = basis[0, r + 1], basis[RAW[1], r + 1], basis[RAW[2], r + 1]
        basis[1, r + 1] = (one - center * zero) * inv_e
        basis[2, r + 1] = mix[0] * two + mix[1] * one + mix[2] * zero
        diag[r] = diag[r] - center
        return carry

    lax.fori_loop(0, rows, convert, 0)
    for k in range(2, ITERS):
        apply(k, scale)
        if k + 1 in DEEP:
            send_deep(DEEP.index(k + 1))
        if k == 2:
            gram_row(1)
        gram_row(k)
        if k + 1 == ITERS:
            last_sums = gram_sums(ITERS, 1, rows - 1, gram_none(ITERS))
        finish(k, scale, mix if k == 2 else None)
        if k + 1 in SKIP:
            extend(DEEP.index(k))
    last_sums = gram_sums(ITERS, rows - 1, rows, gram_sums(ITERS, 0, 1, last_sums))
    gram_keep(ITERS, last_sums)

    near_slots[1, low_id] = gram_tile[...]
    near_start(1)
    near_wait(1)
    summed = near_slots[1, 0]
    for i in range(1, inner):
        summed = summed + near_slots[1, i]
    far_slots[1, high_id] = summed
    far_start(1)
    near_sent(0)
    near_sent(1)

    @pl.when(solid)
    def _():
        for g in range(groups - 1):
            wall_copy(g).wait_send()

    @pl.when(fluid)
    def _():
        near_copy.wait_send()

    @pl.when(fluid & has_up)
    def _():
        coef_a.wait_send()
        coef_g.wait_send()

    @pl.when(solid & has_up)
    def _():
        coef_up.wait_send()

    @pl.when(solid & has_down)
    def _():
        coef_down.wait_send()

    @pl.when(far_up)
    def _():
        for n in range(6):
            ghost_up(n).wait_send()
        for i in range(len(DEEP)):
            deep_up(i).wait_send()

    @pl.when(far_down)
    def _():
        for n in range(6):
            ghost_down(n).wait_send()
        for i in range(len(DEEP)):
            deep_down(i).wait_send()

    for k in range(ITERS):
        sent_up, sent_down = linked(k)
        for j in range(PARTS):

            @pl.when(sent_up)
            def _():
                halo_up(k, j).wait_send()

            @pl.when(sent_down)
            def _():
                halo_down(k, j).wait_send()

    far_wait(1)
    gram_fluid = far_slots[1, 0]
    for i in range(1, split):
        gram_fluid = gram_fluid + far_slots[1, i]
    gram_solid = far_slots[1, split]
    for i in range(split + 1, n_far):
        gram_solid = gram_solid + far_slots[1, i]
    y_fluid, ok_fluid = projected(gram_fluid, c_fluid / e_fluid, True)
    y_solid, ok_solid = projected(gram_solid, c_solid / e_solid, False)
    coeffs = jnp.where(solid, y_solid, y_fluid) * inv_e
    flag[0] = jnp.max(ok_fluid * ok_solid).astype(jnp.int32)
    weights = [coeffs[k : k + 1, :1] for k in range(ITERS)]

    def combine(r, carry):
        acc = weights[0] * basis[0, r + 1]
        for k in range(1, ITERS):
            acc = acc + weights[k] * basis[k, r + 1]
        out[r] = acc
        return carry

    lax.fori_loop(0, rows, combine, 0)


def handed_on(result):
    def body(source, target, sem):
        copy = pltpu.make_async_copy(source, target, sem)
        copy.start()
        copy.wait()

    return pl.pallas_call(
        body,
        out_shape=jax.ShapeDtypeStruct(result.shape, result.dtype),
        in_specs=[pl.BlockSpec(memory_space=pltpu.VMEM)],
        out_specs=pl.BlockSpec(memory_space=pl.ANY),
        scratch_shapes=[pltpu.SemaphoreType.DMA],
        name="handed_on",
    )(pltpu.with_memory_space_constraint(result, pltpu.VMEM))


def shards(*arguments):
    groups, bricks = lax.axis_size("group"), lax.axis_size("brick")
    forcing = arguments[0]
    rows, width, depth = slab = forcing.shape
    lines = arguments[8].shape[0]
    points = lines * 128
    n_far = groups * (bricks // 8)
    vm = pltpu.VMEM
    scratch = (
        [vm(slab, F32)] * 3
        + [vm((3,) + slab, F32)] * 2
        + [vm(slab, F32)] * 2
        + [vm((3, 8, 8), F32)]
        + [vm((lines, 128), jnp.int32)] * 3
        + [vm((lines, 128), F32)]
        + [vm((ITERS + 3, rows + 2, width, depth), F32)]
        + [vm((rows + 1, width, depth), F32)] * 2
        + [vm(slab, F32)] * 5
        + [vm((width // 8, 64, depth), F32)]
        + [vm((width // 8, 64, depth), BF16)] * 2
        + [vm((2, depth, depth), BF16), vm((64, 192), BF16)]
        + [vm((width, depth), F32)] * 2
        + [vm((rows * width, points), BF16), vm((depth, points), BF16)]
        + [vm((8, 128), F32)] * 2
        + [vm((groups - 1, 8, 128), F32)]
        + [vm((1, 128), F32), vm((2, 8, 1, 128), F32), vm((2, n_far, 1, 128), F32)]
        + [vm((2, len(DEEP), width, depth), F32), vm((2, 6, width, depth), F32), vm((2, width, depth), F32)]
    )
    dma = pltpu.SemaphoreType.DMA
    semaphores = [
        dma((12,)),
        dma((ITERS, 2, PARTS)),
        dma((ITERS, 2, PARTS)),
        dma((2,)),
        dma((2,)),
        dma((groups,)),
        dma((groups,)),
        dma((2, 8)),
        dma((2, 8)),
        dma((2, n_far)),
        dma((2, n_far)),
        dma((len(DEEP), 2)),
        dma((len(DEEP), 2)),
        dma((2, 6)),
        dma((2, 6)),
    ]
    result, flag = pl.pallas_call(
        functools.partial(kernel, groups, bricks),
        out_shape=(pltpu.VMEM(slab, F32), jax.ShapeDtypeStruct((1,), jnp.int32)),
        in_specs=[pl.BlockSpec(memory_space=pl.ANY)] * 12,
        out_specs=(pl.BlockSpec(memory_space=pltpu.VMEM), pl.BlockSpec(memory_space=pltpu.SMEM)),
        scratch_shapes=scratch + semaphores,
        compiler_params=pltpu.CompilerParams(collective_id=0, has_side_effects=True, vmem_limit_bytes=56 * 2**20),
        name="coupled",
    )(*arguments)
    return lax.cond(flag[0] > 0, lambda: handed_on(result), lambda: iterated(*arguments))


def solution(mesh):
    return jax.shard_map(
        shards,
        mesh=mesh,
        in_specs=(
            P(("group", "brick"), None, None),
            P(("group", "brick"), None, None),
            P(("group", "brick"), None, None),
            P(None, ("group", "brick"), None, None),
            P(None, ("group", "brick"), None, None),
            P(("group", "brick"), None, None),
            P(("group", "brick"), None, None),
            P(),
            P("brick", None),
            P("brick", None),
            P("brick", None),
            P("brick", None),
        ),
        out_specs=P(("group", "brick"), None, None),
        check_vma=False,
    )
```
